128 devices in a mesh: section: 2 (over core), seq: 2 (over x_lo), fsdp: 32 (over x_hi, y, z).
Axes of the slice: x: 4 (x_hi: 2, x_lo: 2; x = x_hi * 2 + x_lo), y: 4, z: 4, core: 2. Of those that a mesh axis runs over, the one named last changes fastest.
Arguments:
- inputs: bfloat16 [2, 4096, 1536], P(None, ('seq', 'fsdp')), may hold values from -6 to 6
- cotangent: bfloat16 [2, 4096, 1536], P(None, ('seq', 'fsdp')), may hold values from -6 to 6
- w_in: bfloat16 [2, 1536, 4608], P('section', 'fsdp'), may hold values from -0.15625 to 0.15625
- w_out: bfloat16 [2, 1536, 1536], P('section', 'fsdp'), may hold values from -0.15625 to 0.15625
- w_gate: bfloat16 [2, 1536, 6912], P('section', 'fsdp'), may hold values from -0.15625 to 0.15625
- w_up: bfloat16 [2, 1536, 6912], P('section', 'fsdp'), may hold values from -0.15625 to 0.15625
- w_down: bfloat16 [2, 6912, 1536], P('section', 'fsdp'), may hold values from -0.078125 to 0.078125
- kernel: bfloat16 [2, 3, 1536], P('section', None, 'fsdp'), may hold values from -3.5 to 3.5
- gain_mix: bfloat16 [2, 1536], P('section', 'fsdp'), may hold values from 0.5 to 1.5
- gain_ffn: bfloat16 [2, 1536], P('section', 'fsdp'), may hold values from 0.5 to 1.5
Outputs:
- layer_outputs: bfloat16 [2, 2, 4096, 1536], P('section', None, ('seq', 'fsdp'))
- input_grads: float32 [2, 2, 4096, 1536], P('section', None, ('seq', 'fsdp'))
- grad_w_in: float32 [2, 1536, 4608], P('section', 'fsdp')
- grad_w_out: float32 [2, 1536, 1536], P('section', 'fsdp')
- grad_w_gate: float32 [2, 1536, 6912], P('section', 'fsdp')
- grad_w_up: float32 [2, 1536, 6912], P('section', 'fsdp')
- grad_w_down: float32 [2, 6912, 1536], P('section', 'fsdp')
- grad_kernel: float32 [2, 3, 1536], P('section', None, 'fsdp')
- grad_gain_mix: float32 [2, 1536], P('section', 'fsdp')
- grad_gain_ffn: float32 [2, 1536], P('section', 'fsdp')
The draws below stay inside these ranges and needn't reach their ends.
All inputs are finite; a program needn't handle non-finite values.
Results may differ from the reference program's by a relative error of at most 0.03.
Values may be sent and summed in bfloat16 or wider, within the bound.
A program may use at most 320 MiB of HBM per device.

```python
import jax
import jax.numpy as jnp
from jax import lax

D = 1536
FF = 6912
KW = 3
MICRO = 2
LENGTH = 4096


def block_levels(rng, shape, cuts, low, top_value):
    def one(dim, shards_of):
        heights = jax.random.uniform(jax.random.fold_in(jax.random.fold_in(rng, 6), dim), (shards_of,), jnp.float32, low / len(cuts), top_value / len(cuts))
        return jnp.repeat(jnp.exp(heights), shape[dim] // shards_of).reshape((-1,) + (1,) * (len(shape) - dim - 1))

    level = one(*cuts[0])
    for cut in cuts[1:]:
        level = level * one(*cut)
    return level


def bell_draw(key, extent, width, limit, pieces=(), held_as=jnp.bfloat16):
    values = width * jax.random.normal(key, extent, jnp.float32)
    if pieces:
        values = values * block_levels(key, extent, pieces, -0.22, 0.18)
    return jnp.clip(values, -limit, limit).astype(held_as)


def setup_inputs(seed: int = 0) -> dict:
    splits = jax.random.split(jax.random.key(seed), 11)
    return {
        "inputs": bell_draw(splits[0], (MICRO, LENGTH, D), 1.0, 6.0, ((1, 64),)),
        "cotangent": bell_draw(splits[1], (MICRO, LENGTH, D), 1.0, 6.0, ((1, 64),)),
        "w_in": bell_draw(splits[2], (2, D, 3 * D), D ** -0.5, 0.15625, ((0, 2), (1, 32))),
        "w_out": bell_draw(splits[3], (2, D, D), D ** -0.5, 0.15625, ((0, 2), (1, 32))),
        "w_gate": bell_draw(splits[4], (2, D, FF), D ** -0.5, 0.15625, ((0, 2), (1, 32))),
        "w_up": bell_draw(splits[5], (2, D, FF), D ** -0.5, 0.15625, ((0, 2), (1, 32))),
        "w_down": bell_draw(splits[6], (2, FF, D), FF ** -0.5, 0.078125, ((0, 2), (1, 32))),
        "kernel": bell_draw(splits[7], (2, KW, D), KW ** -0.5, 3.5, ((0, 2), (2, 32))),
        "gain_mix": jnp.clip(1.0 + 0.1 * jax.random.normal(splits[8], (2, D), jnp.float32), 0.5, 1.5).astype(jnp.bfloat16),
        "gain_ffn": jnp.clip(1.0 + 0.1 * jax.random.normal(splits[9], (2, D), jnp.float32), 0.5, 1.5).astype(jnp.bfloat16),
    }


epsilon = 1e-06
highest = lax.Precision.HIGHEST

@jax.custom_vjp
def low(v):
    return lax.optimization_barrier(v.astype(jnp.bfloat16)).astype(jnp.float32)

@jax.custom_vjp
def low_back(v):
    return v

def low_keep(v):
    return (low(v), None)

def low_pass(kept, grad):
    return (grad,)

def back_keep(v):
    return (v, None)

def back_low(kept, grad):
    return (low(grad),)
low.defvjp(low_keep, low_pass)
low_back.defvjp(back_keep, back_low)

def conv_block(values, w_in, w_out, w_gate, w_up, w_down, kernel, gain_mix, gain_ffn):
    token_rows = values.shape[0]
    feature_count = values.shape[1]
    inverse = lax.rsqrt(lax.optimization_barrier(jnp.mean(values * values, axis=-1, keepdims=True)) + epsilon)
    normed = low(values * inverse * gain_mix)
    projected = low_back(jnp.dot(normed, w_in, precision=highest))
    b_part = projected[:, :feature_count]
    c_part = projected[:, feature_count:2 * feature_count]
    x_part = projected[:, 2 * feature_count:]
    gated = b_part * x_part
    padded = jnp.pad(gated, ((KW - 1, 0), (0, 0)))
    convolved = jnp.zeros_like(gated)
    for offset in range(KW):
        first_row = KW - 1 - offset
        convolved = convolved + kernel[offset] * padded[first_row:first_row + token_rows]
    mixed_low = low(c_part * convolved)
    middle = values + low_back(jnp.dot(mixed_low, w_out, precision=highest))
    inverse_ffn = lax.rsqrt(lax.optimization_barrier(jnp.mean(middle * middle, axis=-1, keepdims=True)) + epsilon)
    normed_ffn = low(middle * inverse_ffn * gain_ffn)
    gating = low_back(jnp.dot(normed_ffn, w_gate, precision=highest))
    up_proj = low_back(jnp.dot(normed_ffn, w_up, precision=highest))
    hidden = low(jax.nn.silu(gating) * up_proj)
    return middle + low_back(jnp.dot(hidden, w_down, precision=highest))

def reference(inputs, cotangent, w_in, w_out, w_gate, w_up, w_down, kernel, gain_mix, gain_ffn):
    float_params = tuple((p.astype(jnp.float32) for p in (w_in, w_out, w_gate, w_up, w_down, kernel, gain_mix, gain_ffn)))
    first_block = tuple((p[0] for p in float_params))
    second_block = tuple((p[1] for p in float_params))

    def one_sequence(totals, seq_pair):
        values, seq_cotangent = seq_pair
        values = values.astype(jnp.float32)
        out_first, back_first = jax.vjp(conv_block, values, *first_block)
        between = low(out_first)
        out_second, back_second = jax.vjp(conv_block, between, *second_block)
        grads_second = back_second(seq_cotangent.astype(jnp.float32))
        grads_first = back_first(low(grads_second[0]))
        totals = tuple((t + jnp.stack([a, b]) for t, a, b in zip(totals, grads_first[1:], grads_second[1:])))
        outputs = jnp.stack([between, out_second]).astype(jnp.bfloat16)
        input_pair = jnp.stack([grads_first[0], grads_second[0]])
        return (totals, (outputs, input_pair))
    zero_totals = tuple((jnp.zeros_like(p) for p in float_params))
    totals, (outputs, input_pairs) = lax.scan(one_sequence, zero_totals, (inputs, cotangent))
    layer_outputs = jnp.transpose(outputs, (1, 0, 2, 3))
    input_grads = jnp.transpose(input_pairs, (1, 0, 2, 3))
    return (layer_outputs, input_grads, totals[0], totals[1], totals[2], totals[3], totals[4], totals[5], totals[6], totals[7])
```

```python
import functools

import jax
import jax.numpy as jnp
from jax import lax
from jax.experimental import pallas as pl
from jax.experimental.pallas import tpu as pltpu
from jax.sharding import Mesh
from jax.sharding import PartitionSpec as P

F32, BF16 = jnp.float32, jnp.bfloat16
MESH = pl.DeviceIdType.MESH
EPS = 1e-06
ANY = pl.BlockSpec(memory_space=pl.ANY)
VMEM = pl.BlockSpec(memory_space=pltpu.VMEM)
ORDER = (1, 3, 2)


def place():
    return tuple(lax.axis_index(name) for name in ("section", "xl", "xh", "y", "z"))


def barrier_all(devices):
    barrier = pltpu.get_barrier_semaphore()
    for device in devices:
        pl.semaphore_signal(barrier, inc=1, device_id=device, device_id_type=MESH)
    pl.semaphore_wait(barrier, len(devices))


def remote(src, dst, send, recv, device):
    return pltpu.make_async_remote_copy(
        src_ref=src, dst_ref=dst, send_sem=send, recv_sem=recv, device_id=device, device_id_type=MESH
    )


def plane_peers():
    section, xl, xh, y, z = place()
    partner = {"xh": 1 - xh, "xl": 1 - xl}
    twin = {"xl": 1 - xl}
    zs = {r: {"z": lax.rem(z + r, 4)} for r in ORDER}
    ys = {r: {"y": lax.rem(y + r, 4)} for r in ORDER}
    return partner, twin, zs, ys


def gather_kernel(
    a_s, a_in, a_g, a_u, w_o, w_d,
    o_s, o_in, o_o, o_g, o_u, o_d,
    z_send, z_recv, y_send, y_recv, p_send, p_recv, q_send, q_recv, local, go,
):
    section, xl, xh, y, z = place()
    partner, twin, zs, ys = plane_peers()
    core = {"section": 1 - section}
    barrier_all([partner, twin, core, *zs.values(), *ys.values()])

    @pl.when(section == 1)
    def _():
        pl.semaphore_wait(go, 1)

    me = xh * 4 + y
    outs = (o_s, o_in, o_o, o_g, o_u, o_d)
    cut = (a_s, a_in, None, a_g, a_u, None)
    whole = (None, None, w_o, None, None, w_d)

    def half(n, ref, row, h):
        if n == 2:
            return ref.at[row, :, pl.ds(pl.multiple_of(h * 768, 128), 768)]
        if n == 5:
            return ref.at[row, pl.ds(pl.multiple_of(h * 112, 16), 112)]
        return ref.at[row, pl.ds(h * 2, 2)]

    sent, locals_, z_copies = [], {}, {}
    for n in range(6):
        if cut[n] is not None:
            block = (lambda zz: a_s) if n == 0 else (lambda zz, a=cut[n]: a.at[zz])
            for r in ORDER:
                copy = remote(block(lax.rem(z + r, 4)), outs[n].at[me, z], z_send.at[n, r - 1], z_recv.at[n, r - 1], zs[r])
                copy.start()
                z_copies[n, r] = copy
                sent.append(copy)
            own = pltpu.make_async_copy(block(z), outs[n].at[me, z], local.at[n])
        else:
            own = pltpu.make_async_copy(whole[n], outs[n].at[me], local.at[n])
        own.start()
        locals_[n] = own

    y_copies, p_copies, q_copies = {}, {}, {}

    def stage_y(n):
        locals_[n].wait()
        if cut[n] is not None:
            for r in ORDER:
                z_copies[n, r].wait_recv()
        for r in ORDER:
            copy = remote(outs[n].at[me], outs[n].at[me], y_send.at[n, r - 1], y_recv.at[n, r - 1], ys[r])
            copy.start()
            y_copies[n, r] = copy
            sent.append(copy)
        push_p(n, 0)

    def push_p(n, r):
        row = xh * 4 + lax.rem(y + 4 - r, 4)
        src = half(n, outs[n], row, xl)
        copy = remote(src, src, p_send.at[n, r], p_recv.at[n, r], partner)
        copy.start()
        p_copies[n, r] = copy
        sent.append(copy)

    def stage_p(n):
        for r in ORDER:
            y_copies[n, r].wait_recv()
            push_p(n, r)

    def stage_q(n):
        for r in (0, *ORDER):
            p_copies[n, r].wait_recv()
            row = (1 - xh) * 4 + lax.rem(y + 4 - r, 4)
            src = half(n, outs[n], row, 1 - xl)
            copy = remote(src, src, q_send.at[n, r], q_recv.at[n, r], twin)
            copy.start()
            q_copies[n, r] = copy
            sent.append(copy)

    for step in range(8):
        if step < 6:
            stage_y(step)
        if 0 <= step - 1 < 6:
            stage_p(step - 1)
        if 0 <= step - 2 < 6:
            stage_q(step - 2)
    for copy in q_copies.values():
        copy.wait_recv()

    @pl.when(section == 0)
    def _():
        pl.semaphore_signal(go, inc=1, device_id=core, device_id_type=MESH)

    for copy in sent:
        copy.wait_send()


def gather(a_s, a_in, a_g, a_u, w_o, w_d):
    shape = jax.ShapeDtypeStruct
    dma = pltpu.SemaphoreType.DMA
    return pl.pallas_call(
        gather_kernel,
        out_shape=(
            shape((8, 4, 16, 128), BF16),
            shape((8, 4, 48, 1152), BF16),
            shape((8, 48, 1536), BF16),
            shape((8, 4, 48, 1792), BF16),
            shape((8, 4, 48, 1792), BF16),
            shape((8, 224, 1536), BF16),
        ),
        in_specs=[ANY] * 6,
        out_specs=[ANY] * 6,
        scratch_shapes=[
            dma((6, 3)), dma((6, 3)), dma((6, 3)), dma((6, 3)),
            dma((6, 4)), dma((6, 4)), dma((6, 4)), dma((6, 4)),
            dma((6,)), pltpu.SemaphoreType.REGULAR,
        ],
        compiler_params=pltpu.CompilerParams(collective_id=0, has_side_effects=True),
        name="gather_weights",
    )(a_s, a_in, a_g, a_u, w_o, w_d)


def dot_nn(a, b):
    return lax.dot_general(a, b, (((1,), (0,)), ((), ())), preferred_element_type=F32)


def dot_nt(a, b):
    return lax.dot_general(a, b, (((1,), (1,)), ((), ())), preferred_element_type=F32)


def dot_tn(a, b):
    return lax.dot_general(a, b, (((0,), (0,)), ((), ())), preferred_element_type=F32)


def cols(j, width):
    return pl.ds(pl.multiple_of(j * width, width), width)


def loop(count, body):
    def step(j, carry):
        body(j)
        return carry

    lax.fori_loop(0, count, step, 0)


def main_kernel(
    x_ref, cot_ref, gains, taps, win_h, wout_h, wg_h, wu_h, wd_h,
    y_ref, gx_ref, gin_h, gout_h, gg_h, gu_h, gd_h, gtap_ref, gmix_ref, gffn_ref,
    xa, xn, n2, ea, fa, part, rr, proj, ge, dce, cv, ha, hb, mx, gt, up, hd, dg, du,
    mid, dmid, dp, g0, win, wout, wg, wu, wd,
    load, store, a_send, a_recv, s_send, s_recv, h_send, h_recv, c_send, c_recv, ready,
):
    section, xl, xh, y, z = place()
    zs = {r: {"z": lax.rem(z + r, 4)} for r in ORDER}
    core = {"section": 1 - section}
    group = xl * 8 + xh * 4 + y
    after, before = lax.rem(group + 1, 16), lax.rem(group + 15, 16)

    def at_group(g):
        return {"xl": g // 8, "xh": lax.rem(g // 4, 2), "y": lax.rem(g, 4)}

    has_after, has_before = group < 15, group > 0
    barrier = pltpu.get_barrier_semaphore()

    def hail(device):
        pl.semaphore_signal(barrier, inc=1, device_id=device, device_id_type=MESH)

    loads = [
        pltpu.make_async_copy(src, dst, load.at[n])
        for n, (src, dst) in enumerate(((win_h, win), (wout_h, wout), (wg_h, wg), (wu_h, wu), (wd_h, wd)))
    ]
    for copy in loads:
        copy.start()

    for r in ORDER:
        hail(zs[r])

    @pl.when(has_after)
    def _():
        hail(at_group(after))

    @pl.when(has_before)
    def _():
        hail(at_group(before))

    @pl.when(section == 0)
    def _():
        hail(core)

    pl.semaphore_wait(barrier, 4 - (group + 1) // 16 + (group + 15) // 16 + section)

    @pl.when(section == 1)
    def _():
        pl.semaphore_signal(ready, inc=1, device_id=core, device_id_type=MESH)

    own = pl.ds(pl.multiple_of(z * 128, 128), 128)

    def rows_from(r):
        return pl.multiple_of(lax.rem(z + 4 - r, 4) * 128, 128)

    def spread(n, buf):
        return {r: remote(buf.at[own], buf.at[own], a_send.at[n, r - 1], a_recv.at[n, r - 1], zs[r]) for r in ORDER}

    def scatter(n):
        found = {}
        for r in ORDER:
            src = part.at[pl.ds(pl.multiple_of(lax.rem(z + r, 4) * 128, 128), 128)]
            found[r] = remote(src, rr.at[n, r - 1], s_send.at[n, r - 1], s_recv.at[n, r - 1], zs[r])
        return found

    def summed(n, i):
        at = pl.ds(i * 32, 32)
        total = part[pl.ds(pl.multiple_of(z * 128 + i * 32, 32), 32), :].astype(F32)
        for r in range(3):
            total = total + rr[n, r, at, :].astype(F32)
        return total

    x_all, n_all, e_all, f_all = spread(0, xa), spread(1, n2), spread(2, ea), spread(3, fa)
    to_core_x = remote(y_ref, xa.at[own], c_send.at[0], c_recv.at[0], core)
    to_core_g = remote(g0, ea.at[own], c_send.at[1], c_recv.at[1], core)

    @pl.when(section == 0)
    def _():
        xa[own, :] = x_ref[...]

    @pl.when(section == 1)
    def _():
        ea[own, :] = cot_ref[...]
        for r in ORDER:
            e_all[r].start()
        to_core_x.wait_recv()

    for r in ORDER:
        x_all[r].start()

    gain_mix, gain_ffn = gains[0:1, :], gains[1:2, :]

    def norm_rows(base):
        def body(i):
            at = pl.ds(pl.multiple_of(base + i * 32, 32), 32)
            values = xa[at, :].astype(F32)
            scale = lax.rsqrt(jnp.mean(values * values, axis=-1, keepdims=True) + EPS)
            xn[at, :] = (values * scale * gain_mix).astype(BF16)

        loop(4, body)

    norm_rows(pl.multiple_of(z * 128, 128))
    for r in ORDER:
        x_all[r].wait_recv()
        norm_rows(rows_from(r))

    loads[0].wait()

    def project(j):
        proj[j] = dot_nn(xn[...], win[:, cols(j, 384)])

    loop(3, project)

    blocks = [(mb, zc, zc * 128 + mb * 64) for mb in range(2) for zc in range(4)]
    for mb, zc, r0 in blocks:
        ge[mb, 8 + 64 * zc : 72 + 64 * zc, :] = proj[0, r0 : r0 + 64, :] * proj[2, r0 : r0 + 64, :]

    to_after = remote(ge.at[:, pl.ds(256, 8)], ha, h_send.at[0], h_recv.at[0], at_group(after))
    to_before = remote(dce.at[:, pl.ds(0, 8)], hb, h_send.at[1], h_recv.at[1], at_group(before))

    @pl.when(has_after)
    def _():
        to_after.start()

    @pl.when(has_before)
    def _():
        to_after.wait_recv()
        ge[:, 0:8, :] = ha[...]

    @pl.when(jnp.logical_not(has_before))
    def _():
        ge[:, 0:8, :] = jnp.zeros((2, 8, 384), F32)

    tap = [taps[k : k + 1, :] for k in range(3)]
    for mb, zc, r0 in blocks:
        t0 = 8 + 64 * zc
        total = tap[0] * ge[mb, t0 : t0 + 64, :]
        for k in (1, 2):
            total = total + tap[k] * ge[mb, t0 - k : t0 - k + 64, :]
        cv[r0 : r0 + 64, :] = total
        mx[r0 : r0 + 64, :] = (proj[1, r0 : r0 + 64, :] * total).astype(BF16)

    loads[1].wait()

    def mix_out(j):
        part[:, cols(j, 512)] = dot_nn(mx[...], wout[:, cols(j, 512)]).astype(BF16)

    loop(3, mix_out)
    sums = [scatter(n) for n in range(4)]
    for r in ORDER:
        sums[0][r].start()
    for r in ORDER:
        sums[0][r].wait_recv()

    def middle(i):
        at = pl.ds(i * 32, 32)
        mine = pl.ds(pl.multiple_of(z * 128 + i * 32, 32), 32)
        values = xa[mine, :].astype(F32) + summed(0, i)
        mid[at, :] = values
        scale = lax.rsqrt(jnp.mean(values * values, axis=-1, keepdims=True) + EPS)
        n2[mine, :] = (values * scale * gain_ffn).astype(BF16)

    loop(4, middle)
    for r in ORDER:
        n_all[r].start()
    for r in ORDER:
        sums[0][r].wait_send()
    loads[2].wait()
    loads[3].wait()
    for r in ORDER:
        n_all[r].wait_recv()

    def gate(j):
        at = cols(j, 256)
        gating = dot_nn(n2[...], wg[:, at])
        up_part = dot_nn(n2[...], wu[:, at])
        gt[:, at] = gating
        up[:, at] = up_part
        hd[:, at] = (gating * jax.nn.sigmoid(gating) * up_part).astype(BF16)

    loop(7, gate)
    loads[4].wait()

    def ffn_out(j):
        part[:, cols(j, 256)] = dot_nn(hd[...], wd[:, cols(j, 256)]).astype(BF16)

    loop(6, ffn_out)
    for r in ORDER:
        sums[1][r].start()
    for r in ORDER:
        sums[1][r].wait_recv()

    def finish(i):
        at = pl.ds(i * 32, 32)
        y_ref[at, :] = (mid[at, :] + summed(1, i)).astype(BF16)

    loop(4, finish)

    @pl.when(section == 0)
    def _():
        pl.semaphore_wait(ready, 1)
        to_core_x.start()
        to_core_g.wait_recv()
        for r in ORDER:
            e_all[r].start()

    for r in ORDER:
        sums[1][r].wait_send()
    for r in ORDER:
        e_all[r].wait_recv()

    def back_hidden(j):
        at = cols(j, 256)
        dh = dot_nt(ea[...], wd[at, :])
        gating, up_part = gt[:, at], up[:, at]
        sg = jax.nn.sigmoid(gating)
        dg[:, at] = (dh * up_part * sg * (1.0 + gating * (1.0 - sg))).astype(BF16)
        du[:, at] = (dh * gating * sg).astype(BF16)

    loop(7, back_hidden)

    def back_ffn(j):
        at = cols(j, 256)
        part[:, at] = (dot_nt(dg[...], wg[at, :]) + dot_nt(du[...], wu[at, :])).astype(BF16)

    loop(6, back_ffn)
    for r in ORDER:
        sums[2][r].start()

    def grad_down(j):
        at = cols(j, 256)
        wd[at, :] = dot_tn(hd[:, at], ea[...]).astype(BF16)

    loop(7, grad_down)
    stores = [
        pltpu.make_async_copy(src, dst, store.at[n])
        for n, (src, dst) in enumerate(((win, gin_h), (wout, gout_h), (wg, gg_h), (wu, gu_h), (wd, gd_h)))
    ]
    stores[4].start()
    for r in ORDER:
        sums[2][r].wait_recv()
    gffn_ref[...] = jnp.zeros((1, 1536), F32)
    gmix_ref[...] = jnp.zeros((1, 1536), F32)

    def back_middle(i):
        at = pl.ds(i * 32, 32)
        mine = pl.ds(pl.multiple_of(z * 128 + i * 32, 32), 32)
        dn2 = summed(2, i)
        values = mid[at, :]
        scale = lax.rsqrt(jnp.mean(values * values, axis=-1, keepdims=True) + EPS)
        weighted = dn2 * gain_ffn
        mean_term = jnp.mean(weighted * values, axis=-1, keepdims=True)
        grad = ea[mine, :].astype(F32) + scale * weighted - values * (scale * scale * scale) * mean_term
        gffn_ref[...] += jnp.sum(dn2 * values * scale, axis=0, keepdims=True)
        dmid[at, :] = grad
        fa[mine, :] = grad.astype(BF16)

    loop(4, back_middle)
    for r in ORDER:
        f_all[r].start()

    def grad_gate(j):
        at = cols(j, 256)
        wg[at, :] = dot_tn(n2[:, at], dg[...]).astype(BF16)

    loop(6, grad_gate)
    stores[2].start()

    def grad_up(j):
        at = cols(j, 256)
        wu[at, :] = dot_tn(n2[:, at], du[...]).astype(BF16)

    loop(6, grad_up)
    stores[3].start()
    for r in ORDER:
        sums[2][r].wait_send()
    for r in ORDER:
        f_all[r].wait_recv()

    for zc in range(4):
        dm = dot_nt(fa[zc * 128 : zc * 128 + 128, :], wout[...])
        for mb in range(2):
            r0 = zc * 128 + mb * 64
            piece = dm[mb * 64 : mb * 64 + 64, :]
            dp[r0 : r0 + 64, 384:768] = (piece * cv[r0 : r0 + 64, :]).astype(BF16)
            dce[mb, 64 * zc : 64 * zc + 64, :] = piece * proj[1, r0 : r0 + 64, :]

    @pl.when(has_before)
    def _():
        to_before.start()

    def grad_out(j):
        at = cols(j, 128)
        wout[at, :] = dot_tn(mx[:, at], fa[...]).astype(BF16)

    loop(3, grad_out)
    stores[1].start()
    for k in range(3):
        total = jnp.zeros((1, 384), F32)
        for mb, zc, r0 in blocks:
            t0 = 8 + 64 * zc - k
            total = total + jnp.sum(
                dce[mb, 64 * zc : 64 * zc + 64, :] * ge[mb, t0 : t0 + 64, :], axis=0, keepdims=True
            )
        gtap_ref[k : k + 1, :] = total

    @pl.when(has_after)
    def _():
        to_before.wait_recv()
        dce[:, 256:264, :] = hb[...]

    @pl.when(jnp.logical_not(has_after))
    def _():
        dce[:, 256:264, :] = jnp.zeros((2, 8, 384), F32)

    for mb, zc, r0 in blocks:
        t0 = 64 * zc
        total = tap[0] * dce[mb, t0 : t0 + 64, :]
        for k in (1, 2):
            total = total + tap[k] * dce[mb, t0 + k : t0 + k + 64, :]
        dp[r0 : r0 + 64, 0:384] = (total * proj[2, r0 : r0 + 64, :]).astype(BF16)
        dp[r0 : r0 + 64, 768:1152] = (total * proj[0, r0 : r0 + 64, :]).astype(BF16)

    def back_in(j):
        at = cols(j, 256)
        part[:, at] = dot_nt(dp[...], win[at, :]).astype(BF16)

    loop(6, back_in)
    for r in ORDER:
        sums[3][r].start()

    def grad_in(j):
        at = cols(j, 256)
        win[at, :] = dot_tn(xn[:, at], dp[...]).astype(BF16)

    loop(6, grad_in)
    stores[0].start()
    for r in ORDER:
        sums[3][r].wait_recv()

    def back_input(i):
        at = pl.ds(i * 32, 32)
        mine = pl.ds(pl.multiple_of(z * 128 + i * 32, 32), 32)
        dn = summed(3, i)
        values = xa[mine, :].astype(F32)
        scale = lax.rsqrt(jnp.mean(values * values, axis=-1, keepdims=True) + EPS)
        weighted = dn * gain_mix
        mean_term = jnp.mean(weighted * values, axis=-1, keepdims=True)
        grad = dmid[at, :] + scale * weighted - values * (scale * scale * scale) * mean_term
        gmix_ref[...] += jnp.sum(dn * values * scale, axis=0, keepdims=True)
        gx_ref[at, :] = grad
        g0[at, :] = grad.astype(BF16)

    loop(4, back_input)

    @pl.when(section == 1)
    def _():
        to_core_g.start()
        to_core_g.wait_send()

    @pl.when(section == 0)
    def _():
        to_core_x.wait_send()

    @pl.when(has_after)
    def _():
        to_after.wait_send()

    @pl.when(has_before)
    def _():
        to_before.wait_send()

    for r in ORDER:
        sums[3][r].wait_send()
        for copies in (x_all, n_all, e_all, f_all):
            copies[r].wait_send()
    for copy in stores:
        copy.wait()


def main(x, cot, gains, taps, win, wout, wg, wu, wd):
    shape = jax.ShapeDtypeStruct
    dma = pltpu.SemaphoreType.DMA
    vm = pltpu.VMEM
    return pl.pallas_call(
        main_kernel,
        out_shape=(
            shape((128, 1536), BF16),
            shape((128, 1536), F32),
            shape((1536, 1152), BF16),
            shape((384, 1536), BF16),
            shape((1536, 1792), BF16),
            shape((1536, 1792), BF16),
            shape((1792, 1536), BF16),
            shape((3, 384), F32),
            shape((1, 1536), F32),
            shape((1, 1536), F32),
        ),
        in_specs=[VMEM] * 4 + [ANY] * 5,
        out_specs=[VMEM] * 2 + [ANY] * 5 + [VMEM] * 3,
        scratch_shapes=[
            vm((512, 1536), BF16), vm((512, 1536), BF16), vm((512, 1536), BF16), vm((512, 1536), BF16),
            vm((512, 1536), BF16), vm((512, 1536), BF16), vm((4, 3, 128, 1536), BF16),
            vm((3, 512, 384), F32), vm((2, 264, 384), F32), vm((2, 264, 384), F32), vm((512, 384), F32),
            vm((2, 8, 384), F32), vm((2, 8, 384), F32), vm((512, 384), BF16),
            vm((512, 1792), F32), vm((512, 1792), F32), vm((512, 1792), BF16), vm((512, 1792), BF16),
            vm((512, 1792), BF16), vm((128, 1536), F32), vm((128, 1536), F32), vm((512, 1152), BF16),
            vm((128, 1536), BF16),
            vm((1536, 1152), BF16), vm((384, 1536), BF16), vm((1536, 1792), BF16), vm((1536, 1792), BF16),
            vm((1792, 1536), BF16),
            dma((5,)), dma((5,)), dma((4, 3)), dma((4, 3)), dma((4, 3)), dma((4, 3)),
            dma((2,)), dma((2,)), dma((2,)), dma((2,)), pltpu.SemaphoreType.REGULAR,
        ],
        compiler_params=pltpu.CompilerParams(
            collective_id=1, has_side_effects=True, vmem_limit_bytes=63 * 2**20
        ),
        name="two_blocks",
    )(x, cot, gains, taps, win, wout, wg, wu, wd)


def reduce_kernel(
    g_d, g_g, g_u, g_o, g_in, g_s,
    o_d, o_g, o_u, o_o, o_in, o_s,
    v_d, v_g, v_u, v_o, v_in, v_s,
    q1_g, q1_u, q1_o, q1_in, q1_s,
    p_d, p_g, p_u, p_o, p_in, p_s,
    y_d, y_g, y_u, y_o, y_in, y_s,
    f_d, f_g, f_u, f_o, f_in, f_s,
    t_d, t_g, t_u, t_o, t_in, t_s,
    e_g, e_u, e_in, e_s, b_s,
    load, q_send, q_recv, p_send, p_recv, y_send, y_recv, t_send, t_recv, z_send, z_recv, keep,
):
    section, xl, xh, y, z = place()
    partner, twin, zs, ys = plane_peers()
    grads = (g_d, g_g, g_u, g_o, g_in, g_s)
    held = (v_d, v_g, v_u, v_o, v_in, v_s)
    from_twin = (None, q1_g, q1_u, q1_o, q1_in, q1_s)
    from_partner = (p_d, p_g, p_u, p_o, p_in, p_s)
    from_y = (y_d, y_g, y_u, y_o, y_in, y_s)
    mine = (f_d, f_g, f_u, f_o, f_in, f_s)
    theirs = (t_d, t_g, t_u, t_o, t_in, t_s)
    ended = (None, e_g, e_u, None, e_in, e_s)
    outs = (o_d, o_g, o_u, o_o, o_in, b_s)
    loads = [pltpu.make_async_copy(grads[n], held[n], load.at[n]) for n in range(6)]
    for copy in loads:
        copy.start()
    barrier_all([partner, twin, *zs.values(), *ys.values()])
    near, far = xh * 4, (1 - xh) * 4
    me = near + y
    sent = []
    copies = {}

    def begin(key, copy):
        copy.start()
        copies[key] = copy
        sent.append(copy)

    def half(n, ref, first, h):
        if n == 3:
            return ref.at[pl.ds(first, 4), :, pl.ds(pl.multiple_of(h * 768, 128), 768)]
        return ref.at[pl.ds(first, 4), pl.ds(h * 2, 2)]

    def add(n, first, h, other):
        if n == 0:
            def body(i):
                row, at = i // 7, pl.ds(lax.rem(i, 7) * 32, 32)
                v_d[first + row, at, :] = (v_d[first + row, at, :].astype(F32) + other[row, at, :].astype(F32)).astype(BF16)

            loop(28, body)
        elif n == 3:
            at = pl.ds(pl.multiple_of(h * 768, 128), 768)

            def body(i):
                v_o[first + i, :, at] = (v_o[first + i, :, at].astype(F32) + other[i].astype(F32)).astype(BF16)

            loop(4, body)
        else:
            ref = held[n]

            def body(i):
                a, b = first + i // 2, h * 2 + lax.rem(i, 2)
                ref[a, b] = (ref[a, b].astype(F32) + other[i // 2, lax.rem(i, 2)].astype(F32)).astype(ref.dtype)

            loop(8, body)

    def stage_0(n):
        loads[n].wait()
        if n:
            begin(("q", n), remote(half(n, held[n], far, 1 - xl), from_twin[n], q_send.at[n], q_recv.at[n], twin))
        else:
            begin(("p", n), remote(held[n].at[pl.ds(far, 4)], from_partner[n], p_send.at[n], p_recv.at[n], partner))

    def stage_1(n):
        if n:
            copies["q", n].wait_recv()
            add(n, far, xl, from_twin[n])
            begin(("p", n), remote(half(n, held[n], far, xl), from_partner[n], p_send.at[n], p_recv.at[n], partner))

    def stage_2(n):
        copies["p", n].wait_recv()
        add(n, near, 1 - xl, from_partner[n])
        for r in ORDER:
            row = near + lax.rem(y + r, 4)
            begin(("y", n, r), remote(held[n].at[row], from_y[n].at[r - 1], y_send.at[n, r - 1], y_recv.at[n, r - 1], ys[r]))

    def pieces(n):
        if n == 0:
            return 7, lambda ref, i: ref[pl.ds(i * 32, 32), :]
        if n == 3:
            return 3, lambda ref, i: ref[pl.ds(i * 16, 16), :]
        return 4, lambda ref, i: ref[i]

    def put(n, ref, i, value):
        if n == 0:
            ref[pl.ds(i * 32, 32), :] = value
        elif n == 3:
            ref[pl.ds(i * 16, 16), :] = value
        else:
            ref[i] = value

    def stage_3(n):
        for r in ORDER:
            copies["y", n, r].wait_recv()
        count, get = pieces(n)

        def body(i):
            total = get(held[n].at[me], i).astype(F32)
            for r in range(3):
                total = total + get(from_y[n].at[r], i).astype(F32)
            put(n, mine[n], i, total.astype(mine[n].dtype))

        loop(count, body)
        begin(("t", n), remote(mine[n], theirs[n], t_send.at[n], t_recv.at[n], twin))

    def stage_4(n):
        copies["t", n].wait_recv()
        count, get = pieces(n)
        target = outs[n] if ended[n] is None else ended[n]

        def body(i):
            total = get(mine[n], i).astype(F32) + get(theirs[n], i).astype(F32)
            put(n, target, i, total.astype(target.dtype))

        loop(count, body)
        if ended[n] is not None:
            for r in ORDER:
                begin(("z", n, r), remote(target.at[lax.rem(z + r, 4)], outs[n].at[z], z_send.at[n, r - 1], z_recv.at[n, r - 1], zs[r]))
            copy = pltpu.make_async_copy(target.at[z], outs[n].at[z], keep.at[n])
            copy.start()
            copies["keep", n] = copy

    stages = (stage_0, stage_1, stage_2, stage_3, stage_4)
    for step in range(10):
        for s, stage in enumerate(stages):
            if 0 <= step - s < 6:
                stage(step - s)
    for n in (1, 2, 4, 5):
        copies["keep", n].wait()
        for r in ORDER:
            copies["z", n, r].wait_recv()
    o_s[...] = b_s[0] + b_s[1] + b_s[2] + b_s[3]
    for copy in sent:
        copy.wait_send()


def reduce(g_d, g_g, g_u, g_o, g_in, g_s):
    shape = jax.ShapeDtypeStruct
    dma = pltpu.SemaphoreType.DMA
    vm = pltpu.VMEM
    big = ((4, 48, 1792), (4, 48, 1792), (4, 48, 1152))
    return pl.pallas_call(
        reduce_kernel,
        out_shape=(
            shape((224, 1536), F32),
            shape((4, 48, 1792), BF16),
            shape((4, 48, 1792), BF16),
            shape((48, 1536), F32),
            shape((4, 48, 1152), BF16),
            shape((8, 128), F32),
        ),
        in_specs=[ANY] * 6,
        out_specs=[VMEM, ANY, ANY, VMEM, ANY, VMEM],
        scratch_shapes=[
            vm((8, 224, 1536), BF16), vm((8, 4, 48, 1792), BF16), vm((8, 4, 48, 1792), BF16),
            vm((8, 48, 1536), BF16), vm((8, 4, 48, 1152), BF16), vm((8, 4, 8, 128), F32),
            vm((4, 2, 48, 1792), BF16), vm((4, 2, 48, 1792), BF16), vm((4, 48, 768), BF16),
            vm((4, 2, 48, 1152), BF16), vm((4, 2, 8, 128), F32),
            vm((4, 224, 1536), BF16), vm((4, 2, 48, 1792), BF16), vm((4, 2, 48, 1792), BF16),
            vm((4, 48, 768), BF16), vm((4, 2, 48, 1152), BF16), vm((4, 2, 8, 128), F32),
            vm((3, 224, 1536), BF16), vm((3, 4, 48, 1792), BF16), vm((3, 4, 48, 1792), BF16),
            vm((3, 48, 1536), BF16), vm((3, 4, 48, 1152), BF16), vm((3, 4, 8, 128), F32),
            vm((224, 1536), BF16), vm(big[0], BF16), vm(big[1], BF16), vm((48, 1536), BF16), vm(big[2], BF16),
            vm((4, 8, 128), F32),
            vm((224, 1536), BF16), vm(big[0], BF16), vm(big[1], BF16), vm((48, 1536), BF16), vm(big[2], BF16),
            vm((4, 8, 128), F32),
            vm(big[0], BF16), vm(big[1], BF16), vm(big[2], BF16), vm((4, 8, 128), F32), vm((4, 8, 128), F32),
            dma((6,)), dma((6,)), dma((6,)), dma((6,)), dma((6,)), dma((6, 3)), dma((6, 3)),
            dma((6,)), dma((6,)), dma((6, 3)), dma((6, 3)), dma((6,)),
        ],
        compiler_params=pltpu.CompilerParams(
            collective_id=2, has_side_effects=True, vmem_limit_bytes=63 * 2**20
        ),
        name="reduce_grads",
    )(g_d, g_g, g_u, g_o, g_in, g_s)


def cut_ffn(weight):
    tiles = jnp.pad(weight.reshape(48, 8, 4, 216), ((0, 0), (0, 0), (0, 0), (0, 8)))
    return tiles.transpose(2, 0, 1, 3).reshape(4, 48, 1792)


def uncut_ffn(value):
    tiles = value.reshape(4, 48, 8, 224)[..., :216]
    return tiles.transpose(1, 2, 0, 3).reshape(1, 48, 6912).astype(F32)


def local(inputs, cotangent, w_in, w_out, w_gate, w_up, w_down, kernel, gain_mix, gain_ffn):
    a_in = w_in.reshape(48, 3, 8, 4, 48).transpose(3, 0, 1, 2, 4).reshape(4, 48, 1152)
    small = jnp.concatenate([kernel[0], gain_mix, gain_ffn], axis=0)
    small = jnp.pad(small, ((0, 11), (0, 80)))
    s_all, win, wout, wg, wu, wd = gather(
        small, a_in, cut_ffn(w_gate[0]), cut_ffn(w_up[0]), w_out[0], jnp.pad(w_down[0], ((0, 8), (0, 0)))
    )
    z = lax.axis_index("z")
    gains = s_all[:, :, 3:5, :48].astype(F32).transpose(2, 0, 1, 3).reshape(2, 1536)
    own_taps = lax.dynamic_index_in_dim(s_all, z, axis=1, keepdims=False)[:, 0:3, :48]
    taps = own_taps.astype(F32).transpose(1, 0, 2).reshape(3, 384)
    y, gx, g_in, g_o, g_g, g_u, g_d, g_tap, g_mix, g_ffn = main(
        inputs.reshape(128, 1536),
        cotangent.reshape(128, 1536),
        gains,
        taps,
        win.reshape(1536, 1152),
        wout.reshape(384, 1536),
        wg.reshape(1536, 1792),
        wu.reshape(1536, 1792),
        wd.reshape(1792, 1536),
    )
    tap_rows = g_tap.reshape(3, 8, 48).transpose(1, 0, 2)
    at_z = (lax.broadcasted_iota(jnp.int32, (1, 4, 1, 1), 1) == z).astype(F32)
    tap_rows = tap_rows[:, None] * at_z
    gain_rows = jnp.stack([g_mix.reshape(8, 4, 48), g_ffn.reshape(8, 4, 48)], axis=2)
    g_s = jnp.pad(jnp.concatenate([tap_rows, gain_rows], axis=2), ((0, 0), (0, 0), (0, 3), (0, 80)))
    o_d, o_g, o_u, o_o, o_in, o_s = reduce(
        g_d.reshape(8, 224, 1536),
        g_g.reshape(8, 4, 48, 1792),
        g_u.reshape(8, 4, 48, 1792),
        g_o.reshape(8, 48, 1536),
        g_in.reshape(8, 4, 48, 1152),
        g_s,
    )
    grad_in = o_in.reshape(4, 48, 3, 8, 48).transpose(1, 2, 3, 0, 4).reshape(1, 48, 4608).astype(F32)
    return (
        y.reshape(1, 2, 64, 1536),
        gx.reshape(1, 2, 64, 1536),
        grad_in,
        o_o[None],
        uncut_ffn(o_g),
        uncut_ffn(o_u),
        o_d[None, :216],
        o_s[None, 0:3, :48],
        o_s[3:4, :48],
        o_s[4:5, :48],
    )


def solution(mesh):
    names = ("section", "xl", "xh", "y", "z")
    fine = Mesh(mesh.devices.reshape(2, 2, 2, 4, 4), names)
    tokens, shard = ("xl", "xh", "y", "z"), ("xh", "y", "z")
    weight = P("section", shard, None)
    acts = P("section", None, tokens, None)
    return jax.shard_map(
        local,
        mesh=fine,
        in_specs=(
            P(None, tokens, None),
            P(None, tokens, None),
            weight,
            weight,
            weight,
            weight,
            weight,
            P("section", None, shard),
            P("section", shard),
            P("section", shard),
        ),
        out_specs=(
            acts,
            acts,
            weight,
            weight,
            weight,
            weight,
            weight,
            P("section", None, shard),
            P("section", shard),
            P("section", shard),
        ),
        check_vma=False,
    )
```

```python
import functools

import jax
import jax.numpy as jnp
from jax import lax
from jax.experimental import pallas as pl
from jax.experimental.pallas import tpu as pltpu
from jax.sharding import Mesh
from jax.sharding import PartitionSpec as P

F32, BF16 = jnp.float32, jnp.bfloat16
MESH = pl.DeviceIdType.MESH
EPS = 1e-06
ANY = pl.BlockSpec(memory_space=pl.ANY)
VMEM = pl.BlockSpec(memory_space=pltpu.VMEM)
ORDER = (1, 3, 2)

GATHER_UNITS = (
    (0, 0, 128), (1, 0, 1152), (2, 0, 1536),
    (3, 0, 640), (4, 0, 640), (3, 640, 640), (4, 640, 640), (3, 1280, 512), (4, 1280, 512),
    (5, 0, 80), (5, 80, 80), (5, 160, 64),
)
REDUCE_UNITS = (
    (0, 0, 80), (0, 80, 80), (0, 160, 64),
    (1, 0, 640), (1, 640, 640), (1, 1280, 512), (2, 0, 640), (2, 640, 640), (2, 1280, 512),
    (3, 0, 1536), (4, 0, 640), (4, 640, 512), (5, 0, 128),
)


def place():
    return tuple(lax.axis_index(name) for name in ("section", "xl", "xh", "y", "z"))


def barrier_all(devices):
    barrier = pltpu.get_barrier_semaphore()
    for device in devices:
        pl.semaphore_signal(barrier, inc=1, device_id=device, device_id_type=MESH)
    pl.semaphore_wait(barrier, len(devices))


def remote(src, dst, send, recv, device):
    return pltpu.make_async_remote_copy(
        src_ref=src, dst_ref=dst, send_sem=send, recv_sem=recv, device_id=device, device_id_type=MESH
    )


def plane_peers():
    section, xl, xh, y, z = place()
    partner = {"xh": 1 - xh, "xl": 1 - xl}
    twin = {"xl": 1 - xl}
    zs = {r: {"z": lax.rem(z + r, 4)} for r in ORDER}
    ys = {r: {"y": lax.rem(y + r, 4)} for r in ORDER}
    return partner, twin, zs, ys


def gather_kernel(
    a_s, a_in, a_g, a_u, w_o, w_d,
    o_s, o_in, o_o, o_g, o_u, o_d,
    z_send, z_recv, y_send, y_recv, p_send, p_recv, q_send, q_recv, local, go,
):
    section, xl, xh, y, z = place()
    partner, twin, zs, ys = plane_peers()
    core = {"section": 1 - section}
    barrier_all([partner, twin, core, *zs.values(), *ys.values()])

    @pl.when(section == 1)
    def _():
        pl.semaphore_wait(go, 1)

    me = xh * 4 + y
    outs = (o_s, o_in, o_o, o_g, o_u, o_d)
    cut = (a_s, a_in, None, a_g, a_u, None)
    whole = (None, None, w_o, None, None, w_d)

    def piece(u, row):
        n, first, size = GATHER_UNITS[u]
        if n == 2:
            return outs[n].at[row]
        if n == 5:
            return outs[n].at[row, pl.ds(first, size)]
        return outs[n].at[row, :, :, pl.ds(first, size)]

    def half(u, row, h):
        n, first, size = GATHER_UNITS[u]
        if n == 2:
            return outs[n].at[row, :, pl.ds(pl.multiple_of(h * 768, 128), 768)]
        if n == 5:
            return outs[n].at[row, pl.ds(first, size), pl.ds(pl.multiple_of(h * 768, 128), 768)]
        return outs[n].at[row, pl.ds(h * 2, 2), :, pl.ds(first, size)]

    sent, locals_, z_copies = [], {}, {}
    for n in range(6):
        if cut[n] is not None:
            block = (lambda zz: a_s) if n == 0 else (lambda zz, a=cut[n]: a.at[zz])
            for r in ORDER:
                copy = remote(block(lax.rem(z + r, 4)), outs[n].at[me, z], z_send.at[n, r - 1], z_recv.at[n, r - 1], zs[r])
                copy.start()
                z_copies[n, r] = copy
                sent.append(copy)
            own = pltpu.make_async_copy(block(z), outs[n].at[me, z], local.at[n])
        else:
            own = pltpu.make_async_copy(whole[n], outs[n].at[me], local.at[n])
        own.start()
        locals_[n] = own

    y_copies, p_copies, q_copies, ready = {}, {}, {}, set()

    def stage_y(u):
        n = GATHER_UNITS[u][0]
        if n not in ready:
            ready.add(n)
            locals_[n].wait()
            if cut[n] is not None:
                for r in ORDER:
                    z_copies[n, r].wait_recv()
        for r in ORDER:
            src = piece(u, me)
            copy = remote(src, src, y_send.at[u, r - 1], y_recv.at[u, r - 1], ys[r])
            copy.start()
            y_copies[u, r] = copy
            sent.append(copy)
        push_p(u, 0)

    def push_p(u, r):
        src = half(u, xh * 4 + lax.rem(y + 4 - r, 4), xl)
        copy = remote(src, src, p_send.at[u, r], p_recv.at[u, r], partner)
        copy.start()
        p_copies[u, r] = copy
        sent.append(copy)

    def stage_p(u):
        for r in ORDER:
            y_copies[u, r].wait_recv()
            push_p(u, r)

    def stage_q(u):
        for r in (0, *ORDER):
            p_copies[u, r].wait_recv()
            src = half(u, (1 - xh) * 4 + lax.rem(y + 4 - r, 4), 1 - xl)
            copy = remote(src, src, q_send.at[u, r], q_recv.at[u, r], twin)
            copy.start()
            q_copies[u, r] = copy
            sent.append(copy)

    count = len(GATHER_UNITS)
    for step in range(count + 4):
        if step < count:
            stage_y(step)
        if 0 <= step - 2 < count:
            stage_p(step - 2)
        if step - 2 == count - 1:

            @pl.when(section == 0)
            def _():
                pl.semaphore_signal(go, inc=1, device_id=core, device_id_type=MESH)

        if 0 <= step - 4 < count:
            stage_q(step - 4)
    for copy in q_copies.values():
        copy.wait_recv()
    for copy in sent:
        copy.wait_send()


def gather(a_s, a_in, a_g, a_u, w_o, w_d):
    shape = jax.ShapeDtypeStruct
    dma = pltpu.SemaphoreType.DMA
    count = len(GATHER_UNITS)
    return pl.pallas_call(
        gather_kernel,
        out_shape=(
            shape((8, 4, 16, 128), BF16),
            shape((8, 4, 48, 1152), BF16),
            shape((8, 48, 1536), BF16),
            shape((8, 4, 48, 1792), BF16),
            shape((8, 4, 48, 1792), BF16),
            shape((8, 224, 1536), BF16),
        ),
        in_specs=[ANY] * 6,
        out_specs=[ANY] * 6,
        scratch_shapes=[
            dma((6, 3)), dma((6, 3)), dma((count, 3)), dma((count, 3)),
            dma((count, 4)), dma((count, 4)), dma((count, 4)), dma((count, 4)),
            dma((6,)), pltpu.SemaphoreType.REGULAR,
        ],
        compiler_params=pltpu.CompilerParams(collective_id=0, has_side_effects=True),
        name="gather_weights",
    )(a_s, a_in, a_g, a_u, w_o, w_d)


def dot_nn(a, b):
    return lax.dot_general(a, b, (((1,), (0,)), ((), ())), preferred_element_type=F32)


def dot_nt(a, b):
    return lax.dot_general(a, b, (((1,), (1,)), ((), ())), preferred_element_type=F32)


def dot_tn(a, b):
    return lax.dot_general(a, b, (((0,), (0,)), ((), ())), preferred_element_type=F32)


def cols(j, width):
    return pl.ds(pl.multiple_of(j * width, width), width)


def loop(count, body):
    def step(j, carry):
        body(j)
        return carry

    lax.fori_loop(0, count, step, 0)


def main_kernel(
    x_ref, cot_ref, gains, taps, win_h, wout_h, wg_h, wu_h, wd_h,
    y_ref, gx_ref, gin_h, gout_h, gg_h, gu_h, gd_h, gtap_ref, gmix_ref, gffn_ref,
    xa, xn, n2, ea, fa, part, rr, proj, ge, dce, cv, ha, hb, mx, gt, up, hd, dg, du,
    mid, dmid, dp, g0, win, wout, wg, wu, wd,
    load, store, a_send, a_recv, s_send, s_recv, h_send, h_recv, c_send, c_recv, ready,
):
    section, xl, xh, y, z = place()
    zs = {r: {"z": lax.rem(z + r, 4)} for r in ORDER}
    core = {"section": 1 - section}
    group = xl * 8 + xh * 4 + y
    after, before = lax.rem(group + 1, 16), lax.rem(group + 15, 16)

    def at_group(g):
        return {"xl": g // 8, "xh": lax.rem(g // 4, 2), "y": lax.rem(g, 4)}

    has_after, has_before = group < 15, group > 0
    barrier = pltpu.get_barrier_semaphore()

    def hail(device):
        pl.semaphore_signal(barrier, inc=1, device_id=device, device_id_type=MESH)

    loads = [
        pltpu.make_async_copy(src, dst, load.at[n])
        for n, (src, dst) in enumerate(((win_h, win), (wout_h, wout), (wg_h, wg), (wu_h, wu), (wd_h, wd)))
    ]
    for copy in loads:
        copy.start()

    for r in ORDER:
        hail(zs[r])

    @pl.when(has_after)
    def _():
        hail(at_group(after))

    @pl.when(has_before)
    def _():
        hail(at_group(before))

    @pl.when(section == 0)
    def _():
        hail(core)

    pl.semaphore_wait(barrier, 4 - (group + 1) // 16 + (group + 15) // 16 + section)

    @pl.when(section == 1)
    def _():
        pl.semaphore_signal(ready, inc=1, device_id=core, device_id_type=MESH)

    own = pl.ds(pl.multiple_of(z * 128, 128), 128)

    def rows_from(r):
        return pl.multiple_of(lax.rem(z + 4 - r, 4) * 128, 128)

    def spread(n, buf):
        return {r: remote(buf.at[own], buf.at[own], a_send.at[n, r - 1], a_recv.at[n, r - 1], zs[r]) for r in ORDER}

    def scatter(n, j, r):
        at = cols(j, 256)
        src = part.at[pl.ds(pl.multiple_of(lax.rem(z + r, 4) * 128, 128), 128), at]
        return remote(src, rr.at[n, r - 1, :, at], s_send.at[n, j, r - 1], s_recv.at[n, j, r - 1], zs[r])

    def sum_over_z(n, block):
        def body(j):
            part[:, cols(j, 256)] = block(j).astype(BF16)
            for r in ORDER:
                scatter(n, j, r).start()

        loop(6, body)

    def sum_arrived(n):
        def body(j):
            for r in ORDER:
                scatter(n, j, r).wait_recv()

        loop(6, body)

    def sum_sent(n):
        def body(j):
            for r in ORDER:
                scatter(n, j, r).wait_send()

        loop(6, body)

    def summed(n, i):
        at = pl.ds(i * 32, 32)
        total = part[pl.ds(pl.multiple_of(z * 128 + i * 32, 32), 32), :].astype(F32)
        for r in range(3):
            total = total + rr[n, r, at, :].astype(F32)
        return total

    x_all, n_all, e_all, f_all = spread(0, xa), spread(1, n2), spread(2, ea), spread(3, fa)
    to_core_x = remote(y_ref, xa.at[own], c_send.at[0], c_recv.at[0], core)
    to_core_g = remote(g0, ea.at[own], c_send.at[1], c_recv.at[1], core)

    @pl.when(section == 0)
    def _():
        xa[own, :] = x_ref[...]

    @pl.when(section == 1)
    def _():
        ea[own, :] = cot_ref[...]
        for r in ORDER:
            e_all[r].start()
        to_core_x.wait_recv()

    for r in ORDER:
        x_all[r].start()

    gain_mix, gain_ffn = gains[0:1, :], gains[1:2, :]

    def norm_rows(base):
        def body(i):
            at = pl.ds(pl.multiple_of(base + i * 32, 32), 32)
            values = xa[at, :].astype(F32)
            scale = lax.rsqrt(jnp.mean(values * values, axis=-1, keepdims=True) + EPS)
            xn[at, :] = (values * scale * gain_mix).astype(BF16)

        loop(4, body)

    norm_rows(pl.multiple_of(z * 128, 128))
    for r in ORDER:
        x_all[r].wait_recv()
        norm_rows(rows_from(r))

    loads[0].wait()

    def project(j):
        proj[j] = dot_nn(xn[...], win[:, cols(j, 384)])

    loop(3, project)

    blocks = [(mb, zc, zc * 128 + mb * 64) for mb in range(2) for zc in range(4)]
    for mb, zc, r0 in blocks:
        ge[mb, 8 + 64 * zc : 72 + 64 * zc, :] = proj[0, r0 : r0 + 64, :] * proj[2, r0 : r0 + 64, :]

    to_after = remote(ge.at[:, pl.ds(256, 8)], ha, h_send.at[0], h_recv.at[0], at_group(after))
    to_before = remote(dce.at[:, pl.ds(0, 8)], hb, h_send.at[1], h_recv.at[1], at_group(before))

    @pl.when(has_after)
    def _():
        to_after.start()

    @pl.when(has_before)
    def _():
        to_after.wait_recv()
        ge[:, 0:8, :] = ha[...]

    @pl.when(jnp.logical_not(has_before))
    def _():
        ge[:, 0:8, :] = jnp.zeros((2, 8, 384), F32)

    tap = [taps[k : k + 1, :] for k in range(3)]
    for mb, zc, r0 in blocks:
        t0 = 8 + 64 * zc
        total = tap[0] * ge[mb, t0 : t0 + 64, :]
        for k in (1, 2):
            total = total + tap[k] * ge[mb, t0 - k : t0 - k + 64, :]
        cv[r0 : r0 + 64, :] = total
        mx[r0 : r0 + 64, :] = (proj[1, r0 : r0 + 64, :] * total).astype(BF16)

    loads[1].wait()

    sum_over_z(0, lambda j: dot_nn(mx[...], wout[:, cols(j, 256)]))
    sum_arrived(0)

    def middle(i):
        at = pl.ds(i * 32, 32)
        mine = pl.ds(pl.multiple_of(z * 128 + i * 32, 32), 32)
        values = xa[mine, :].astype(F32) + summed(0, i)
        mid[at, :] = values
        scale = lax.rsqrt(jnp.mean(values * values, axis=-1, keepdims=True) + EPS)
        n2[mine, :] = (values * scale * gain_ffn).astype(BF16)

    loop(4, middle)
    for r in ORDER:
        n_all[r].start()
    sum_sent(0)
    loads[2].wait()
    loads[3].wait()
    for r in ORDER:
        n_all[r].wait_recv()

    def gate(j):
        at = cols(j, 256)
        gating = dot_nn(n2[...], wg[:, at])
        up_part = dot_nn(n2[...], wu[:, at])
        gt[:, at] = gating
        up[:, at] = up_part
        hd[:, at] = (gating * jax.nn.sigmoid(gating) * up_part).astype(BF16)

    loop(7, gate)
    loads[4].wait()

    sum_over_z(1, lambda j: dot_nn(hd[...], wd[:, cols(j, 256)]))
    sum_arrived(1)

    def finish(i):
        at = pl.ds(i * 32, 32)
        y_ref[at, :] = (mid[at, :] + summed(1, i)).astype(BF16)

    loop(4, finish)

    @pl.when(section == 0)
    def _():
        pl.semaphore_wait(ready, 1)
        to_core_x.start()
        to_core_g.wait_recv()
        for r in ORDER:
            e_all[r].start()

    sum_sent(1)
    for r in ORDER:
        e_all[r].wait_recv()

    def back_hidden(j):
        at = cols(j, 256)
        dh = dot_nt(ea[...], wd[at, :])
        gating, up_part = gt[:, at], up[:, at]
        sg = jax.nn.sigmoid(gating)
        dg[:, at] = (dh * up_part * sg * (1.0 + gating * (1.0 - sg))).astype(BF16)
        du[:, at] = (dh * gating * sg).astype(BF16)

    loop(7, back_hidden)

    sum_over_z(2, lambda j: dot_nt(dg[...], wg[cols(j, 256), :]) + dot_nt(du[...], wu[cols(j, 256), :]))

    def grad_down(j):
        at = cols(j, 256)
        wd[at, :] = dot_tn(hd[:, at], ea[...]).astype(BF16)

    loop(7, grad_down)
    stores = [
        pltpu.make_async_copy(src, dst, store.at[n])
        for n, (src, dst) in enumerate(((win, gin_h), (wout, gout_h), (wg, gg_h), (wu, gu_h), (wd, gd_h)))
    ]
    stores[4].start()
    sum_arrived(2)
    gffn_ref[...] = jnp.zeros((1, 1536), F32)
    gmix_ref[...] = jnp.zeros((1, 1536), F32)

    def back_middle(i):
        at = pl.ds(i * 32, 32)
        mine = pl.ds(pl.multiple_of(z * 128 + i * 32, 32), 32)
        dn2 = summed(2, i)
        values = mid[at, :]
        scale = lax.rsqrt(jnp.mean(values * values, axis=-1, keepdims=True) + EPS)
        weighted = dn2 * gain_ffn
        mean_term = jnp.mean(weighted * values, axis=-1, keepdims=True)
        grad = ea[mine, :].astype(F32) + scale * weighted - values * (scale * scale * scale) * mean_term
        gffn_ref[...] += jnp.sum(dn2 * values * scale, axis=0, keepdims=True)
        dmid[at, :] = grad
        fa[mine, :] = grad.astype(BF16)

    loop(4, back_middle)
    for r in ORDER:
        f_all[r].start()

    def grad_gate(j):
        at = cols(j, 256)
        wg[at, :] = dot_tn(n2[:, at], dg[...]).astype(BF16)

    loop(6, grad_gate)
    stores[2].start()

    def grad_up(j):
        at = cols(j, 256)
        wu[at, :] = dot_tn(n2[:, at], du[...]).astype(BF16)

    loop(6, grad_up)
    stores[3].start()
    sum_sent(2)
    for r in ORDER:
        f_all[r].wait_recv()

    for zc in range(4):
        dm = dot_nt(fa[zc * 128 : zc * 128 + 128, :], wout[...])
        for mb in range(2):
            r0 = zc * 128 + mb * 64
            piece = dm[mb * 64 : mb * 64 + 64, :]
            dp[r0 : r0 + 64, 384:768] = (piece * cv[r0 : r0 + 64, :]).astype(BF16)
            dce[mb, 64 * zc : 64 * zc + 64, :] = piece * proj[1, r0 : r0 + 64, :]

    @pl.when(has_before)
    def _():
        to_before.start()

    def grad_out(j):
        at = cols(j, 128)
        wout[at, :] = dot_tn(mx[:, at], fa[...]).astype(BF16)

    loop(3, grad_out)
    stores[1].start()
    for k in range(3):
        total = jnp.zeros((1, 384), F32)
        for mb, zc, r0 in blocks:
            t0 = 8 + 64 * zc - k
            total = total + jnp.sum(
                dce[mb, 64 * zc : 64 * zc + 64, :] * ge[mb, t0 : t0 + 64, :], axis=0, keepdims=True
            )
        gtap_ref[k : k + 1, :] = total

    @pl.when(has_after)
    def _():
        to_before.wait_recv()
        dce[:, 256:264, :] = hb[...]

    @pl.when(jnp.logical_not(has_after))
    def _():
        dce[:, 256:264, :] = jnp.zeros((2, 8, 384), F32)

    for mb, zc, r0 in blocks:
        t0 = 64 * zc
        total = tap[0] * dce[mb, t0 : t0 + 64, :]
        for k in (1, 2):
            total = total + tap[k] * dce[mb, t0 + k : t0 + k + 64, :]
        dp[r0 : r0 + 64, 0:384] = (total * proj[2, r0 : r0 + 64, :]).astype(BF16)
        dp[r0 : r0 + 64, 768:1152] = (total * proj[0, r0 : r0 + 64, :]).astype(BF16)

    sum_over_z(3, lambda j: dot_nt(dp[...], win[cols(j, 256), :]))

    def grad_in(j):
        at = cols(j, 256)
        win[at, :] = dot_tn(xn[:, at], dp[...]).astype(BF16)

    loop(6, grad_in)
    stores[0].start()
    sum_arrived(3)

    def back_input(i):
        at = pl.ds(i * 32, 32)
        mine = pl.ds(pl.multiple_of(z * 128 + i * 32, 32), 32)
        dn = summed(3, i)
        values = xa[mine, :].astype(F32)
        scale = lax.rsqrt(jnp.mean(values * values, axis=-1, keepdims=True) + EPS)
        weighted = dn * gain_mix
        mean_term = jnp.mean(weighted * values, axis=-1, keepdims=True)
        grad = dmid[at, :] + scale * weighted - values * (scale * scale * scale) * mean_term
        gmix_ref[...] += jnp.sum(dn * values * scale, axis=0, keepdims=True)
        gx_ref[at, :] = grad
        g0[at, :] = grad.astype(BF16)

    loop(4, back_input)

    @pl.when(section == 1)
    def _():
        to_core_g.start()
        to_core_g.wait_send()

    @pl.when(section == 0)
    def _():
        to_core_x.wait_send()

    @pl.when(has_after)
    def _():
        to_after.wait_send()

    @pl.when(has_before)
    def _():
        to_before.wait_send()

    sum_sent(3)
    for r in ORDER:
        for copies in (x_all, n_all, e_all, f_all):
            copies[r].wait_send()
    for copy in stores:
        copy.wait()


def main(x, cot, gains, taps, win, wout, wg, wu, wd):
    shape = jax.ShapeDtypeStruct
    dma = pltpu.SemaphoreType.DMA
    vm = pltpu.VMEM
    return pl.pallas_call(
        main_kernel,
        out_shape=(
            shape((128, 1536), BF16),
            shape((128, 1536), F32),
            shape((1536, 1152), BF16),
            shape((384, 1536), BF16),
            shape((1536, 1792), BF16),
            shape((1536, 1792), BF16),
            shape((1792, 1536), BF16),
            shape((3, 384), F32),
            shape((1, 1536), F32),
            shape((1, 1536), F32),
        ),
        in_specs=[VMEM] * 4 + [ANY] * 5,
        out_specs=[VMEM] * 2 + [ANY] * 5 + [VMEM] * 3,
        scratch_shapes=[
            vm((512, 1536), BF16), vm((512, 1536), BF16), vm((512, 1536), BF16), vm((512, 1536), BF16),
            vm((512, 1536), BF16), vm((512, 1536), BF16), vm((4, 3, 128, 1536), BF16),
            vm((3, 512, 384), F32), vm((2, 264, 384), F32), vm((2, 264, 384), F32), vm((512, 384), F32),
            vm((2, 8, 384), F32), vm((2, 8, 384), F32), vm((512, 384), BF16),
            vm((512, 1792), F32), vm((512, 1792), F32), vm((512, 1792), BF16), vm((512, 1792), BF16),
            vm((512, 1792), BF16), vm((128, 1536), F32), vm((128, 1536), F32), vm((512, 1152), BF16),
            vm((128, 1536), BF16),
            vm((1536, 1152), BF16), vm((384, 1536), BF16), vm((1536, 1792), BF16), vm((1536, 1792), BF16),
            vm((1792, 1536), BF16),
            dma((5,)), dma((5,)), dma((4, 3)), dma((4, 3)), dma((4, 6, 3)), dma((4, 6, 3)),
            dma((2,)), dma((2,)), dma((2,)), dma((2,)), pltpu.SemaphoreType.REGULAR,
        ],
        compiler_params=pltpu.CompilerParams(
            collective_id=1, has_side_effects=True, vmem_limit_bytes=63 * 2**20
        ),
        name="two_blocks",
    )(x, cot, gains, taps, win, wout, wg, wu, wd)


def reduce_kernel(
    g_d, g_g, g_u, g_o, g_in, g_s,
    o_d, o_g, o_u, o_o, o_in, o_s,
    v_d, v_g, v_u, v_o, v_in, v_s,
    q1_g, q1_u, q1_o, q1_in, q1_s,
    p_d, p_g, p_u, p_o, p_in, p_s,
    y_d, y_g, y_u, y_o, y_in, y_s,
    f_d, f_g, f_u, f_o, f_in, f_s,
    t_d, t_g, t_u, t_o, t_in, t_s,
    e_g, e_u, e_in, e_s, b_s,
    load, q_send, q_recv, p_send, p_recv, y_send, y_recv, t_send, t_recv, z_send, z_recv, keep,
):
    section, xl, xh, y, z = place()
    partner, twin, zs, ys = plane_peers()
    grads = (g_d, g_g, g_u, g_o, g_in, g_s)
    held = (v_d, v_g, v_u, v_o, v_in, v_s)
    from_twin = (None, q1_g, q1_u, q1_o, q1_in, q1_s)
    from_partner = (p_d, p_g, p_u, p_o, p_in, p_s)
    from_y = (y_d, y_g, y_u, y_o, y_in, y_s)
    mine = (f_d, f_g, f_u, f_o, f_in, f_s)
    theirs = (t_d, t_g, t_u, t_o, t_in, t_s)
    ended = (None, e_g, e_u, None, e_in, e_s)
    outs = (o_d, o_g, o_u, o_o, o_in, b_s)
    loads = [pltpu.make_async_copy(grads[n], held[n], load.at[n]) for n in range(6)]
    for copy in loads:
        copy.start()
    barrier_all([partner, twin, *zs.values(), *ys.values()])
    near, far = xh * 4, (1 - xh) * 4
    me = near + y
    sent = []
    copies = {}

    def begin(key, copy):
        copy.start()
        copies[key] = copy
        sent.append(copy)

    def half(u, ref, first, h):
        n, c0, size = REDUCE_UNITS[u]
        if n == 3:
            return ref.at[pl.ds(first, 4), :, pl.ds(pl.multiple_of(h * 768, 128), 768)]
        return ref.at[pl.ds(first, 4), pl.ds(h * 2, 2), :, pl.ds(c0, size)]

    def arrived(u, ref):
        n, c0, size = REDUCE_UNITS[u]
        return ref if n == 3 else ref.at[:, :, :, pl.ds(c0, size)]

    def row_of(u, ref, *lead):
        n, c0, size = REDUCE_UNITS[u]
        if n == 0:
            return ref.at[*lead, pl.ds(c0, size)]
        if n == 3:
            return ref.at[*lead] if lead else ref
        return ref.at[*lead, :, :, pl.ds(c0, size)]

    def add(u, first, h, other):
        n, c0, size = REDUCE_UNITS[u]
        if n == 0:
            rows = size // 16

            def body(i):
                row, at = i // rows, pl.ds(pl.multiple_of(c0 + lax.rem(i, rows) * 16, 16), 16)
                v_d[first + row, at, :] = v_d[first + row, at, :] + other[row, at, :]

            loop(4 * rows, body)
        elif n == 3:
            at = pl.ds(pl.multiple_of(h * 768, 128), 768)

            def body(i):
                v_o[first + i, :, at] = v_o[first + i, :, at] + other[i]

            loop(4, body)
        else:
            ref, at = held[n], slice(c0, c0 + size)

            def body(i):
                a, b = first + i // 2, h * 2 + lax.rem(i, 2)
                ref[a, b, :, at] = ref[a, b, :, at] + other[i // 2, lax.rem(i, 2), :, at]

            loop(8, body)

    def stage_0(u):
        n = REDUCE_UNITS[u][0]
        if n not in ready:
            ready.add(n)
            loads[n].wait()
        if n:
            dst = arrived(u, from_twin[n])
            begin(("q", u), remote(half(u, held[n], far, 1 - xl), dst, q_send.at[u], q_recv.at[u], twin))
        else:
            begin_p(u, held[n].at[pl.ds(far, 4), pl.ds(*REDUCE_UNITS[u][1:])])

    def begin_p(u, src):
        n, c0, size = REDUCE_UNITS[u]
        dst = from_partner[n].at[:, pl.ds(c0, size)] if n == 0 else arrived(u, from_partner[n])
        begin(("p", u), remote(src, dst, p_send.at[u], p_recv.at[u], partner))

    def stage_1(u):
        n = REDUCE_UNITS[u][0]
        if n:
            copies["q", u].wait_recv()
            add(u, far, xl, from_twin[n])
            begin_p(u, half(u, held[n], far, xl))

    def stage_2(u):
        n = REDUCE_UNITS[u][0]
        copies["p", u].wait_recv()
        add(u, near, 1 - xl, from_partner[n])
        for r in ORDER:
            src, dst = row_of(u, held[n], near + lax.rem(y + r, 4)), row_of(u, from_y[n], r - 1)
            begin(("y", u, r), remote(src, dst, y_send.at[u, r - 1], y_recv.at[u, r - 1], ys[r]))

    def blocks(u):
        n, c0, size = REDUCE_UNITS[u]
        if n == 0:
            return size // 16, lambda i: (pl.ds(pl.multiple_of(c0 + i * 16, 16), 16), slice(None))
        if n == 3:
            return 3, lambda i: (pl.ds(pl.multiple_of(i * 16, 16), 16), slice(None))
        return 4, lambda i: (i, slice(None), slice(c0, c0 + size))

    def stage_3(u):
        n = REDUCE_UNITS[u][0]
        for r in ORDER:
            copies["y", u, r].wait_recv()
        number, at = blocks(u)

        def body(i):
            total = held[n][me, *at(i)].astype(F32)
            for r in range(3):
                total = total + from_y[n][r, *at(i)].astype(F32)
            mine[n][at(i)] = total.astype(mine[n].dtype)

        loop(number, body)
        begin(("t", u), remote(row_of(u, mine[n]), row_of(u, theirs[n]), t_send.at[u], t_recv.at[u], twin))

    def stage_4(u):
        n, c0, size = REDUCE_UNITS[u]
        copies["t", u].wait_recv()
        number, at = blocks(u)
        target = outs[n] if ended[n] is None else ended[n]

        def body(i):
            if ended[n] is None:
                target[at(i)] = mine[n][at(i)].astype(F32) + theirs[n][at(i)].astype(F32)
            else:
                target[at(i)] = mine[n][at(i)] + theirs[n][at(i)]

        loop(number, body)
        if ended[n] is not None:
            part = (slice(None), pl.ds(c0, size))
            for r in ORDER:
                src, dst = target.at[lax.rem(z + r, 4), *part], outs[n].at[z, *part]
                begin(("z", u, r), remote(src, dst, z_send.at[u, r - 1], z_recv.at[u, r - 1], zs[r]))
            copy = pltpu.make_async_copy(target.at[z, *part], outs[n].at[z, *part], keep.at[u])
            copy.start()
            copies["keep", u] = copy

    ready = set()
    count = len(REDUCE_UNITS)
    stages = (stage_0, stage_1, stage_2, stage_3, stage_4)
    for step in range(count + 8):
        for s, stage in enumerate(stages):
            if 0 <= step - 2 * s < count:
                stage(step - 2 * s)
    for u in range(count):
        if ("keep", u) in copies:
            copies["keep", u].wait()
            for r in ORDER:
                copies["z", u, r].wait_recv()
    o_s[...] = b_s[0] + b_s[1] + b_s[2] + b_s[3]
    for copy in sent:
        copy.wait_send()


def reduce(g_d, g_g, g_u, g_o, g_in, g_s):
    shape = jax.ShapeDtypeStruct
    dma = pltpu.SemaphoreType.DMA
    vm = pltpu.VMEM
    count = len(REDUCE_UNITS)
    big = ((4, 48, 1792), (4, 48, 1792), (4, 48, 1152))
    return pl.pallas_call(
        reduce_kernel,
        out_shape=(
            shape((224, 1536), F32),
            shape((4, 48, 1792), BF16),
            shape((4, 48, 1792), BF16),
            shape((48, 1536), F32),
            shape((4, 48, 1152), BF16),
            shape((8, 128), F32),
        ),
        in_specs=[ANY] * 6,
        out_specs=[VMEM, ANY, ANY, VMEM, ANY, VMEM],
        scratch_shapes=[
            vm((8, 224, 1536), BF16), vm((8, 4, 48, 1792), BF16), vm((8, 4, 48, 1792), BF16),
            vm((8, 48, 1536), BF16), vm((8, 4, 48, 1152), BF16), vm((8, 4, 8, 128), F32),
            vm((4, 2, 48, 1792), BF16), vm((4, 2, 48, 1792), BF16), vm((4, 48, 768), BF16),
            vm((4, 2, 48, 1152), BF16), vm((4, 2, 8, 128), F32),
            vm((4, 224, 1536), BF16), vm((4, 2, 48, 1792), BF16), vm((4, 2, 48, 1792), BF16),
            vm((4, 48, 768), BF16), vm((4, 2, 48, 1152), BF16), vm((4, 2, 8, 128), F32),
            vm((3, 224, 1536), BF16), vm((3, 4, 48, 1792), BF16), vm((3, 4, 48, 1792), BF16),
            vm((3, 48, 1536), BF16), vm((3, 4, 48, 1152), BF16), vm((3, 4, 8, 128), F32),
            vm((224, 1536), BF16), vm(big[0], BF16), vm(big[1], BF16), vm((48, 1536), BF16), vm(big[2], BF16),
            vm((4, 8, 128), F32),
            vm((224, 1536), BF16), vm(big[0], BF16), vm(big[1], BF16), vm((48, 1536), BF16), vm(big[2], BF16),
            vm((4, 8, 128), F32),
            vm(big[0], BF16), vm(big[1], BF16), vm(big[2], BF16), vm((4, 8, 128), F32), vm((4, 8, 128), F32),
            dma((6,)), dma((count,)), dma((count,)), dma((count,)), dma((count,)), dma((count, 3)), dma((count, 3)),
            dma((count,)), dma((count,)), dma((count, 3)), dma((count, 3)), dma((count,)),
        ],
        compiler_params=pltpu.CompilerParams(
            collective_id=2, has_side_effects=True, vmem_limit_bytes=63 * 2**20
        ),
        name="reduce_grads",
    )(g_d, g_g, g_u, g_o, g_in, g_s)


def cut_ffn(weight):
    tiles = jnp.pad(weight.reshape(48, 8, 4, 216), ((0, 0), (0, 0), (0, 0), (0, 8)))
    return tiles.transpose(2, 0, 1, 3).reshape(4, 48, 1792)


def uncut_ffn(value):
    tiles = value.reshape(4, 48, 8, 224)[..., :216]
    return tiles.transpose(1, 2, 0, 3).reshape(1, 48, 6912).astype(F32)


def local(inputs, cotangent, w_in, w_out, w_gate, w_up, w_down, kernel, gain_mix, gain_ffn):
    a_in = w_in.reshape(48, 3, 8, 4, 48).transpose(3, 0, 1, 2, 4).reshape(4, 48, 1152)
    small = jnp.concatenate([kernel[0], gain_mix, gain_ffn], axis=0)
    small = jnp.pad(small, ((0, 11), (0, 80)))
    s_all, win, wout, wg, wu, wd = gather(
        small, a_in, cut_ffn(w_gate[0]), cut_ffn(w_up[0]), w_out[0], jnp.pad(w_down[0], ((0, 8), (0, 0)))
    )
    z = lax.axis_index("z")
    gains = s_all[:, :, 3:5, :48].astype(F32).transpose(2, 0, 1, 3).reshape(2, 1536)
    own_taps = lax.dynamic_index_in_dim(s_all, z, axis=1, keepdims=False)[:, 0:3, :48]
    taps = own_taps.astype(F32).transpose(1, 0, 2).reshape(3, 384)
    y, gx, g_in, g_o, g_g, g_u, g_d, g_tap, g_mix, g_ffn = main(
        inputs.reshape(128, 1536),
        cotangent.reshape(128, 1536),
        gains,
        taps,
        win.reshape(1536, 1152),
        wout.reshape(384, 1536),
        wg.reshape(1536, 1792),
        wu.reshape(1536, 1792),
        wd.reshape(1792, 1536),
    )
    tap_rows = g_tap.reshape(3, 8, 48).transpose(1, 0, 2)
    at_z = (lax.broadcasted_iota(jnp.int32, (1, 4, 1, 1), 1) == z).astype(F32)
    tap_rows = tap_rows[:, None] * at_z
    gain_rows = jnp.stack([g_mix.reshape(8, 4, 48), g_ffn.reshape(8, 4, 48)], axis=2)
    g_s = jnp.pad(jnp.concatenate([tap_rows, gain_rows], axis=2), ((0, 0), (0, 0), (0, 3), (0, 80)))
    o_d, o_g, o_u, o_o, o_in, o_s = reduce(
        g_d.reshape(8, 224, 1536),
        g_g.reshape(8, 4, 48, 1792),
        g_u.reshape(8, 4, 48, 1792),
        g_o.reshape(8, 48, 1536),
        g_in.reshape(8, 4, 48, 1152),
        g_s,
    )
    grad_in = o_in.reshape(4, 48, 3, 8, 48).transpose(1, 2, 3, 0, 4).reshape(1, 48, 4608).astype(F32)
    return (
        y.reshape(1, 2, 64, 1536),
        gx.reshape(1, 2, 64, 1536),
        grad_in,
        o_o[None],
        uncut_ffn(o_g),
        uncut_ffn(o_u),
        o_d[None, :216],
        o_s[None, 0:3, :48],
        o_s[3:4, :48],
        o_s[4:5, :48],
    )


def solution(mesh):
    names = ("section", "xl", "xh", "y", "z")
    fine = Mesh(mesh.devices.reshape(2, 2, 2, 4, 4), names)
    tokens, shard = ("xl", "xh", "y", "z"), ("xh", "y", "z")
    weight = P("section", shard, None)
    acts = P("section", None, tokens, None)
    return jax.shard_map(
        local,
        mesh=fine,
        in_specs=(
            P(None, tokens, None),
            P(None, tokens, None),
            weight,
            weight,
            weight,
            weight,
            weight,
            P("section", None, shard),
            P("section", shard),
            P("section", shard),
        ),
        out_specs=(
            acts,
            acts,
            weight,
            weight,
            weight,
            weight,
            weight,
            P("section", None, shard),
            P("section", shard),
            P("section", shard),
        ),
        check_vma=False,
    )
```

```python
import functools

import jax
import jax.numpy as jnp
from jax import lax
from jax.experimental import pallas as pl
from jax.experimental.pallas import tpu as pltpu
from jax.sharding import Mesh
from jax.sharding import PartitionSpec as P

F32, BF16 = jnp.float32, jnp.bfloat16
MESH = pl.DeviceIdType.MESH
EPS = 1e-06
ANY = pl.BlockSpec(memory_space=pl.ANY)
VMEM = pl.BlockSpec(memory_space=pltpu.VMEM)
ORDER = (1, 3, 2)

GATHER_UNITS = (
    (0, 0, 128), (1, 0, 1152), (2, 0, 1536),
    (3, 0, 640), (4, 0, 640), (3, 640, 640), (4, 640, 640), (3, 1280, 512), (4, 1280, 512),
    (5, 0, 80), (5, 80, 80), (5, 160, 64),
)
REDUCE_UNITS = (
    (0, 0, 80), (0, 80, 80), (0, 160, 64),
    (1, 0, 640), (1, 640, 640), (1, 1280, 512), (2, 0, 640), (2, 640, 640), (2, 1280, 512),
    (3, 0, 1536), (4, 0, 640), (4, 640, 512), (5, 0, 128),
)


def place():
    return tuple(lax.axis_index(name) for name in ("section", "xl", "xh", "y", "z"))


def barrier_all(devices):
    barrier = pltpu.get_barrier_semaphore()
    for device in devices:
        pl.semaphore_signal(barrier, inc=1, device_id=device, device_id_type=MESH)
    pl.semaphore_wait(barrier, len(devices))


def remote(src, dst, send, recv, device):
    return pltpu.make_async_remote_copy(
        src_ref=src, dst_ref=dst, send_sem=send, recv_sem=recv, device_id=device, device_id_type=MESH
    )


def plane_peers():
    section, xl, xh, y, z = place()
    partner = {"xh": 1 - xh, "xl": 1 - xl}
    twin = {"xl": 1 - xl}
    zs = {r: {"z": lax.rem(z + r, 4)} for r in ORDER}
    ys = {r: {"y": lax.rem(y + r, 4)} for r in ORDER}
    return partner, twin, zs, ys


def dot_nn(a, b):
    return lax.dot_general(a, b, (((1,), (0,)), ((), ())), preferred_element_type=F32)


def dot_nt(a, b):
    return lax.dot_general(a, b, (((1,), (1,)), ((), ())), preferred_element_type=F32)


def dot_tn(a, b):
    return lax.dot_general(a, b, (((0,), (0,)), ((), ())), preferred_element_type=F32)


def cols(j, width):
    return pl.ds(pl.multiple_of(j * width, width), width)


def loop(count, body):
    def step(j, carry):
        body(j)
        return carry

    lax.fori_loop(0, count, step, 0)


def blocks_kernel(
    x_ref, cot_ref, small, w_in, w_out, w_gate, w_up, w_down,
    y_ref, gx_ref, gin_h, gout_h, gg_h, gu_h, gd_h, gs_ref,
    xa, xn, n2, ea, fa, part, rr, proj, ge, dce, cv, ha, hb, mx, gt, up, hd, dg, du,
    mid, dmid, dp, g0, win, wout, wg, wu, wd, sm, gains, taps, gtap, ggain,
    store, a_send, a_recv, s_send, s_recv, h_send, h_recv, c_send, c_recv,
    z_send, z_recv, y_send, y_recv, p_send, p_recv, q_send, q_recv, go,
):
    section, xl, xh, y, z = place()
    partner, twin, zs, ys = plane_peers()
    core = {"section": 1 - section}
    group = xl * 8 + xh * 4 + y
    after, before = lax.rem(group + 1, 16), lax.rem(group + 15, 16)
    has_after, has_before = group < 15, group > 0

    def at_group(g):
        return {"xl": g // 8, "xh": lax.rem(g // 4, 2), "y": lax.rem(g, 4)}

    barrier = pltpu.get_barrier_semaphore()

    def hail(device):
        pl.semaphore_signal(barrier, inc=1, device_id=device, device_id_type=MESH)

    for device in (partner, twin, core, *zs.values(), *ys.values()):
        hail(device)

    @pl.when(has_after)
    def _():
        hail(at_group(after))

    @pl.when(has_before)
    def _():
        hail(at_group(before))

    me = xh * 4 + y
    weights = (sm, win, wout, wg, wu, wd)
    cut = (None, dp, None, hd, dg, None)
    rows = (32, 192, 48, 192, 192, 224)
    cut_conv(w_in, dp)
    wout[pl.ds(pl.multiple_of(me * 48, 16), 48), :] = w_out[...]
    pl.semaphore_wait(barrier, 10 - (group + 1) // 16 + (group + 15) // 16)

    def of_z(n, ref, first, zz):
        size = rows[n] // 4
        return ref.at[pl.ds(pl.multiple_of(first + zz * size, 8 if n == 0 else 16), size)]

    def rows_q(n, q):
        return pl.multiple_of(q * rows[n], 8 if n == 0 else 16)

    sent, z_copies = [], {}

    def push_z(n):
        size = rows[n] // 4
        for r in ORDER:
            src = small if n == 0 else of_z(n, cut[n], 0, lax.rem(z + r, 4))
            dst = of_z(n, weights[n], me * rows[n], z)
            copy = remote(src, dst, z_send.at[n, r - 1], z_recv.at[n, r - 1], zs[r])
            copy.start()
            z_copies[n, r] = copy
            sent.append(copy)
        mine = pl.ds(pl.multiple_of(me * rows[n] + z * size, 8 if n == 0 else 16), size)
        if n == 0:
            sm[mine, :] = small[...]
        else:
            weights[n][mine, :] = cut[n][pl.ds(pl.multiple_of(z * size, 16), size), 0 : weights[n].shape[1]]

    @pl.when(section == 1)
    def _():
        pl.semaphore_wait(go, 1)

    def own_rows(mb):
        return pl.ds(pl.multiple_of(mb * 256 + z * 64, 64), 64)

    def spread(n, buf, mb):
        at = buf.at[own_rows(mb)]
        return [remote(at, at, a_send.at[n, mb, r - 1], a_recv.at[n, mb, r - 1], zs[r]) for r in ORDER]

    x_all, n_all, e_all, f_all = ([spread(n, buf, mb) for mb in range(2)] for n, buf in enumerate((xa, n2, ea, fa)))

    def begin(copies):
        for copy in copies:
            copy.start()

    def arrived(copies):
        for copy in copies:
            copy.wait_recv()

    mb_rows = [slice(0, 256), slice(256, 512)]
    core_x, core_g = [], []
    for mb in range(2):
        at = pl.ds(mb * 64, 64)
        core_x.append(remote(y_ref.at[at], xa.at[own_rows(mb)], c_send.at[0, mb], c_recv.at[0, mb], core))
        core_g.append(remote(g0.at[at], ea.at[own_rows(mb)], c_send.at[1, mb], c_recv.at[1, mb], core))

    push_z(0)
    push_z(1)

    @pl.when(section == 0)
    def _():
        for mb in range(2):
            xa[own_rows(mb), :] = x_ref[mb * 64 : mb * 64 + 64, :]
            begin(x_all[mb])

    @pl.when(section == 1)
    def _():
        for mb in range(2):
            ea[own_rows(mb), :] = cot_ref[mb * 64 : mb * 64 + 64, :]
            begin(e_all[mb])

    cut_ffn(w_gate, hd)
    push_z(3)
    cut_ffn(w_up, dg)
    push_z(4)
    first_d = pl.multiple_of(me * 224, 16)
    wd[pl.ds(first_d, 224), :] = jnp.concatenate([w_down[...], jnp.zeros((8, 1536), BF16)], axis=0)

    def piece(u, q):
        n, first, size = GATHER_UNITS[u]
        if n == 5:
            return wd.at[pl.ds(pl.multiple_of(q * 224 + first, 16), size)]
        if n == 2:
            return wout.at[pl.ds(rows_q(2, q), 48)]
        return weights[n].at[pl.ds(rows_q(n, q), rows[n]), pl.ds(first, size)]

    def half(u, q, h):
        n, first, size = GATHER_UNITS[u]
        if n in (2, 5):
            left = pl.ds(pl.multiple_of(h * 768, 128), 768)
            if n == 5:
                return wd.at[pl.ds(pl.multiple_of(q * 224 + first, 16), size), left]
            return wout.at[pl.ds(rows_q(2, q), 48), left]
        part_rows = rows[n] // 2
        return weights[n].at[
            pl.ds(pl.multiple_of(q * rows[n] + h * part_rows, 8 if n == 0 else 16), part_rows), pl.ds(first, size)
        ]

    y_copies, p_copies, q_copies, started = {}, {}, {}, set()

    def stage_y(u):
        n = GATHER_UNITS[u][0]
        if n not in started:
            started.add(n)
            if n not in (2, 5):
                for r in ORDER:
                    z_copies[n, r].wait_recv()
        for r in ORDER:
            src = piece(u, me)
            copy = remote(src, src, y_send.at[u, r - 1], y_recv.at[u, r - 1], ys[r])
            copy.start()
            y_copies[u, r] = copy
            sent.append(copy)
        push_p(u, 0)

    def push_p(u, r):
        src = half(u, xh * 4 + lax.rem(y + 4 - r, 4), xl)
        copy = remote(src, src, p_send.at[u, r], p_recv.at[u, r], partner)
        copy.start()
        p_copies[u, r] = copy
        sent.append(copy)

    def stage_p(u):
        for r in ORDER:
            y_copies[u, r].wait_recv()
            push_p(u, r)

    def stage_q(u):
        for r in (0, *ORDER):
            p_copies[u, r].wait_recv()
            src = half(u, (1 - xh) * 4 + lax.rem(y + 4 - r, 4), 1 - xl)
            copy = remote(src, src, q_send.at[u, r], q_recv.at[u, r], twin)
            copy.start()
            q_copies[u, r] = copy
            sent.append(copy)

    def need(n):
        for u, unit in enumerate(GATHER_UNITS):
            if unit[0] == n:
                for r in (0, *ORDER):
                    q_copies[u, r].wait_recv()

    def scatter(n, mb, j, r):
        at = cols(j, 512)
        src = part.at[pl.ds(pl.multiple_of(mb * 256 + lax.rem(z + r, 4) * 64, 64), 64), at]
        dst = rr.at[n, r - 1, pl.ds(mb * 64, 64), at]
        return remote(src, dst, s_send.at[n, mb, j, r - 1], s_recv.at[n, mb, j, r - 1], zs[r])

    def sum_over_z(n, mb, block):
        def body(j):
            part[mb_rows[mb], cols(j, 512)] = block(cols(j, 512)).astype(BF16)
            for r in ORDER:
                scatter(n, mb, j, r).start()

        loop(3, body)

    def sum_arrived(n, mb):
        def body(j):
            for r in ORDER:
                scatter(n, mb, j, r).wait_recv()

        loop(3, body)

    def sum_sent(n, mb):
        def body(j):
            for r in ORDER:
                scatter(n, mb, j, r).wait_send()

        loop(3, body)

    def summed(n, at, mine):
        total = part[mine, :].astype(F32)
        for r in range(3):
            total = total + rr[n, r, at, :].astype(F32)
        return total

    def own_blocks(mb, body):
        def step(i):
            at = pl.ds(pl.multiple_of(mb * 64 + i * 32, 32), 32)
            mine = pl.ds(pl.multiple_of(mb * 256 + z * 64 + i * 32, 32), 32)
            body(at, mine)

        loop(2, step)

    def rms(values):
        return lax.rsqrt(jnp.mean(values * values, axis=-1, keepdims=True) + EPS)

    def take_input():
        for f in range(32):
            gains[0:2, 48 * f : 48 * f + 48] = sm[8 * f + 3 : 8 * f + 5, 0:48]
        for q in range(8):
            taps[0:3, 48 * q : 48 * q + 48] = sm[pl.ds(pl.multiple_of(q * 32 + z * 8, 8), 8), :][0:3, 0:48]

    halo_after = [
        remote(ge.at[mb, pl.ds(256, 8)], ha.at[mb], h_send.at[0, mb], h_recv.at[0, mb], at_group(after)) for mb in range(2)
    ]
    halo_before = [
        remote(dce.at[mb, pl.ds(0, 8)], hb.at[mb], h_send.at[1, mb], h_recv.at[1, mb], at_group(before)) for mb in range(2)
    ]

    def project(mb):
        arrived(x_all[mb])

        def norm(i):
            at = pl.ds(pl.multiple_of(mb * 256 + i * 32, 32), 32)
            values = xa[at, :].astype(F32)
            xn[at, :] = (values * rms(values) * gains[0:1, :]).astype(BF16)

        loop(8, norm)

        def body(j):
            proj[j, mb_rows[mb], :] = dot_nn(xn[mb_rows[mb], :], win[:, cols(j, 384)])

        loop(3, body)
        ge[mb, 8:264, :] = proj[0, mb_rows[mb], :] * proj[2, mb_rows[mb], :]

        @pl.when(has_after)
        def _():
            halo_after[mb].start()

    def tap(k):
        return taps[k : k + 1, :]

    def mix(mb):
        @pl.when(has_before)
        def _():
            halo_after[mb].wait_recv()
            ge[mb, 0:8, :] = ha[mb]

        @pl.when(jnp.logical_not(has_before))
        def _():
            ge[mb, 0:8, :] = jnp.zeros((8, 384), F32)

        for zc in range(4):
            t0, at = 8 + 64 * zc, slice(mb * 256 + 64 * zc, mb * 256 + 64 * zc + 64)
            total = tap(0) * ge[mb, t0 : t0 + 64, :]
            for k in (1, 2):
                total = total + tap(k) * ge[mb, t0 - k : t0 - k + 64, :]
            cv[at, :] = total
            mx[at, :] = (proj[1, at, :] * total).astype(BF16)
        sum_over_z(0, mb, lambda at: dot_nn(mx[mb_rows[mb], :], wout[:, at]))

    def middle(mb):
        sum_arrived(0, mb)

        def body(at, mine):
            values = xa[mine, :].astype(F32) + summed(0, at, mine)
            mid[at, :] = values
            n2[mine, :] = (values * rms(values) * gains[1:2, :]).astype(BF16)

        own_blocks(mb, body)
        begin(n_all[mb])

    def gate(mb):
        arrived(n_all[mb])

        def body(j):
            at = cols(j, 256)
            gating = dot_nn(n2[mb_rows[mb], :], wg[:, at])
            up_part = dot_nn(n2[mb_rows[mb], :], wu[:, at])
            gt[mb_rows[mb], at] = gating
            up[mb_rows[mb], at] = up_part
            hd[mb_rows[mb], at] = (gating * jax.nn.sigmoid(gating) * up_part).astype(BF16)

        loop(7, body)

    def down(mb):
        sum_sent(0, mb)
        sum_over_z(1, mb, lambda at: dot_nn(hd[mb_rows[mb], :], wd[:, at]))

    def finish(mb):
        sum_arrived(1, mb)

        def body(at, mine):
            y_ref[at, :] = (mid[at, :] + summed(1, at, mine)).astype(BF16)

        own_blocks(mb, body)

        @pl.when(section == 0)
        def _():
            core_x[mb].start()

    def wait_x():
        @pl.when(section == 1)
        def _():
            for mb in range(2):
                core_x[mb].wait_recv()
                begin(x_all[mb])

    def free_cuts():
        for n in (1, 3, 4):
            for r in ORDER:
                z_copies[n, r].wait_send()

    def both(stage):
        stage(0)
        stage(1)

    def forward_1():
        need(0)
        take_input()
        need(1)
        wait_x()
        both(project)

    def forward_2():
        need(2)
        both(mix)

    def forward_3():
        both(middle)

    def forward_4():
        need(3)
        need(4)
        free_cuts()
        both(gate)

    def forward_5():
        need(5)
        both(down)

    segments = {5: forward_1, 7: forward_2, 9: forward_3, 13: forward_4}
    count = len(GATHER_UNITS)
    for step in range(count + 4):
        if step < count:
            stage_y(step)
        if 0 <= step - 2 < count:
            stage_p(step - 2)
        if step - 2 == count - 1:

            @pl.when(section == 0)
            def _():
                pl.semaphore_signal(go, inc=1, device_id=core, device_id_type=MESH)

        if 0 <= step - 4 < count:
            stage_q(step - 4)
        if step in segments:
            pl.when(section == 0)(segments[step])

    @pl.when(section == 1)
    def _():
        for segment in segments.values():
            segment()

    forward_5()
    both(finish)
    for copy in sent:
        if not any(copy is z_copies[n, r] for n in (1, 3, 4) for r in ORDER):
            copy.wait_send()

    ggain[...] = jnp.zeros((2, 1536), F32)

    def take_gradient(mb):
        @pl.when(section == 0)
        def _():
            core_g[mb].wait_recv()
            begin(e_all[mb])

    def back_hidden(mb):
        arrived(e_all[mb])

        def body(j):
            at = cols(j, 256)
            dh = dot_nt(ea[mb_rows[mb], :], wd[at, :])
            gating, up_part = gt[mb_rows[mb], at], up[mb_rows[mb], at]
            sg = jax.nn.sigmoid(gating)
            dg[mb_rows[mb], at] = (dh * up_part * sg * (1.0 + gating * (1.0 - sg))).astype(BF16)
            du[mb_rows[mb], at] = (dh * gating * sg).astype(BF16)

        loop(7, body)

    def back_ffn(mb):
        sum_sent(1, mb)
        sum_over_z(2, mb, lambda at: dot_nt(dg[mb_rows[mb], :], wg[at, :]) + dot_nt(du[mb_rows[mb], :], wu[at, :]))

    def back_middle(mb):
        sum_arrived(2, mb)

        def body(at, mine):
            dn2 = summed(2, at, mine)
            values = mid[at, :]
            scale = rms(values)
            weighted = dn2 * gains[1:2, :]
            mean_term = jnp.mean(weighted * values, axis=-1, keepdims=True)
            grad = ea[mine, :].astype(F32) + scale * weighted - values * (scale * scale * scale) * mean_term
            ggain[1:2, :] += jnp.sum(dn2 * values * scale, axis=0, keepdims=True)
            dmid[at, :] = grad
            fa[mine, :] = grad.astype(BF16)

        own_blocks(mb, body)
        begin(f_all[mb])

    def back_mix(mb):
        arrived(f_all[mb])
        dce[mb, 0:256, :] = dot_nt(fa[mb_rows[mb], :], wout[...])
        for zc in range(4):
            at, here = slice(mb * 256 + 64 * zc, mb * 256 + 64 * zc + 64), slice(64 * zc, 64 * zc + 64)
            dm = dce[mb, here, :]
            dp[at, 384:768] = (dm * cv[at, :]).astype(BF16)
            dce[mb, here, :] = dm * proj[1, at, :]

        @pl.when(has_before)
        def _():
            halo_before[mb].start()

    def back_conv(mb):
        @pl.when(has_after)
        def _():
            halo_before[mb].wait_recv()
            dce[mb, 256:264, :] = hb[mb]

        @pl.when(jnp.logical_not(has_after))
        def _():
            dce[mb, 256:264, :] = jnp.zeros((8, 384), F32)

        for zc in range(4):
            at, t0 = slice(mb * 256 + 64 * zc, mb * 256 + 64 * zc + 64), 64 * zc
            total = tap(0) * dce[mb, t0 : t0 + 64, :]
            for k in (1, 2):
                total = total + tap(k) * dce[mb, t0 + k : t0 + k + 64, :]
            dp[at, 0:384] = (total * proj[2, at, :]).astype(BF16)
            dp[at, 768:1152] = (total * proj[0, at, :]).astype(BF16)

    def back_in(mb):
        sum_sent(2, mb)
        sum_over_z(3, mb, lambda at: dot_nt(dp[mb_rows[mb], :], win[at, :]))

    def back_input(mb):
        sum_arrived(3, mb)

        def body(at, mine):
            dn = summed(3, at, mine)
            values = xa[mine, :].astype(F32)
            scale = rms(values)
            weighted = dn * gains[0:1, :]
            mean_term = jnp.mean(weighted * values, axis=-1, keepdims=True)
            grad = dmid[at, :] + scale * weighted - values * (scale * scale * scale) * mean_term
            ggain[0:1, :] += jnp.sum(dn * values * scale, axis=0, keepdims=True)
            gx_ref[at, :] = grad
            g0[at, :] = grad.astype(BF16)

        own_blocks(mb, body)

        @pl.when(section == 1)
        def _():
            core_g[mb].start()

    stores = [
        pltpu.make_async_copy(src, dst, store.at[n])
        for n, (src, dst) in enumerate(((win, gin_h), (wout, gout_h), (wg, gg_h), (wu, gu_h), (wd, gd_h)))
    ]

    def grad(n, width, left, right):
        target = (win, wout, wg, wu, wd)[n]

        def body(j):
            at = cols(j, width)
            target[at, :] = dot_tn(left[:, at], right[...]).astype(BF16)

        loop(target.shape[0] // width, body)
        stores[n].start()

    both(take_gradient)
    both(lambda mb: (back_hidden(mb), back_ffn(mb)))
    grad(4, 256, hd, ea)
    back_middle(0)
    grad(2, 256, n2, dg)
    back_middle(1)
    grad(3, 256, n2, du)
    both(back_mix)
    grad(1, 128, mx, fa)
    for k in range(3):
        total = jnp.zeros((1, 384), F32)
        for mb in range(2):
            for zc in range(4):
                t0 = 8 + 64 * zc - k
                products = dce[mb, 64 * zc : 64 * zc + 64, :] * ge[mb, t0 : t0 + 64, :]
                total = total + jnp.sum(products, axis=0, keepdims=True)
        gtap[k : k + 1, :] = total
    both(lambda mb: (back_conv(mb), back_in(mb)))
    grad(0, 256, xn, dp)
    both(back_input)

    gs_ref[...] = jnp.zeros((256, 128), F32)
    for q in range(8):
        at = pl.ds(pl.multiple_of(q * 32 + z * 8, 8), 8)
        gs_ref[at, 0:48] = gtap[:, 48 * q : 48 * q + 48]
    for f in range(32):
        gs_ref[8 * f + 3 : 8 * f + 5, 0:48] = ggain[0:2, 48 * f : 48 * f + 48]

    for mb in range(2):

        @pl.when(section == 1)
        def _():
            core_g[mb].wait_send()

        @pl.when(section == 0)
        def _():
            core_x[mb].wait_send()

        @pl.when(has_after)
        def _():
            halo_after[mb].wait_send()

        @pl.when(has_before)
        def _():
            halo_before[mb].wait_send()

        sum_sent(3, mb)
        for copies in (x_all, n_all, e_all, f_all):
            for copy in copies[mb]:
                copy.wait_send()
    for copy in stores:
        copy.wait()


def cut_conv(weight, out):
    for q in range(8):
        for zz in range(4):
            for part in range(3):
                first, to = part * 1536 + (4 * q + zz) * 48, part * 384 + q * 48
                out[zz * 48 : zz * 48 + 48, to : to + 48] = weight[:, first : first + 48]


def cut_ffn(weight, out):
    for zz in range(4):
        for q in range(8):
            first = (4 * q + zz) * 216
            out[zz * 48 : zz * 48 + 48, 224 * q : 224 * q + 216] = weight[:, first : first + 216]
            out[zz * 48 : zz * 48 + 48, 224 * q + 216 : 224 * q + 224] = jnp.zeros((48, 8), BF16)


def run_blocks(x, cot, small, w_in, w_out, w_gate, w_up, w_down):
    shape = jax.ShapeDtypeStruct
    dma = pltpu.SemaphoreType.DMA
    vm = pltpu.VMEM
    count = len(GATHER_UNITS)
    return pl.pallas_call(
        blocks_kernel,
        out_shape=(
            shape((128, 1536), BF16),
            shape((128, 1536), F32),
            shape((1536, 1152), BF16),
            shape((384, 1536), BF16),
            shape((1536, 1792), BF16),
            shape((1536, 1792), BF16),
            shape((1792, 1536), BF16),
            shape((256, 128), F32),
        ),
        in_specs=[VMEM] * 8,
        out_specs=[VMEM] * 2 + [ANY] * 5 + [VMEM],
        scratch_shapes=[
            vm((512, 1536), BF16), vm((512, 1536), BF16), vm((512, 1536), BF16), vm((512, 1536), BF16),
            vm((512, 1536), BF16), vm((512, 1536), BF16), vm((4, 3, 128, 1536), BF16),
            vm((3, 512, 384), F32), vm((2, 264, 384), F32), vm((2, 264, 384), F32), vm((512, 384), F32),
            vm((2, 8, 384), F32), vm((2, 8, 384), F32), vm((512, 384), BF16),
            vm((512, 1792), F32), vm((512, 1792), F32), vm((512, 1792), BF16), vm((512, 1792), BF16),
            vm((512, 1792), BF16), vm((128, 1536), F32), vm((128, 1536), F32), vm((512, 1152), BF16),
            vm((128, 1536), BF16),
            vm((1536, 1152), BF16), vm((384, 1536), BF16), vm((1536, 1792), BF16), vm((1536, 1792), BF16),
            vm((1792, 1536), BF16), vm((256, 128), F32), vm((8, 1536), F32), vm((8, 384), F32), vm((8, 384), F32),
            vm((2, 1536), F32),
            dma((5,)), dma((4, 2, 3)), dma((4, 2, 3)), dma((4, 2, 3, 3)), dma((4, 2, 3, 3)),
            dma((2, 2)), dma((2, 2)), dma((2, 2)), dma((2, 2)),
            dma((5, 3)), dma((5, 3)), dma((count, 3)), dma((count, 3)), dma((count, 4)), dma((count, 4)),
            dma((count, 4)), dma((count, 4)), pltpu.SemaphoreType.REGULAR,
        ],
        compiler_params=pltpu.CompilerParams(
            collective_id=1, has_side_effects=True, vmem_limit_bytes=63 * 2**20
        ),
        name="two_blocks",
    )(x, cot, small, w_in, w_out, w_gate, w_up, w_down)


def reduce_kernel(
    g_d, g_g, g_u, g_o, g_in, g_s,
    o_d, o_g, o_u, o_o, o_in, o_s,
    v_d, v_g, v_u, v_o, v_in, v_s,
    q1_g, q1_u, q1_o, q1_in, q1_s,
    p_d, p_g, p_u, p_o, p_in, p_s,
    y_d, y_g, y_u, y_o, y_in, y_s,
    f_d, f_g, f_u, f_o, f_in, f_s,
    t_d, t_g, t_u, t_o, t_in, t_s,
    e_g, e_u, e_in, e_s, l_d, l_g, l_u, l_in, b_s,
    load, q_send, q_recv, p_send, p_recv, y_send, y_recv, t_send, t_recv, z_send, z_recv, keep,
):
    section, xl, xh, y, z = place()
    partner, twin, zs, ys = plane_peers()
    grads = (g_d, g_g, g_u, g_o, g_in, g_s)
    held = (v_d, v_g, v_u, v_o, v_in, v_s)
    from_twin = (None, q1_g, q1_u, q1_o, q1_in, q1_s)
    from_partner = (p_d, p_g, p_u, p_o, p_in, p_s)
    from_y = (y_d, y_g, y_u, y_o, y_in, y_s)
    mine = (f_d, f_g, f_u, f_o, f_in, f_s)
    theirs = (t_d, t_g, t_u, t_o, t_in, t_s)
    ended = (None, e_g, e_u, None, e_in, e_s)
    outs = (l_d, l_g, l_u, o_o, l_in, b_s)
    loads = [pltpu.make_async_copy(grads[n], held[n], load.at[n]) for n in range(6)]
    for copy in loads:
        copy.start()
    barrier_all([partner, twin, *zs.values(), *ys.values()])
    near, far = xh * 4, (1 - xh) * 4
    me = near + y
    sent = []
    copies = {}

    def begin(key, copy):
        copy.start()
        copies[key] = copy
        sent.append(copy)

    def half(u, ref, first, h):
        n, c0, size = REDUCE_UNITS[u]
        if n == 3:
            return ref.at[pl.ds(first, 4), :, pl.ds(pl.multiple_of(h * 768, 128), 768)]
        return ref.at[pl.ds(first, 4), pl.ds(h * 2, 2), :, pl.ds(c0, size)]

    def arrived(u, ref):
        n, c0, size = REDUCE_UNITS[u]
        return ref if n == 3 else ref.at[:, :, :, pl.ds(c0, size)]

    def row_of(u, ref, *lead):
        n, c0, size = REDUCE_UNITS[u]
        if n == 0:
            return ref.at[*lead, pl.ds(c0, size)]
        if n == 3:
            return ref.at[*lead] if lead else ref
        return ref.at[*lead, :, :, pl.ds(c0, size)]

    def add(u, first, h, other):
        n, c0, size = REDUCE_UNITS[u]
        if n == 0:
            rows = size // 16

            def body(i):
                row, at = i // rows, pl.ds(pl.multiple_of(c0 + lax.rem(i, rows) * 16, 16), 16)
                v_d[first + row, at, :] = v_d[first + row, at, :] + other[row, at, :]

            loop(4 * rows, body)
        elif n == 3:
            at = pl.ds(pl.multiple_of(h * 768, 128), 768)

            def body(i):
                v_o[first + i, :, at] = v_o[first + i, :, at] + other[i]

            loop(4, body)
        else:
            ref, at = held[n], slice(c0, c0 + size)

            def body(i):
                a, b = first + i // 2, h * 2 + lax.rem(i, 2)
                ref[a, b, :, at] = ref[a, b, :, at] + other[i // 2, lax.rem(i, 2), :, at]

            loop(8, body)

    def stage_0(u):
        n = REDUCE_UNITS[u][0]
        if n not in ready:
            ready.add(n)
            loads[n].wait()
        if n:
            dst = arrived(u, from_twin[n])
            begin(("q", u), remote(half(u, held[n], far, 1 - xl), dst, q_send.at[u], q_recv.at[u], twin))
        else:
            begin_p(u, held[n].at[pl.ds(far, 4), pl.ds(*REDUCE_UNITS[u][1:])])

    def begin_p(u, src):
        n, c0, size = REDUCE_UNITS[u]
        dst = from_partner[n].at[:, pl.ds(c0, size)] if n == 0 else arrived(u, from_partner[n])
        begin(("p", u), remote(src, dst, p_send.at[u], p_recv.at[u], partner))

    def stage_1(u):
        n = REDUCE_UNITS[u][0]
        if n:
            copies["q", u].wait_recv()
            add(u, far, xl, from_twin[n])
            begin_p(u, half(u, held[n], far, xl))

    def stage_2(u):
        n = REDUCE_UNITS[u][0]
        copies["p", u].wait_recv()
        add(u, near, 1 - xl, from_partner[n])
        for r in ORDER:
            src, dst = row_of(u, held[n], near + lax.rem(y + r, 4)), row_of(u, from_y[n], r - 1)
            begin(("y", u, r), remote(src, dst, y_send.at[u, r - 1], y_recv.at[u, r - 1], ys[r]))

    def blocks(u):
        n, c0, size = REDUCE_UNITS[u]
        if n == 0:
            return size // 16, lambda i: (pl.ds(pl.multiple_of(c0 + i * 16, 16), 16), slice(None))
        if n == 3:
            return 3, lambda i: (pl.ds(pl.multiple_of(i * 16, 16), 16), slice(None))
        return 4, lambda i: (i, slice(None), slice(c0, c0 + size))

    def stage_3(u):
        n = REDUCE_UNITS[u][0]
        for r in ORDER:
            copies["y", u, r].wait_recv()
        number, at = blocks(u)

        def body(i):
            total = held[n][me, *at(i)].astype(F32)
            for r in range(3):
                total = total + from_y[n][r, *at(i)].astype(F32)
            mine[n][at(i)] = total.astype(mine[n].dtype)

        loop(number, body)
        begin(("t", u), remote(row_of(u, mine[n]), row_of(u, theirs[n]), t_send.at[u], t_recv.at[u], twin))

    def stage_4(u):
        n, c0, size = REDUCE_UNITS[u]
        copies["t", u].wait_recv()
        number, at = blocks(u)
        target = outs[n] if ended[n] is None else ended[n]

        def body(i):
            if ended[n] is None:
                target[at(i)] = mine[n][at(i)].astype(F32) + theirs[n][at(i)].astype(F32)
            else:
                target[at(i)] = mine[n][at(i)] + theirs[n][at(i)]

        loop(number, body)
        if ended[n] is not None:
            part = (slice(None), pl.ds(c0, size))
            for r in ORDER:
                src, dst = target.at[lax.rem(z + r, 4), *part], outs[n].at[z, *part]
                begin(("z", u, r), remote(src, dst, z_send.at[u, r - 1], z_recv.at[u, r - 1], zs[r]))
            copy = pltpu.make_async_copy(target.at[z, *part], outs[n].at[z, *part], keep.at[u])
            copy.start()
            copies["keep", u] = copy

    ready = set()
    count = len(REDUCE_UNITS)
    stages = (stage_0, stage_1, stage_2, stage_3, stage_4)
    for step in range(count + 16):
        for s, stage in enumerate(stages):
            if 0 <= step - 4 * s < count:
                stage(step - 4 * s)
    o_d[...] = l_d[0:216, :]

    def landed(n):
        for u in range(count):
            if REDUCE_UNITS[u][0] == n:
                copies["keep", u].wait()
                for r in ORDER:
                    copies["z", u, r].wait_recv()

    for n, out in ((1, o_g), (2, o_u)):
        landed(n)
        for zz in range(4):
            for q in range(8):
                first = (4 * q + zz) * 216
                out[:, first : first + 216] = outs[n][zz, :, 224 * q : 224 * q + 216].astype(F32)
    landed(4)
    for zz in range(4):
        for q in range(8):
            for part in range(3):
                first, at = part * 1536 + (4 * q + zz) * 48, part * 384 + q * 48
                o_in[:, first : first + 48] = l_in[zz, :, at : at + 48].astype(F32)
    landed(5)
    o_s[...] = b_s[0] + b_s[1] + b_s[2] + b_s[3]
    for copy in sent:
        copy.wait_send()


def reduce(g_d, g_g, g_u, g_o, g_in, g_s):
    shape = jax.ShapeDtypeStruct
    dma = pltpu.SemaphoreType.DMA
    vm = pltpu.VMEM
    count = len(REDUCE_UNITS)
    big = ((4, 48, 1792), (4, 48, 1792), (4, 48, 1152))
    return pl.pallas_call(
        reduce_kernel,
        out_shape=(
            shape((216, 1536), F32),
            shape((48, 6912), F32),
            shape((48, 6912), F32),
            shape((48, 1536), F32),
            shape((48, 4608), F32),
            shape((8, 128), F32),
        ),
        in_specs=[ANY] * 6,
        out_specs=[VMEM] * 6,
        scratch_shapes=[
            vm((8, 224, 1536), BF16), vm((8, 4, 48, 1792), BF16), vm((8, 4, 48, 1792), BF16),
            vm((8, 48, 1536), BF16), vm((8, 4, 48, 1152), BF16), vm((8, 4, 8, 128), F32),
            vm((4, 2, 48, 1792), BF16), vm((4, 2, 48, 1792), BF16), vm((4, 48, 768), BF16),
            vm((4, 2, 48, 1152), BF16), vm((4, 2, 8, 128), F32),
            vm((4, 224, 1536), BF16), vm((4, 2, 48, 1792), BF16), vm((4, 2, 48, 1792), BF16),
            vm((4, 48, 768), BF16), vm((4, 2, 48, 1152), BF16), vm((4, 2, 8, 128), F32),
            vm((3, 224, 1536), BF16), vm((3, 4, 48, 1792), BF16), vm((3, 4, 48, 1792), BF16),
            vm((3, 48, 1536), BF16), vm((3, 4, 48, 1152), BF16), vm((3, 4, 8, 128), F32),
            vm((224, 1536), BF16), vm(big[0], BF16), vm(big[1], BF16), vm((48, 1536), BF16), vm(big[2], BF16),
            vm((4, 8, 128), F32),
            vm((224, 1536), BF16), vm(big[0], BF16), vm(big[1], BF16), vm((48, 1536), BF16), vm(big[2], BF16),
            vm((4, 8, 128), F32),
            vm(big[0], BF16), vm(big[1], BF16), vm(big[2], BF16), vm((4, 8, 128), F32),
            vm((224, 1536), F32), vm(big[0], BF16), vm(big[1], BF16), vm(big[2], BF16), vm((4, 8, 128), F32),
            dma((6,)), dma((count,)), dma((count,)), dma((count,)), dma((count,)), dma((count, 3)), dma((count, 3)),
            dma((count,)), dma((count,)), dma((count, 3)), dma((count, 3)), dma((count,)),
        ],
        compiler_params=pltpu.CompilerParams(
            collective_id=2, has_side_effects=True, vmem_limit_bytes=63 * 2**20
        ),
        name="reduce_grads",
    )(g_d, g_g, g_u, g_o, g_in, g_s)


def local(inputs, cotangent, w_in, w_out, w_gate, w_up, w_down, kernel, gain_mix, gain_ffn):
    small = jnp.concatenate([kernel[0], gain_mix, gain_ffn], axis=0).astype(F32)
    small = jnp.pad(small, ((0, 3), (0, 80)))
    y, gx, g_in, g_o, g_g, g_u, g_d, g_s = run_blocks(
        inputs.reshape(128, 1536), cotangent.reshape(128, 1536), small, w_in[0], w_out[0], w_gate[0], w_up[0], w_down[0]
    )
    o_d, o_g, o_u, o_o, o_in, o_s = reduce(
        g_d.reshape(8, 224, 1536),
        g_g.reshape(8, 4, 48, 1792),
        g_u.reshape(8, 4, 48, 1792),
        g_o.reshape(8, 48, 1536),
        g_in.reshape(8, 4, 48, 1152),
        g_s.reshape(8, 4, 8, 128),
    )
    return (
        y.reshape(1, 2, 64, 1536),
        gx.reshape(1, 2, 64, 1536),
        o_in[None],
        o_o[None],
        o_g[None],
        o_u[None],
        o_d[None],
        o_s[None, 0:3, :48],
        o_s[3:4, :48],
        o_s[4:5, :48],
    )


def solution(mesh):
    names = ("section", "xl", "xh", "y", "z")
    fine = Mesh(mesh.devices.reshape(2, 2, 2, 4, 4), names)
    tokens, shard = ("xl", "xh", "y", "z"), ("xh", "y", "z")
    weight = P("section", shard, None)
    acts = P("section", None, tokens, None)
    return jax.shard_map(
        local,
        mesh=fine,
        in_specs=(
            P(None, tokens, None),
            P(None, tokens, None),
            weight,
            weight,
            weight,
            weight,
            weight,
            P("section", None, shard),
            P("section", shard),
            P("section", shard),
        ),
        out_specs=(
            acts,
            acts,
            weight,
            weight,
            weight,
            weight,
            weight,
            P("section", None, shard),
            P("section", shard),
            P("section", shard),
        ),
        check_vma=False,
    )
```

```python
import functools

import jax
import jax.numpy as jnp
from jax import lax
from jax.experimental import pallas as pl
from jax.experimental.pallas import tpu as pltpu
from jax.sharding import Mesh
from jax.sharding import PartitionSpec as P

F32, BF16 = jnp.float32, jnp.bfloat16
MESH = pl.DeviceIdType.MESH
EPS = 1e-06
ANY = pl.BlockSpec(memory_space=pl.ANY)
VMEM = pl.BlockSpec(memory_space=pltpu.VMEM)
ORDER = (1, 3, 2)

GATHER_UNITS = (
    (2, 0, 1536), (0, 0, 128), (1, 0, 640), (1, 640, 512),
    (3, 0, 640), (4, 0, 640), (3, 640, 640), (4, 640, 640), (3, 1280, 512), (4, 1280, 512),
    (5, 0, 80), (5, 80, 80), (5, 160, 64),
)
GATHER_LAGS = (3, 5)
FORWARD_AT = ((8, 9, 12, 15), (11, 13, 15, 17))
GO_AFTER = 15
REDUCE_UNITS = (
    (0, 0, 32, 0),
    (2, 0, 128, 2),
    (0, 32, 48, 1),
    (2, 128, 128, 2),
    (4, 0, 256, 0),
    (1, 0, 768, 0),
    (2, 256, 640, 0),
    (4, 256, 128, 0),
    (4, 384, 128, 1),
    (5, 0, 128, 0),
    (4, 512, 256, 2),
    (1, 768, 512, 0),
    (1, 1280, 512, 0),
    (2, 896, 128, 0),
    (4, 768, 128, 2),
    (4, 896, 256, 2),
    (2, 1024, 640, 0),
    (2, 1664, 128, 1),
    (0, 80, 16, 2),
    (3, 0, 1536, 0),
    (0, 96, 48, 0),
    (0, 144, 16, 2),
    (0, 160, 32, 0),
    (0, 192, 32, 0),
)
REDUCE_LAGS = (0, 21, 27, 35, 41)


def place():
    return tuple(lax.axis_index(name) for name in ("section", "xl", "xh", "y", "z"))


def barrier_all(devices):
    barrier = pltpu.get_barrier_semaphore()
    for device in devices:
        pl.semaphore_signal(barrier, inc=1, device_id=device, device_id_type=MESH)
    pl.semaphore_wait(barrier, len(devices))


def remote(src, dst, send, recv, device):
    return pltpu.make_async_remote_copy(
        src_ref=src, dst_ref=dst, send_sem=send, recv_sem=recv, device_id=device, device_id_type=MESH
    )


def plane_peers():
    section, xl, xh, y, z = place()
    partner = {"xh": 1 - xh, "xl": 1 - xl}
    twin = {"xl": 1 - xl}
    zs = {r: {"z": lax.rem(z + r, 4)} for r in ORDER}
    ys = {r: {"y": lax.rem(y + r, 4)} for r in ORDER}
    return partner, twin, zs, ys


def dot_nn(a, b):
    return lax.dot_general(a, b, (((1,), (0,)), ((), ())), preferred_element_type=F32)


def dot_nt(a, b):
    return lax.dot_general(a, b, (((1,), (1,)), ((), ())), preferred_element_type=F32)


def dot_tn(a, b):
    return lax.dot_general(a, b, (((0,), (0,)), ((), ())), preferred_element_type=F32)


def cols(j, width):
    return pl.ds(pl.multiple_of(j * width, width), width)


def loop(count, body):
    def step(j, carry):
        body(j)
        return carry

    lax.fori_loop(0, count, step, 0)


def blocks_kernel(
    x_ref, cot_ref, small, w_in, w_out, w_gate, w_up, w_down,
    y_ref, gx_ref, gin_h, gout_h, gg_h, gu_h, gd_h, gs_ref,
    xa, xn, n2, ea, fa, part, rr, proj, ge, dce, cv, ha, hb, mx, by_gate, by_up, hd, dg, du,
    mid, dmid, dp, g0, win, wout, wg, wu, wd, sm, gains, taps, gtap, ggain,
    store, a_send, a_recv, s_send, s_recv, h_send, h_recv, c_send, c_recv,
    z_send, z_recv, y_send, y_recv, p_send, p_recv, q_send, q_recv, go,
):
    section, xl, xh, y, z = place()
    partner, twin, zs, ys = plane_peers()
    core = {"section": 1 - section}
    group = xl * 8 + xh * 4 + y
    after, before = lax.rem(group + 1, 16), lax.rem(group + 15, 16)
    has_after, has_before = group < 15, group > 0

    def at_group(g):
        return {"xl": g // 8, "xh": lax.rem(g // 4, 2), "y": lax.rem(g, 4)}

    barrier = pltpu.get_barrier_semaphore()

    def hail(device):
        pl.semaphore_signal(barrier, inc=1, device_id=device, device_id_type=MESH)

    for device in (partner, twin, core, *zs.values(), *ys.values()):
        hail(device)

    @pl.when(has_after)
    def _():
        hail(at_group(after))

    @pl.when(has_before)
    def _():
        hail(at_group(before))

    me = xh * 4 + y
    weights = (sm, win, wout, wg, wu, wd)
    cut = (None, dp, None, hd, dg, None)
    rows = (32, 192, 48, 192, 192, 224)
    cut_conv(w_in, dp)
    wout[pl.ds(pl.multiple_of(me * 48, 16), 48), :] = w_out[...]
    first_d = pl.multiple_of(me * 224, 16)
    wd[pl.ds(first_d, 224), :] = jnp.concatenate([w_down[...], jnp.zeros((8, 1536), BF16)], axis=0)
    pl.semaphore_wait(barrier, 10 - (group + 1) // 16 + (group + 15) // 16)

    def of_z(n, ref, first, zz):
        size = rows[n] // 4
        return ref.at[pl.ds(pl.multiple_of(first + zz * size, 8 if n == 0 else 16), size)]

    def rows_q(n, q):
        return pl.multiple_of(q * rows[n], 8 if n == 0 else 16)

    sent, z_copies = [], {}

    def push_z(n):
        size = rows[n] // 4
        for r in ORDER:
            src = small if n == 0 else of_z(n, cut[n], 0, lax.rem(z + r, 4))
            dst = of_z(n, weights[n], me * rows[n], z)
            copy = remote(src, dst, z_send.at[n, r - 1], z_recv.at[n, r - 1], zs[r])
            copy.start()
            z_copies[n, r] = copy
            sent.append(copy)
        mine = pl.ds(pl.multiple_of(me * rows[n] + z * size, 8 if n == 0 else 16), size)
        if n == 0:
            sm[mine, :] = small[...]
        else:
            weights[n][mine, :] = cut[n][pl.ds(pl.multiple_of(z * size, 16), size), 0 : weights[n].shape[1]]

    @pl.when(section == 1)
    def _():
        pl.semaphore_wait(go, 1)

    def own_rows(mb):
        return pl.ds(pl.multiple_of(mb * 256 + z * 64, 64), 64)

    def spread(n, buf, mb):
        at = buf.at[own_rows(mb)]
        return [remote(at, at, a_send.at[n, mb, r - 1], a_recv.at[n, mb, r - 1], zs[r]) for r in ORDER]

    x_all, n_all, e_all, f_all = ([spread(n, buf, mb) for mb in range(2)] for n, buf in enumerate((xa, n2, ea, fa)))

    def begin(copies):
        for copy in copies:
            copy.start()

    def arrived(copies):
        for copy in copies:
            copy.wait_recv()

    mb_rows = [slice(0, 256), slice(256, 512)]
    core_x, core_g = [], []
    for mb in range(2):
        at = pl.ds(mb * 64, 64)
        core_x.append(remote(y_ref.at[at], xa.at[own_rows(mb)], c_send.at[0, mb], c_recv.at[0, mb], core))
        core_g.append(remote(g0.at[at], ea.at[own_rows(mb)], c_send.at[1, mb], c_recv.at[1, mb], core))

    push_z(0)
    push_z(1)

    @pl.when(section == 0)
    def _():
        for mb in range(2):
            xa[own_rows(mb), :] = x_ref[mb * 64 : mb * 64 + 64, :]
            begin(x_all[mb])

    @pl.when(section == 1)
    def _():
        for mb in range(2):
            ea[own_rows(mb), :] = cot_ref[mb * 64 : mb * 64 + 64, :]
            begin(e_all[mb])

    cut_ffn(w_gate, hd)
    push_z(3)
    cut_ffn(w_up, dg)
    push_z(4)

    def piece(u, q):
        n, first, size = GATHER_UNITS[u]
        if n == 5:
            return wd.at[pl.ds(pl.multiple_of(q * 224 + first, 16), size)]
        if n == 2:
            return wout.at[pl.ds(rows_q(2, q), 48)]
        return weights[n].at[pl.ds(rows_q(n, q), rows[n]), pl.ds(first, size)]

    def half(u, q, h):
        n, first, size = GATHER_UNITS[u]
        if n in (2, 5):
            left = pl.ds(pl.multiple_of(h * 768, 128), 768)
            if n == 5:
                return wd.at[pl.ds(pl.multiple_of(q * 224 + first, 16), size), left]
            return wout.at[pl.ds(rows_q(2, q), 48), left]
        part_rows = rows[n] // 2
        return weights[n].at[
            pl.ds(pl.multiple_of(q * rows[n] + h * part_rows, 8 if n == 0 else 16), part_rows), pl.ds(first, size)
        ]

    y_copies, p_copies, q_copies, started = {}, {}, {}, set()

    def stage_y(u):
        n = GATHER_UNITS[u][0]
        if n not in started:
            started.add(n)
            if n not in (2, 5):
                for r in ORDER:
                    z_copies[n, r].wait_recv()
        for r in ORDER:
            src = piece(u, me)
            copy = remote(src, src, y_send.at[u, r - 1], y_recv.at[u, r - 1], ys[r])
            copy.start()
            y_copies[u, r] = copy
            sent.append(copy)
        push_p(u, 0)

    def push_p(u, r):
        src = half(u, xh * 4 + lax.rem(y + 4 - r, 4), xl)
        copy = remote(src, src, p_send.at[u, r], p_recv.at[u, r], partner)
        copy.start()
        p_copies[u, r] = copy
        sent.append(copy)

    def stage_p(u):
        for r in ORDER:
            y_copies[u, r].wait_recv()
            push_p(u, r)

    def stage_q(u):
        for r in (0, *ORDER):
            p_copies[u, r].wait_recv()
            src = half(u, (1 - xh) * 4 + lax.rem(y + 4 - r, 4), 1 - xl)
            copy = remote(src, src, q_send.at[u, r], q_recv.at[u, r], twin)
            copy.start()
            q_copies[u, r] = copy
            sent.append(copy)

    def need(n):
        for u, unit in enumerate(GATHER_UNITS):
            if unit[0] == n:
                for r in (0, *ORDER):
                    q_copies[u, r].wait_recv()

    def scatter(n, mb, j, r):
        at = cols(j, 512)
        src = part.at[pl.ds(pl.multiple_of(mb * 256 + lax.rem(z + r, 4) * 64, 64), 64), at]
        dst = rr.at[n, r - 1, pl.ds(mb * 64, 64), at]
        return remote(src, dst, s_send.at[n, mb, j, r - 1], s_recv.at[n, mb, j, r - 1], zs[r])

    def sum_over_z(n, mb, block):
        def body(j):
            part[mb_rows[mb], cols(j, 512)] = block(cols(j, 512)).astype(BF16)
            for r in ORDER:
                scatter(n, mb, j, r).start()

        loop(3, body)

    def sum_arrived(n, mb):
        def body(j):
            for r in ORDER:
                scatter(n, mb, j, r).wait_recv()

        loop(3, body)

    def sum_sent(n, mb):
        def body(j):
            for r in ORDER:
                scatter(n, mb, j, r).wait_send()

        loop(3, body)

    def summed(n, at, mine):
        total = part[mine, :].astype(F32)
        for r in range(3):
            total = total + rr[n, r, at, :].astype(F32)
        return total

    def own_blocks(mb, body):
        def step(i):
            at = pl.ds(pl.multiple_of(mb * 64 + i * 32, 32), 32)
            mine = pl.ds(pl.multiple_of(mb * 256 + z * 64 + i * 32, 32), 32)
            body(at, mine)

        loop(2, step)

    def rms(values):
        return lax.rsqrt(jnp.mean(values * values, axis=-1, keepdims=True) + EPS)

    def take_input():
        for f in range(32):
            gains[0:2, 48 * f : 48 * f + 48] = sm[8 * f + 3 : 8 * f + 5, 0:48]
        for q in range(8):
            taps[0:3, 48 * q : 48 * q + 48] = sm[pl.ds(pl.multiple_of(q * 32 + z * 8, 8), 8), :][0:3, 0:48]

    halo_after = [
        remote(ge.at[mb, pl.ds(256, 8)], ha.at[mb], h_send.at[0, mb], h_recv.at[0, mb], at_group(after)) for mb in range(2)
    ]
    halo_before = [
        remote(dce.at[mb, pl.ds(0, 8)], hb.at[mb], h_send.at[1, mb], h_recv.at[1, mb], at_group(before)) for mb in range(2)
    ]

    def project(mb):
        arrived(x_all[mb])

        def norm(i):
            at = pl.ds(pl.multiple_of(mb * 256 + i * 32, 32), 32)
            values = xa[at, :].astype(F32)
            xn[at, :] = (values * rms(values) * gains[0:1, :]).astype(BF16)

        loop(8, norm)

        def body(j):
            proj[j, mb_rows[mb], :] = dot_nn(xn[mb_rows[mb], :], win[:, cols(j, 384)])

        loop(3, body)
        ge[mb, 8:264, :] = proj[0, mb_rows[mb], :] * proj[2, mb_rows[mb], :]

        @pl.when(has_after)
        def _():
            halo_after[mb].start()

    def tap(k):
        return taps[k : k + 1, :]

    def mix(mb):
        @pl.when(has_before)
        def _():
            halo_after[mb].wait_recv()
            ge[mb, 0:8, :] = ha[mb]

        @pl.when(jnp.logical_not(has_before))
        def _():
            ge[mb, 0:8, :] = jnp.zeros((8, 384), F32)

        for zc in range(4):
            t0, at = 8 + 64 * zc, slice(mb * 256 + 64 * zc, mb * 256 + 64 * zc + 64)
            total = tap(0) * ge[mb, t0 : t0 + 64, :]
            for k in (1, 2):
                total = total + tap(k) * ge[mb, t0 - k : t0 - k + 64, :]
            cv[at, :] = total
            mx[at, :] = (proj[1, at, :] * total).astype(BF16)
        sum_over_z(0, mb, lambda at: dot_nn(mx[mb_rows[mb], :], wout[:, at]))

    def middle(mb):
        sum_arrived(0, mb)

        def body(at, mine):
            values = xa[mine, :].astype(F32) + summed(0, at, mine)
            mid[at, :] = values
            n2[mine, :] = (values * rms(values) * gains[1:2, :]).astype(BF16)

        own_blocks(mb, body)
        begin(n_all[mb])

    def gate(mb):
        arrived(n_all[mb])

        def body(j):
            at = cols(j, 896)
            gating = dot_nn(n2[mb_rows[mb], :], wg[:, at])
            up_part = dot_nn(n2[mb_rows[mb], :], wu[:, at])
            sg = jax.nn.sigmoid(gating)
            silu = gating * sg
            by_gate[mb_rows[mb], at] = up_part * sg * (1.0 + gating * (1.0 - sg))
            by_up[mb_rows[mb], at] = silu
            hd[mb_rows[mb], at] = (silu * up_part).astype(BF16)

        loop(2, body)

    def down(mb):
        sum_sent(0, mb)
        sum_over_z(1, mb, lambda at: dot_nn(hd[mb_rows[mb], :], wd[:, at]))

    def finish(mb):
        sum_arrived(1, mb)

        def body(at, mine):
            y_ref[at, :] = (mid[at, :] + summed(1, at, mine)).astype(BF16)

        own_blocks(mb, body)

        @pl.when(section == 0)
        def _():
            core_x[mb].start()

    def wait_x():
        @pl.when(section == 1)
        def _():
            for mb in range(2):
                core_x[mb].wait_recv()
                begin(x_all[mb])

    def free_cuts():
        for n in (1, 3, 4):
            for r in ORDER:
                z_copies[n, r].wait_send()

    def both(stage):
        stage(0)
        stage(1)

    def forward_1():
        need(0)
        take_input()
        need(1)
        wait_x()
        both(project)

    def forward_2():
        need(2)
        both(mix)

    def forward_3():
        both(middle)

    def forward_4():
        need(3)
        need(4)
        free_cuts()
        both(gate)

    def forward_5():
        need(5)
        both(down)

    segments = (forward_1, forward_2, forward_3, forward_4)
    count = len(GATHER_UNITS)
    lag_p, lag_q = GATHER_LAGS
    for step in range(count + lag_q):
        if step < count:
            stage_y(step)
        if 0 <= step - lag_p < count:
            stage_p(step - lag_p)
        if step == GO_AFTER:

            @pl.when(section == 0)
            def _():
                pl.semaphore_signal(go, inc=1, device_id=core, device_id_type=MESH)

        if 0 <= step - lag_q < count:
            stage_q(step - lag_q)
        for turn, segment in enumerate(segments):
            if step == FORWARD_AT[0][turn]:
                pl.when(section == 0)(segment)
            if step == FORWARD_AT[1][turn]:
                pl.when(section == 1)(segment)

    forward_5()
    both(finish)
    for copy in sent:
        if not any(copy is z_copies[n, r] for n in (1, 3, 4) for r in ORDER):
            copy.wait_send()

    ggain[...] = jnp.zeros((2, 1536), F32)

    def take_gradient(mb):
        @pl.when(section == 0)
        def _():
            core_g[mb].wait_recv()
            begin(e_all[mb])

    def back_hidden(mb):
        arrived(e_all[mb])

        def body(j):
            at = cols(j, 896)
            dh = dot_nt(ea[mb_rows[mb], :], wd[at, :])
            dg[mb_rows[mb], at] = (dh * by_gate[mb_rows[mb], at]).astype(BF16)
            du[mb_rows[mb], at] = (dh * by_up[mb_rows[mb], at]).astype(BF16)

        loop(2, body)

    def back_ffn(mb):
        sum_sent(1, mb)
        sum_over_z(2, mb, lambda at: dot_nt(dg[mb_rows[mb], :], wg[at, :]) + dot_nt(du[mb_rows[mb], :], wu[at, :]))

    def back_middle(mb):
        sum_arrived(2, mb)

        def body(at, mine):
            dn2 = summed(2, at, mine)
            values = mid[at, :]
            scale = rms(values)
            weighted = dn2 * gains[1:2, :]
            mean_term = jnp.mean(weighted * values, axis=-1, keepdims=True)
            grad = ea[mine, :].astype(F32) + scale * weighted - values * (scale * scale * scale) * mean_term
            ggain[1:2, :] += jnp.sum(dn2 * values * scale, axis=0, keepdims=True)
            dmid[at, :] = grad
            fa[mine, :] = grad.astype(BF16)

        own_blocks(mb, body)
        begin(f_all[mb])

    def back_mix(mb):
        arrived(f_all[mb])
        dce[mb, 0:256, :] = dot_nt(fa[mb_rows[mb], :], wout[...])
        for zc in range(4):
            at, here = slice(mb * 256 + 64 * zc, mb * 256 + 64 * zc + 64), slice(64 * zc, 64 * zc + 64)
            dm = dce[mb, here, :]
            dp[at, 384:768] = (dm * cv[at, :]).astype(BF16)
            dce[mb, here, :] = dm * proj[1, at, :]

        @pl.when(has_before)
        def _():
            halo_before[mb].start()

    def back_conv(mb):
        @pl.when(has_after)
        def _():
            halo_before[mb].wait_recv()
            dce[mb, 256:264, :] = hb[mb]

        @pl.when(jnp.logical_not(has_after))
        def _():
            dce[mb, 256:264, :] = jnp.zeros((8, 384), F32)

        for zc in range(4):
            at, t0 = slice(mb * 256 + 64 * zc, mb * 256 + 64 * zc + 64), 64 * zc
            total = tap(0) * dce[mb, t0 : t0 + 64, :]
            for k in (1, 2):
                total = total + tap(k) * dce[mb, t0 + k : t0 + k + 64, :]
            dp[at, 0:384] = (total * proj[2, at, :]).astype(BF16)
            dp[at, 768:1152] = (total * proj[0, at, :]).astype(BF16)

    def back_in(mb):
        sum_sent(2, mb)
        sum_over_z(3, mb, lambda at: dot_nt(dp[mb_rows[mb], :], win[at, :]))

    def back_input(mb):
        sum_arrived(3, mb)

        def body(at, mine):
            dn = summed(3, at, mine)
            values = xa[mine, :].astype(F32)
            scale = rms(values)
            weighted = dn * gains[0:1, :]
            mean_term = jnp.mean(weighted * values, axis=-1, keepdims=True)
            grad = dmid[at, :] + scale * weighted - values * (scale * scale * scale) * mean_term
            ggain[0:1, :] += jnp.sum(dn * values * scale, axis=0, keepdims=True)
            gx_ref[at, :] = grad
            g0[at, :] = grad.astype(BF16)

        own_blocks(mb, body)

        @pl.when(section == 1)
        def _():
            core_g[mb].start()

    stores = [
        pltpu.make_async_copy(src, dst, store.at[n])
        for n, (src, dst) in enumerate(((win, gin_h), (wout, gout_h), (wg, gg_h), (wu, gu_h), (wd, gd_h)))
    ]

    def grad(n, width, left, right):
        target = (win, wout, wg, wu, wd)[n]

        def body(j):
            at = cols(j, width)
            target[at, :] = dot_tn(left[:, at], right[...]).astype(BF16)

        loop(target.shape[0] // width, body)
        stores[n].start()

    both(take_gradient)
    both(lambda mb: (back_hidden(mb), back_ffn(mb)))
    grad(4, 896, hd, ea)
    back_middle(0)
    grad(2, 768, n2, dg)
    back_middle(1)
    grad(3, 768, n2, du)
    both(back_mix)
    grad(1, 384, mx, fa)
    for k in range(3):
        total = jnp.zeros((1, 384), F32)
        for mb in range(2):
            for zc in range(4):
                t0 = 8 + 64 * zc - k
                products = dce[mb, 64 * zc : 64 * zc + 64, :] * ge[mb, t0 : t0 + 64, :]
                total = total + jnp.sum(products, axis=0, keepdims=True)
        gtap[k : k + 1, :] = total
    both(lambda mb: (back_conv(mb), back_in(mb)))
    grad(0, 768, xn, dp)
    both(back_input)

    gs_ref[...] = jnp.zeros((256, 128), F32)
    for q in range(8):
        at = pl.ds(pl.multiple_of(q * 32 + z * 8, 8), 8)
        gs_ref[at, 0:48] = gtap[:, 48 * q : 48 * q + 48]
    for f in range(32):
        gs_ref[8 * f + 3 : 8 * f + 5, 0:48] = ggain[0:2, 48 * f : 48 * f + 48]

    for mb in range(2):

        @pl.when(section == 1)
        def _():
            core_g[mb].wait_send()

        @pl.when(section == 0)
        def _():
            core_x[mb].wait_send()

        @pl.when(has_after)
        def _():
            halo_after[mb].wait_send()

        @pl.when(has_before)
        def _():
            halo_before[mb].wait_send()

        sum_sent(3, mb)
        for copies in (x_all, n_all, e_all, f_all):
            for copy in copies[mb]:
                copy.wait_send()
    for copy in stores:
        copy.wait()


def cut_conv(weight, out):
    for q in range(8):
        for zz in range(4):
            for part in range(3):
                first, to = part * 1536 + (4 * q + zz) * 48, part * 384 + q * 48
                out[zz * 48 : zz * 48 + 48, to : to + 48] = weight[:, first : first + 48]


def cut_ffn(weight, out):
    for zz in range(4):
        for q in range(8):
            first = (4 * q + zz) * 216
            out[zz * 48 : zz * 48 + 48, 224 * q : 224 * q + 216] = weight[:, first : first + 216]
            out[zz * 48 : zz * 48 + 48, 224 * q + 216 : 224 * q + 224] = jnp.zeros((48, 8), BF16)


def run_blocks(x, cot, small, w_in, w_out, w_gate, w_up, w_down):
    shape = jax.ShapeDtypeStruct
    dma = pltpu.SemaphoreType.DMA
    vm = pltpu.VMEM
    count = len(GATHER_UNITS)
    return pl.pallas_call(
        blocks_kernel,
        out_shape=(
            shape((128, 1536), BF16),
            shape((128, 1536), F32),
            shape((1536, 1152), BF16),
            shape((384, 1536), BF16),
            shape((1536, 1792), BF16),
            shape((1536, 1792), BF16),
            shape((1792, 1536), BF16),
            shape((256, 128), F32),
        ),
        in_specs=[VMEM] * 8,
        out_specs=[VMEM] * 2 + [ANY] * 5 + [VMEM],
        scratch_shapes=[
            vm((512, 1536), BF16), vm((512, 1536), BF16), vm((512, 1536), BF16), vm((512, 1536), BF16),
            vm((512, 1536), BF16), vm((512, 1536), BF16), vm((4, 3, 128, 1536), BF16),
            vm((3, 512, 384), F32), vm((2, 264, 384), F32), vm((2, 264, 384), F32), vm((512, 384), F32),
            vm((2, 8, 384), F32), vm((2, 8, 384), F32), vm((512, 384), BF16),
            vm((512, 1792), F32), vm((512, 1792), F32), vm((512, 1792), BF16), vm((512, 1792), BF16),
            vm((512, 1792), BF16), vm((128, 1536), F32), vm((128, 1536), F32), vm((512, 1152), BF16),
            vm((128, 1536), BF16),
            vm((1536, 1152), BF16), vm((384, 1536), BF16), vm((1536, 1792), BF16), vm((1536, 1792), BF16),
            vm((1792, 1536), BF16), vm((256, 128), F32), vm((8, 1536), F32), vm((8, 384), F32), vm((8, 384), F32),
            vm((2, 1536), F32),
            dma((5,)), dma((4, 2, 3)), dma((4, 2, 3)), dma((4, 2, 3, 3)), dma((4, 2, 3, 3)),
            dma((2, 2)), dma((2, 2)), dma((2, 2)), dma((2, 2)),
            dma((5, 3)), dma((5, 3)), dma((count, 3)), dma((count, 3)), dma((count, 4)), dma((count, 4)),
            dma((count, 4)), dma((count, 4)), pltpu.SemaphoreType.REGULAR,
        ],
        compiler_params=pltpu.CompilerParams(
            collective_id=1, has_side_effects=True, vmem_limit_bytes=63 * 2**20
        ),
        name="two_blocks",
    )(x, cot, small, w_in, w_out, w_gate, w_up, w_down)


def unit_shape(u):
    n, first, size, mode = REDUCE_UNITS[u]
    if n == 0:
        return (size, 1536), (size, 768)
    if n == 3:
        return (48, 1536), (48, 768)
    height = 8 if n == 5 else 48
    return (4, height, size), (2, height, size)


def unit_buffers(u):
    n, first, size, mode = REDUCE_UNITS[u]
    whole, part = unit_shape(u)
    dtype = F32 if n == 5 else BF16
    shapes = {
        0: ((4, *part), (4, *part), (3, *whole)),
        1: (None, (4, *whole), (3, *whole)),
        2: (None, whole, (3, 2, *whole)),
    }[mode]
    shapes += (whole, whole if n in (1, 2, 4, 5) else None)
    return [None if shape is None else pltpu.VMEM(shape, dtype) for shape in shapes]


def reduce_kernel(
    g_d, g_g, g_u, g_o, g_in, g_s,
    o_d, o_g, o_u, o_o, o_in, o_s,
    v_d, v_g, v_u, v_o, v_in, v_s, l_d, l_g, l_u, l_in, l_s,
    load, q_send, q_recv, p_send, p_recv, y_send, y_recv, t_send, t_recv, z_send, z_recv,
    *buffers,
):
    section, xl, xh, y, z = place()
    partner, twin, zs, ys = plane_peers()
    held = (v_d, v_g, v_u, v_o, v_in, v_s)
    landing = (l_d, l_g, l_u, o_o, l_in, l_s)
    loads = [pltpu.make_async_copy(src, held[n], load.at[n]) for n, src in enumerate((g_d, g_g, g_u, g_o, g_in, g_s))]
    for copy in loads:
        copy.start()
    barrier_all([partner, twin, *zs.values(), *ys.values()])
    count = len(REDUCE_UNITS)
    left = list(buffers)
    slots = [[None if shape is None else left.pop(0) for shape in unit_buffers(u)] for u in range(count)]
    from_twin, from_partner, from_y, theirs, ended = zip(*slots)
    near, far = xh, 1 - xh
    sent, copies = [], {}

    def begin(key, copy):
        copy.start()
        copies[key] = copy
        sent.append(copy)

    def tail(u, h=None):
        n, first, size, mode = REDUCE_UNITS[u]
        across = slice(None) if h is None else pl.ds(pl.multiple_of(h * 768, 128), 768)
        if n == 0:
            return pl.ds(first, size), across
        if n == 3:
            return slice(None), across
        return slice(None) if h is None else pl.ds(h * 2, 2), slice(None), pl.ds(first, size)

    def blocks(u, h=None):
        n, first, size, mode = REDUCE_UNITS[u]
        if n in (0, 3):
            across = slice(None) if h is None else pl.ds(pl.multiple_of(h * 768, 128), 768)
            start = first if n == 0 else 0

            def at(i):
                return (pl.ds(pl.multiple_of(start + i * 16, 16), 16), across), (
                    pl.ds(pl.multiple_of(i * 16, 16), 16),
                    slice(None),
                )

            return (size if n == 0 else 48) // 16, at
        shift = 0 if h is None else h * 2
        return 4 if h is None else 2, lambda i: ((shift + i, slice(None), slice(first, first + size)), (i,))

    def add_rows(u, side, h, other):
        ref = held[REDUCE_UNITS[u][0]]
        number, at = blocks(u, h)

        def body(k):
            row = k // number
            here, there = at(lax.rem(k, number))
            ref[side, row, *here] = ref[side, row, *here] + other[row, *there]

        loop(4 * number, body)

    def send_y(u, source):
        for r in ORDER:
            dst = from_y[u].at[r - 1]
            begin(("y", u, r), remote(source(lax.rem(y + r, 4)), dst, y_send.at[u, r - 1], y_recv.at[u, r - 1], ys[r]))

    def send_p(u, src):
        begin(("p", u), remote(src, from_partner[u], p_send.at[u], p_recv.at[u], partner))

    def send_twin(u):
        src = held[REDUCE_UNITS[u][0]].at[near, y, *tail(u)]
        begin(("t", u), remote(src, theirs[u], t_send.at[u], t_recv.at[u], twin))

    def sum_y(u, sides):
        for r in ORDER:
            copies["y", u, r].wait_recv()
        ref = held[REDUCE_UNITS[u][0]]
        number, at = blocks(u)

        def body(k):
            side = near if len(sides) == 1 else k // number
            here, there = at(lax.rem(k, number))
            total = ref[side, y, *here].astype(F32)
            for r in range(3):
                got = from_y[u][r, *there] if len(sides) == 1 else from_y[u][r, side, *there]
                total = total + got.astype(F32)
            ref[side, y, *here] = total.astype(ref.dtype)

        loop(len(sides) * number, body)

    ready = set()

    def stage_0(u):
        n, first, size, mode = REDUCE_UNITS[u]
        if n not in ready:
            ready.add(n)
            loads[n].wait()
        if mode == 0:
            src = held[n].at[far, :, *tail(u, 1 - xl)]
            begin(("q", u), remote(src, from_twin[u], q_send.at[u], q_recv.at[u], twin))
        elif mode == 1:
            send_p(u, held[n].at[far, :, *tail(u)])
        else:
            send_y(u, lambda row: held[n].at[:, row, *tail(u)])

    def stage_1(u):
        n, first, size, mode = REDUCE_UNITS[u]
        if mode == 0:
            copies["q", u].wait_recv()
            add_rows(u, far, xl, from_twin[u])
            send_p(u, held[n].at[far, :, *tail(u, xl)])
        elif mode == 2:
            sum_y(u, (0, 1))
            send_p(u, held[n].at[far, y, *tail(u)])

    def stage_2(u):
        n, first, size, mode = REDUCE_UNITS[u]
        copies["p", u].wait_recv()
        if mode == 2:
            number, at = blocks(u)

            def body(i):
                here, there = at(i)
                held[n][near, y, *here] = held[n][near, y, *here] + from_partner[u][there]

            loop(number, body)
            send_twin(u)
        else:
            add_rows(u, near, 1 - xl if mode == 0 else None, from_partner[u])
            send_y(u, lambda row: held[n].at[near, row, *tail(u)])

    def stage_3(u):
        if REDUCE_UNITS[u][3] != 2:
            sum_y(u, (0,))
            send_twin(u)

    def stage_4(u):
        n, first, size, mode = REDUCE_UNITS[u]
        copies["t", u].wait_recv()
        number, at = blocks(u)

        def body(i):
            here, there = at(i)
            if n in (0, 3):
                landing[n][here] = held[n][near, y, *here].astype(F32) + theirs[u][there].astype(F32)
            else:
                ended[u][there] = held[n][near, y, *here] + theirs[u][there]

        loop(number, body)
        if n not in (0, 3):
            part = (slice(None), pl.ds(first, size))
            for r in ORDER:
                src, dst = ended[u].at[lax.rem(z + r, 4)], landing[n].at[z, *part]
                begin(("z", u, r), remote(src, dst, z_send.at[u, r - 1], z_recv.at[u, r - 1], zs[r]))
            landing[n][z, :, first : first + size] = ended[u][z]

    stages = (stage_0, stage_1, stage_2, stage_3, stage_4)
    for step in range(count + REDUCE_LAGS[-1]):
        for lag, stage in zip(REDUCE_LAGS, stages):
            if 0 <= step - lag < count:
                stage(step - lag)

    def landed(n):
        for u in range(count):
            if REDUCE_UNITS[u][0] == n:
                for r in ORDER:
                    copies["z", u, r].wait_recv()

    o_d[...] = l_d[0:216, :]
    for n, out in ((1, o_g), (2, o_u)):
        landed(n)
        for zz in range(4):
            for q in range(8):
                first = (4 * q + zz) * 216
                out[:, first : first + 216] = landing[n][zz, :, 224 * q : 224 * q + 216].astype(F32)
    landed(4)
    for zz in range(4):
        for q in range(8):
            for part in range(3):
                first, at = part * 1536 + (4 * q + zz) * 48, part * 384 + q * 48
                o_in[:, first : first + 48] = l_in[zz, :, at : at + 48].astype(F32)
    landed(5)
    o_s[...] = l_s[0] + l_s[1] + l_s[2] + l_s[3]
    for copy in sent:
        copy.wait_send()


def reduce(g_d, g_g, g_u, g_o, g_in, g_s):
    shape = jax.ShapeDtypeStruct
    dma = pltpu.SemaphoreType.DMA
    vm = pltpu.VMEM
    count = len(REDUCE_UNITS)
    return pl.pallas_call(
        reduce_kernel,
        out_shape=(
            shape((216, 1536), F32),
            shape((48, 6912), F32),
            shape((48, 6912), F32),
            shape((48, 1536), F32),
            shape((48, 4608), F32),
            shape((8, 128), F32),
        ),
        in_specs=[ANY] * 6,
        out_specs=[VMEM] * 6,
        scratch_shapes=[
            vm((2, 4, 224, 1536), BF16), vm((2, 4, 4, 48, 1792), BF16), vm((2, 4, 4, 48, 1792), BF16),
            vm((2, 4, 48, 1536), BF16), vm((2, 4, 4, 48, 1152), BF16), vm((2, 4, 4, 8, 128), F32),
            vm((224, 1536), F32), vm((4, 48, 1792), BF16), vm((4, 48, 1792), BF16), vm((4, 48, 1152), BF16),
            vm((4, 8, 128), F32),
            dma((6,)), dma((count,)), dma((count,)), dma((count,)), dma((count,)), dma((count, 3)), dma((count, 3)),
            dma((count,)), dma((count,)), dma((count, 3)), dma((count, 3)),
            *(buffer for u in range(count) for buffer in unit_buffers(u) if buffer is not None),
        ],
        compiler_params=pltpu.CompilerParams(
            collective_id=2, has_side_effects=True, vmem_limit_bytes=63 * 2**20
        ),
        name="reduce_grads",
    )(
        g_d.reshape(2, 4, 224, 1536),
        g_g.reshape(2, 4, 4, 48, 1792),
        g_u.reshape(2, 4, 4, 48, 1792),
        g_o.reshape(2, 4, 48, 1536),
        g_in.reshape(2, 4, 4, 48, 1152),
        g_s.reshape(2, 4, 4, 8, 128),
    )


def local(inputs, cotangent, w_in, w_out, w_gate, w_up, w_down, kernel, gain_mix, gain_ffn):
    small = jnp.concatenate([kernel[0], gain_mix, gain_ffn], axis=0).astype(F32)
    small = jnp.pad(small, ((0, 3), (0, 80)))
    y, gx, g_in, g_o, g_g, g_u, g_d, g_s = run_blocks(
        inputs.reshape(128, 1536), cotangent.reshape(128, 1536), small, w_in[0], w_out[0], w_gate[0], w_up[0], w_down[0]
    )
    o_d, o_g, o_u, o_o, o_in, o_s = reduce(g_d, g_g, g_u, g_o, g_in, g_s)
    return (
        y.reshape(1, 2, 64, 1536),
        gx.reshape(1, 2, 64, 1536),
        o_in[None],
        o_o[None],
        o_g[None],
        o_u[None],
        o_d[None],
        o_s[None, 0:3, :48],
        o_s[3:4, :48],
        o_s[4:5, :48],
    )


def solution(mesh):
    names = ("section", "xl", "xh", "y", "z")
    fine = Mesh(mesh.devices.reshape(2, 2, 2, 4, 4), names)
    tokens, shard = ("xl", "xh", "y", "z"), ("xh", "y", "z")
    weight = P("section", shard, None)
    acts = P("section", None, tokens, None)
    return jax.shard_map(
        local,
        mesh=fine,
        in_specs=(
            P(None, tokens, None),
            P(None, tokens, None),
            weight,
            weight,
            weight,
            weight,
            weight,
            P("section", None, shard),
            P("section", shard),
            P("section", shard),
        ),
        out_specs=(
            acts,
            acts,
            weight,
            weight,
            weight,
            weight,
            weight,
            P("section", None, shard),
            P("section", shard),
            P("section", shard),
        ),
        check_vma=False,
    )
```

```python
import functools

import jax
import jax.numpy as jnp
from jax import lax
from jax.experimental import pallas as pl
from jax.experimental.pallas import tpu as pltpu
from jax.sharding import Mesh
from jax.sharding import PartitionSpec as P

F32, BF16 = jnp.float32, jnp.bfloat16
MESH = pl.DeviceIdType.MESH
EPS = 1e-06
ANY = pl.BlockSpec(memory_space=pl.ANY)
VMEM = pl.BlockSpec(memory_space=pltpu.VMEM)
ORDER = (1, 3, 2)

GATHER_UNITS = (
    (2, 0, 1536),
    (0, 0, 128),
    (1, 0, 640),
    (1, 640, 512),
    (5, 0, 80),
    (3, 0, 640),
    (4, 0, 640),
    (4, 640, 512),
    (4, 1152, 640),
    (3, 640, 640),
    (3, 1280, 512),
    (5, 80, 80),
    (5, 160, 64),
)
GATHER_LAGS = (3, 5)
FORWARD_AT = ((9, 9, 10, 10, 11, 12, 16, 16), (11, 12, 13, 14, 16, 17, 17, 17))
GO_AFTER = 12
REDUCE_UNITS = (
    (1, 0, 768, 1),
    (1, 768, 256, 2),
    (4, 0, 1024, 0),
    (2, 0, 1024, 2),
    (0, 0, 16, 2),
    (1, 1024, 128, 1),
    (2, 1024, 512, 0),
    (1, 1152, 256, 2),
    (0, 16, 48, 0),
    (4, 1024, 128, 0),
    (5, 0, 128, 2),
    (0, 64, 80, 0),
    (0, 144, 16, 2),
    (1, 1408, 384, 2),
    (2, 1536, 256, 2),
    (0, 160, 64, 0),
    (3, 0, 1536, 0),
)
REDUCE_LAGS = (0, 11, 16, 20, 24, 29)


def place():
    return tuple(lax.axis_index(name) for name in ("section", "xl", "xh", "y", "z"))


def barrier_all(devices):
    barrier = pltpu.get_barrier_semaphore()
    for device in devices:
        pl.semaphore_signal(barrier, inc=1, device_id=device, device_id_type=MESH)
    pl.semaphore_wait(barrier, len(devices))


def remote(src, dst, send, recv, device):
    return pltpu.make_async_remote_copy(
        src_ref=src, dst_ref=dst, send_sem=send, recv_sem=recv, device_id=device, device_id_type=MESH
    )


def plane_peers():
    section, xl, xh, y, z = place()
    partner = {"xh": 1 - xh, "xl": 1 - xl}
    twin = {"xl": 1 - xl}
    zs = {r: {"z": lax.rem(z + r, 4)} for r in ORDER}
    ys = {r: {"y": lax.rem(y + r, 4)} for r in ORDER}
    return partner, twin, zs, ys


def dot_nn(a, b):
    return lax.dot_general(a, b, (((1,), (0,)), ((), ())), preferred_element_type=F32)


def dot_nt(a, b):
    return lax.dot_general(a, b, (((1,), (1,)), ((), ())), preferred_element_type=F32)


def dot_tn(a, b):
    return lax.dot_general(a, b, (((0,), (0,)), ((), ())), preferred_element_type=F32)


def cols(j, width):
    return pl.ds(pl.multiple_of(j * width, width), width)


def loop(count, body):
    def step(j, carry):
        body(j)
        return carry

    lax.fori_loop(0, count, step, 0)


def blocks_kernel(
    x_ref, cot_ref, small, w_in, w_out, w_gate, w_up, w_down,
    y_ref, gx_ref, gin_h, gout_h, gg_h, gu_h, gd_h, gs_ref,
    xa, xn, n2, ea, fa, part, rr, proj, ge, dce, cv, ha, hb, mx, by_gate, by_up, hd, dg, du,
    mid, dmid, dp, g0, win, wout, wg, wu, wd, sm, gains, taps, gtap, ggain,
    store, a_send, a_recv, s_send, s_recv, h_send, h_recv, c_send, c_recv,
    z_send, z_recv, y_send, y_recv, p_send, p_recv, q_send, q_recv, go,
):
    section, xl, xh, y, z = place()
    partner, twin, zs, ys = plane_peers()
    core = {"section": 1 - section}
    group = xl * 8 + xh * 4 + y
    after, before = lax.rem(group + 1, 16), lax.rem(group + 15, 16)
    has_after, has_before = group < 15, group > 0

    def at_group(g):
        return {"xl": g // 8, "xh": lax.rem(g // 4, 2), "y": lax.rem(g, 4)}

    barrier = pltpu.get_barrier_semaphore()

    def hail(device):
        pl.semaphore_signal(barrier, inc=1, device_id=device, device_id_type=MESH)

    for device in (partner, twin, core, *zs.values(), *ys.values()):
        hail(device)

    @pl.when(has_after)
    def _():
        hail(at_group(after))

    @pl.when(has_before)
    def _():
        hail(at_group(before))

    me = xh * 4 + y
    weights = (sm, win, wout, wg, wu, wd)
    cut = (None, dp, None, hd, dg, None)
    rows = (32, 192, 48, 192, 192, 224)
    cut_conv(w_in, dp)
    wout[pl.ds(pl.multiple_of(me * 48, 16), 48), :] = w_out[...]
    first_d = pl.multiple_of(me * 224, 16)
    wd[pl.ds(first_d, 224), :] = jnp.concatenate([w_down[...], jnp.zeros((8, 1536), BF16)], axis=0)
    pl.semaphore_wait(barrier, 10 - (group + 1) // 16 + (group + 15) // 16)

    def of_z(n, ref, first, zz):
        size = rows[n] // 4
        return ref.at[pl.ds(pl.multiple_of(first + zz * size, 8 if n == 0 else 16), size)]

    def rows_q(n, q):
        return pl.multiple_of(q * rows[n], 8 if n == 0 else 16)

    sent, z_copies = [], {}

    def push_z(n):
        size = rows[n] // 4
        for r in ORDER:
            src = small if n == 0 else of_z(n, cut[n], 0, lax.rem(z + r, 4))
            dst = of_z(n, weights[n], me * rows[n], z)
            copy = remote(src, dst, z_send.at[n, r - 1], z_recv.at[n, r - 1], zs[r])
            copy.start()
            z_copies[n, r] = copy
            sent.append(copy)
        mine = pl.ds(pl.multiple_of(me * rows[n] + z * size, 8 if n == 0 else 16), size)
        if n == 0:
            sm[mine, :] = small[...]
        else:
            weights[n][mine, :] = cut[n][pl.ds(pl.multiple_of(z * size, 16), size), 0 : weights[n].shape[1]]

    @pl.when(section == 1)
    def _():
        pl.semaphore_wait(go, 1)

    def own_rows(mb):
        return pl.ds(pl.multiple_of(mb * 256 + z * 64, 64), 64)

    def spread(n, buf, mb):
        at = buf.at[own_rows(mb)]
        return [remote(at, at, a_send.at[n, mb, r - 1], a_recv.at[n, mb, r - 1], zs[r]) for r in ORDER]

    x_all, n_all, e_all, f_all = ([spread(n, buf, mb) for mb in range(2)] for n, buf in enumerate((xa, n2, ea, fa)))

    def begin(copies):
        for copy in copies:
            copy.start()

    def arrived(copies):
        for copy in copies:
            copy.wait_recv()

    mb_rows = [slice(0, 256), slice(256, 512)]
    core_x, core_g = [], []
    for mb in range(2):
        at = pl.ds(mb * 64, 64)
        core_x.append(remote(y_ref.at[at], xa.at[own_rows(mb)], c_send.at[0, mb], c_recv.at[0, mb], core))
        core_g.append(remote(g0.at[at], ea.at[own_rows(mb)], c_send.at[1, mb], c_recv.at[1, mb], core))

    push_z(0)
    push_z(1)

    @pl.when(section == 0)
    def _():
        for mb in range(2):
            xa[own_rows(mb), :] = x_ref[mb * 64 : mb * 64 + 64, :]
            begin(x_all[mb])

    @pl.when(section == 1)
    def _():
        for mb in range(2):
            ea[own_rows(mb), :] = cot_ref[mb * 64 : mb * 64 + 64, :]
            begin(e_all[mb])

    cut_ffn(w_gate, hd)
    push_z(3)
    cut_ffn(w_up, dg)
    push_z(4)

    def piece(u, q):
        n, first, size = GATHER_UNITS[u]
        if n == 5:
            return wd.at[pl.ds(pl.multiple_of(q * 224 + first, 16), size)]
        if n == 2:
            return wout.at[pl.ds(rows_q(2, q), 48)]
        return weights[n].at[pl.ds(rows_q(n, q), rows[n]), pl.ds(first, size)]

    def half(u, q, h):
        n, first, size = GATHER_UNITS[u]
        if n in (2, 5):
            left = pl.ds(pl.multiple_of(h * 768, 128), 768)
            if n == 5:
                return wd.at[pl.ds(pl.multiple_of(q * 224 + first, 16), size), left]
            return wout.at[pl.ds(rows_q(2, q), 48), left]
        part_rows = rows[n] // 2
        return weights[n].at[
            pl.ds(pl.multiple_of(q * rows[n] + h * part_rows, 8 if n == 0 else 16), part_rows), pl.ds(first, size)
        ]

    y_copies, p_copies, q_copies, started = {}, {}, {}, set()

    def stage_y(u):
        n = GATHER_UNITS[u][0]
        if n not in started:
            started.add(n)
            if n not in (2, 5):
                for r in ORDER:
                    z_copies[n, r].wait_recv()
        for r in ORDER:
            src = piece(u, me)
            copy = remote(src, src, y_send.at[u, r - 1], y_recv.at[u, r - 1], ys[r])
            copy.start()
            y_copies[u, r] = copy
            sent.append(copy)
        push_p(u, 0)

    def push_p(u, r):
        src = half(u, xh * 4 + lax.rem(y + 4 - r, 4), xl)
        copy = remote(src, src, p_send.at[u, r], p_recv.at[u, r], partner)
        copy.start()
        p_copies[u, r] = copy
        sent.append(copy)

    def stage_p(u):
        for r in ORDER:
            y_copies[u, r].wait_recv()
            push_p(u, r)

    def stage_q(u):
        for r in (0, *ORDER):
            p_copies[u, r].wait_recv()
            src = half(u, (1 - xh) * 4 + lax.rem(y + 4 - r, 4), 1 - xl)
            copy = remote(src, src, q_send.at[u, r], q_recv.at[u, r], twin)
            copy.start()
            q_copies[u, r] = copy
            sent.append(copy)

    def need(n):
        for u, unit in enumerate(GATHER_UNITS):
            if unit[0] == n:
                for r in (0, *ORDER):
                    q_copies[u, r].wait_recv()

    def scatter(n, mb, j, r):
        at = cols(j, 512)
        src = part.at[pl.ds(pl.multiple_of(mb * 256 + lax.rem(z + r, 4) * 64, 64), 64), at]
        dst = rr.at[n, r - 1, pl.ds(mb * 64, 64), at]
        return remote(src, dst, s_send.at[n, mb, j, r - 1], s_recv.at[n, mb, j, r - 1], zs[r])

    def sum_over_z(n, mb, block):
        def body(j):
            part[mb_rows[mb], cols(j, 512)] = block(cols(j, 512)).astype(BF16)
            for r in ORDER:
                scatter(n, mb, j, r).start()

        loop(3, body)

    def sum_arrived(n, mb):
        def body(j):
            for r in ORDER:
                scatter(n, mb, j, r).wait_recv()

        loop(3, body)

    def sum_sent(n, mb):
        def body(j):
            for r in ORDER:
                scatter(n, mb, j, r).wait_send()

        loop(3, body)

    def summed(n, at, mine):
        total = part[mine, :].astype(F32)
        for r in range(3):
            total = total + rr[n, r, at, :].astype(F32)
        return total

    def own_blocks(mb, body):
        def step(i):
            at = pl.ds(pl.multiple_of(mb * 64 + i * 32, 32), 32)
            mine = pl.ds(pl.multiple_of(mb * 256 + z * 64 + i * 32, 32), 32)
            body(at, mine)

        loop(2, step)

    def rms(values):
        return lax.rsqrt(jnp.mean(values * values, axis=-1, keepdims=True) + EPS)

    def take_input():
        for f in range(32):
            gains[0:2, 48 * f : 48 * f + 48] = sm[8 * f + 3 : 8 * f + 5, 0:48]
        for q in range(8):
            taps[0:3, 48 * q : 48 * q + 48] = sm[pl.ds(pl.multiple_of(q * 32 + z * 8, 8), 8), :][0:3, 0:48]

    halo_after = [
        remote(ge.at[mb, pl.ds(256, 8)], ha.at[mb], h_send.at[0, mb], h_recv.at[0, mb], at_group(after)) for mb in range(2)
    ]
    halo_before = [
        remote(dce.at[mb, pl.ds(0, 8)], hb.at[mb], h_send.at[1, mb], h_recv.at[1, mb], at_group(before)) for mb in range(2)
    ]

    def project(mb):
        arrived(x_all[mb])

        def norm(i):
            at = pl.ds(pl.multiple_of(mb * 256 + i * 32, 32), 32)
            values = xa[at, :].astype(F32)
            xn[at, :] = (values * rms(values) * gains[0:1, :]).astype(BF16)

        loop(8, norm)

        def body(j):
            proj[j, mb_rows[mb], :] = dot_nn(xn[mb_rows[mb], :], win[:, cols(j, 384)])

        loop(3, body)
        ge[mb, 8:264, :] = proj[0, mb_rows[mb], :] * proj[2, mb_rows[mb], :]

        @pl.when(has_after)
        def _():
            halo_after[mb].start()

    def tap(k):
        return taps[k : k + 1, :]

    def mix(mb):
        @pl.when(has_before)
        def _():
            halo_after[mb].wait_recv()
            ge[mb, 0:8, :] = ha[mb]

        @pl.when(jnp.logical_not(has_before))
        def _():
            ge[mb, 0:8, :] = jnp.zeros((8, 384), F32)

        for zc in range(4):
            t0, at = 8 + 64 * zc, slice(mb * 256 + 64 * zc, mb * 256 + 64 * zc + 64)
            total = tap(0) * ge[mb, t0 : t0 + 64, :]
            for k in (1, 2):
                total = total + tap(k) * ge[mb, t0 - k : t0 - k + 64, :]
            cv[at, :] = total
            mx[at, :] = (proj[1, at, :] * total).astype(BF16)
        sum_over_z(0, mb, lambda at: dot_nn(mx[mb_rows[mb], :], wout[:, at]))

    def middle(mb):
        sum_arrived(0, mb)

        def body(at, mine):
            values = xa[mine, :].astype(F32) + summed(0, at, mine)
            mid[at, :] = values
            n2[mine, :] = (values * rms(values) * gains[1:2, :]).astype(BF16)

        own_blocks(mb, body)
        begin(n_all[mb])

    def gate(mb):
        arrived(n_all[mb])

        def body(j):
            at = cols(j, 896)
            gating = dot_nn(n2[mb_rows[mb], :], wg[:, at])
            up_part = dot_nn(n2[mb_rows[mb], :], wu[:, at])
            sg = jax.nn.sigmoid(gating)
            silu = gating * sg
            by_gate[mb_rows[mb], at] = up_part * sg * (1.0 + gating * (1.0 - sg))
            by_up[mb_rows[mb], at] = silu
            hd[mb_rows[mb], at] = (silu * up_part).astype(BF16)

        loop(2, body)

    def sent_before(mb, first, second):
        @pl.when(section == 0)
        def _():
            sum_sent(first, mb)

        @pl.when(section == 1)
        def _():
            sum_sent(second, mb)

    def down(mb):
        sent_before(mb, 0, 3)
        sum_over_z(1, mb, lambda at: dot_nn(hd[mb_rows[mb], :], wd[:, at]))

    def finish(mb):
        sum_arrived(1, mb)

        def body(at, mine):
            y_ref[at, :] = (mid[at, :] + summed(1, at, mine)).astype(BF16)

        own_blocks(mb, body)

        @pl.when(section == 0)
        def _():
            core_x[mb].start()

    def wait_x():
        @pl.when(section == 1)
        def _():
            for mb in range(2):
                core_x[mb].wait_recv()
                begin(x_all[mb])

    def free_cuts():
        for n in (1, 3, 4):
            for r in ORDER:
                z_copies[n, r].wait_send()

    def both(stage):
        stage(0)
        stage(1)

    def begin_forward():
        need(0)
        take_input()
        need(1)
        wait_x()
        project(0)

    def begin_mix():
        need(2)
        mix(0)

    def begin_gate():
        need(3)
        need(4)
        free_cuts()
        gate(0)

    segments = (
        begin_forward, lambda: project(1), begin_mix, lambda: mix(1),
        lambda: middle(0), lambda: middle(1), begin_gate, lambda: gate(1),
    )
    count = len(GATHER_UNITS)
    lag_p, lag_q = GATHER_LAGS
    for step in range(count + lag_q):
        if step < count:
            stage_y(step)
        if 0 <= step - lag_p < count:
            stage_p(step - lag_p)
        if step == GO_AFTER:

            @pl.when(section == 0)
            def _():
                pl.semaphore_signal(go, inc=1, device_id=core, device_id_type=MESH)

        if 0 <= step - lag_q < count:
            stage_q(step - lag_q)
        for turn, segment in enumerate(segments):
            if step == FORWARD_AT[0][turn]:
                pl.when(section == 0)(segment)
            if step == FORWARD_AT[1][turn]:
                pl.when(section == 1)(segment)

    need(5)

    @pl.when(section == 0)
    def _():
        both(down)
        both(finish)

    ggain[...] = jnp.zeros((2, 1536), F32)

    def take_gradient(mb):
        @pl.when(section == 0)
        def _():
            core_g[mb].wait_recv()
            begin(e_all[mb])

    def back_hidden(mb):
        arrived(e_all[mb])

        def body(j):
            at = cols(j, 896)
            dh = dot_nt(ea[mb_rows[mb], :], wd[at, :])
            dg[mb_rows[mb], at] = (dh * by_gate[mb_rows[mb], at]).astype(BF16)
            du[mb_rows[mb], at] = (dh * by_up[mb_rows[mb], at]).astype(BF16)

        loop(2, body)

    def back_ffn(mb):
        sent_before(mb, 1, 0)
        sum_over_z(2, mb, lambda at: dot_nt(dg[mb_rows[mb], :], wg[at, :]) + dot_nt(du[mb_rows[mb], :], wu[at, :]))

    def back_middle(mb):
        sum_arrived(2, mb)

        def body(at, mine):
            dn2 = summed(2, at, mine)
            values = mid[at, :]
            scale = rms(values)
            weighted = dn2 * gains[1:2, :]
            mean_term = jnp.mean(weighted * values, axis=-1, keepdims=True)
            grad = ea[mine, :].astype(F32) + scale * weighted - values * (scale * scale * scale) * mean_term
            ggain[1:2, :] += jnp.sum(dn2 * values * scale, axis=0, keepdims=True)
            dmid[at, :] = grad
            fa[mine, :] = grad.astype(BF16)

        own_blocks(mb, body)
        begin(f_all[mb])

    def back_mix(mb):
        arrived(f_all[mb])
        dce[mb, 0:256, :] = dot_nt(fa[mb_rows[mb], :], wout[...])
        for zc in range(4):
            at, here = slice(mb * 256 + 64 * zc, mb * 256 + 64 * zc + 64), slice(64 * zc, 64 * zc + 64)
            dm = dce[mb, here, :]
            dp[at, 384:768] = (dm * cv[at, :]).astype(BF16)
            dce[mb, here, :] = dm * proj[1, at, :]

        @pl.when(has_before)
        def _():
            halo_before[mb].start()

    def back_conv(mb):
        @pl.when(has_after)
        def _():
            halo_before[mb].wait_recv()
            dce[mb, 256:264, :] = hb[mb]

        @pl.when(jnp.logical_not(has_after))
        def _():
            dce[mb, 256:264, :] = jnp.zeros((8, 384), F32)

        for zc in range(4):
            at, t0 = slice(mb * 256 + 64 * zc, mb * 256 + 64 * zc + 64), 64 * zc
            total = tap(0) * dce[mb, t0 : t0 + 64, :]
            for k in (1, 2):
                total = total + tap(k) * dce[mb, t0 + k : t0 + k + 64, :]
            dp[at, 0:384] = (total * proj[2, at, :]).astype(BF16)
            dp[at, 768:1152] = (total * proj[0, at, :]).astype(BF16)

    def back_in(mb):
        sum_sent(2, mb)
        sum_over_z(3, mb, lambda at: dot_nt(dp[mb_rows[mb], :], win[at, :]))

    def back_input(mb):
        sum_arrived(3, mb)

        def body(at, mine):
            dn = summed(3, at, mine)
            values = xa[mine, :].astype(F32)
            scale = rms(values)
            weighted = dn * gains[0:1, :]
            mean_term = jnp.mean(weighted * values, axis=-1, keepdims=True)
            grad = dmid[at, :] + scale * weighted - values * (scale * scale * scale) * mean_term
            ggain[0:1, :] += jnp.sum(dn * values * scale, axis=0, keepdims=True)
            gx_ref[at, :] = grad
            g0[at, :] = grad.astype(BF16)

        own_blocks(mb, body)

        @pl.when(section == 1)
        def _():
            core_g[mb].start()

    stores = [
        pltpu.make_async_copy(src, dst, store.at[n])
        for n, (src, dst) in enumerate(((win, gin_h), (wout, gout_h), (wg, gg_h), (wu, gu_h), (wd, gd_h)))
    ]

    def grad(n, width, left, right):
        target = (win, wout, wg, wu, wd)[n]

        def body(j):
            at = cols(j, width)
            target[at, :] = dot_tn(left[:, at], right[...]).astype(BF16)

        loop(target.shape[0] // width, body)
        stores[n].start()

    def grad_taps():
        for k in range(3):
            total = jnp.zeros((1, 384), F32)
            for mb in range(2):
                for zc in range(4):
                    t0 = 8 + 64 * zc - k
                    products = dce[mb, 64 * zc : 64 * zc + 64, :] * ge[mb, t0 : t0 + 64, :]
                    total = total + jnp.sum(products, axis=0, keepdims=True)
            gtap[k : k + 1, :] = total

    both(take_gradient)
    both(lambda mb: (back_hidden(mb), back_ffn(mb)))
    for copy in sent:
        if not any(copy is z_copies[n, r] for n in (1, 3, 4) for r in ORDER):
            copy.wait_send()
    back_middle(0)
    grad(2, 768, n2, dg)
    back_middle(1)
    grad(3, 768, n2, du)
    both(back_mix)
    both(lambda mb: (back_conv(mb), back_in(mb)))
    grad(1, 384, mx, fa)
    grad_taps()
    for mb in range(2):
        back_input(mb)
        pl.when(section == 1)(functools.partial(down, mb))
    grad(4, 896, hd, ea)
    grad(0, 768, xn, dp)

    @pl.when(section == 1)
    def _():
        both(finish)

    gs_ref[...] = jnp.zeros((256, 128), F32)
    for q in range(8):
        at = pl.ds(pl.multiple_of(q * 32 + z * 8, 8), 8)
        gs_ref[at, 0:48] = gtap[:, 48 * q : 48 * q + 48]
    for f in range(32):
        gs_ref[8 * f + 3 : 8 * f + 5, 0:48] = ggain[0:2, 48 * f : 48 * f + 48]

    for mb in range(2):

        @pl.when(section == 1)
        def _():
            core_g[mb].wait_send()

        @pl.when(section == 0)
        def _():
            core_x[mb].wait_send()

        @pl.when(has_after)
        def _():
            halo_after[mb].wait_send()

        @pl.when(has_before)
        def _():
            halo_before[mb].wait_send()

        sent_before(mb, 3, 1)
        for copies in (x_all, n_all, e_all, f_all):
            for copy in copies[mb]:
                copy.wait_send()
    for copy in stores:
        copy.wait()


def cut_conv(weight, out):
    for q in range(8):
        for zz in range(4):
            for part in range(3):
                first, to = part * 1536 + (4 * q + zz) * 48, part * 384 + q * 48
                out[zz * 48 : zz * 48 + 48, to : to + 48] = weight[:, first : first + 48]


def cut_ffn(weight, out):
    for zz in range(4):
        for q in range(8):
            first = (4 * q + zz) * 216
            out[zz * 48 : zz * 48 + 48, 224 * q : 224 * q + 216] = weight[:, first : first + 216]
            out[zz * 48 : zz * 48 + 48, 224 * q + 216 : 224 * q + 224] = jnp.zeros((48, 8), BF16)


def run_blocks(x, cot, small, w_in, w_out, w_gate, w_up, w_down):
    shape = jax.ShapeDtypeStruct
    dma = pltpu.SemaphoreType.DMA
    vm = pltpu.VMEM
    count = len(GATHER_UNITS)
    return pl.pallas_call(
        blocks_kernel,
        out_shape=(
            shape((128, 1536), BF16),
            shape((128, 1536), F32),
            shape((1536, 1152), BF16),
            shape((384, 1536), BF16),
            shape((1536, 1792), BF16),
            shape((1536, 1792), BF16),
            shape((1792, 1536), BF16),
            shape((256, 128), F32),
        ),
        in_specs=[VMEM] * 8,
        out_specs=[VMEM] * 2 + [ANY] * 5 + [VMEM],
        scratch_shapes=[
            vm((512, 1536), BF16), vm((512, 1536), BF16), vm((512, 1536), BF16), vm((512, 1536), BF16),
            vm((512, 1536), BF16), vm((512, 1536), BF16), vm((4, 3, 128, 1536), BF16),
            vm((3, 512, 384), F32), vm((2, 264, 384), F32), vm((2, 264, 384), F32), vm((512, 384), F32),
            vm((2, 8, 384), F32), vm((2, 8, 384), F32), vm((512, 384), BF16),
            vm((512, 1792), F32), vm((512, 1792), F32), vm((512, 1792), BF16), vm((512, 1792), BF16),
            vm((512, 1792), BF16), vm((128, 1536), F32), vm((128, 1536), F32), vm((512, 1152), BF16),
            vm((128, 1536), BF16),
            vm((1536, 1152), BF16), vm((384, 1536), BF16), vm((1536, 1792), BF16), vm((1536, 1792), BF16),
            vm((1792, 1536), BF16), vm((256, 128), F32), vm((8, 1536), F32), vm((8, 384), F32), vm((8, 384), F32),
            vm((2, 1536), F32),
            dma((5,)), dma((4, 2, 3)), dma((4, 2, 3)), dma((4, 2, 3, 3)), dma((4, 2, 3, 3)),
            dma((2, 2)), dma((2, 2)), dma((2, 2)), dma((2, 2)),
            dma((5, 3)), dma((5, 3)), dma((count, 3)), dma((count, 3)), dma((count, 4)), dma((count, 4)),
            dma((count, 4)), dma((count, 4)), pltpu.SemaphoreType.REGULAR,
        ],
        compiler_params=pltpu.CompilerParams(
            collective_id=1, has_side_effects=True, vmem_limit_bytes=63 * 2**20
        ),
        name="two_blocks",
    )(x, cot, small, w_in, w_out, w_gate, w_up, w_down)


def unit_shape(u):
    n, first, size, mode = REDUCE_UNITS[u]
    if n == 0:
        return (size, 1536), (size, 768)
    if n == 3:
        return (48, 1536), (48, 768)
    height = 8 if n == 5 else 48
    return (4, height, size), (2, height, size)


def unit_buffers(u):
    n, first, size, mode = REDUCE_UNITS[u]
    whole, part = unit_shape(u)
    dtype = F32 if n == 5 else BF16
    shapes = {
        0: ((4, *part), (4, *part), (2, *part), (2, *whole)),
        1: (None, (4, *whole), (2, *part), (2, *whole)),
        2: (None, whole, (2, 2, *part), (2, 2, *whole)),
    }[mode]
    shapes += (whole, whole if n in (1, 2, 4, 5) else None)
    return [None if shape is None else pltpu.VMEM(shape, dtype) for shape in shapes]


def reduce_kernel(
    g_d, g_g, g_u, g_o, g_in, g_s,
    o_d, o_g, o_u, o_o, o_in, o_s,
    v_d, v_g, v_u, v_o, v_in, v_s, l_d, l_g, l_u, l_in, l_s,
    load, q_send, q_recv, p_send, p_recv, y_send, y_recv, t_send, t_recv, z_send, z_recv,
    *buffers,
):
    section, xl, xh, y, z = place()
    partner, twin, zs, ys = plane_peers()
    held = (v_d, v_g, v_u, v_o, v_in, v_s)
    landing = (l_d, l_g, l_u, o_o, l_in, l_s)
    loads = [pltpu.make_async_copy(src, held[n], load.at[n]) for n, src in enumerate((g_d, g_g, g_u, g_o, g_in, g_s))]
    first_use = list(dict.fromkeys(unit[0] for unit in REDUCE_UNITS))
    for n in first_use[:2]:
        loads[n].start()
    barrier_all([partner, twin, *zs.values(), *ys.values()])
    count = len(REDUCE_UNITS)
    left = list(buffers)
    slots = [[None if shape is None else left.pop(0) for shape in unit_buffers(u)] for u in range(count)]
    from_twin, from_partner, halves_y, from_y, theirs, ended = zip(*slots)
    near, far = xh, 1 - xh
    sent, copies = [], {}

    def begin(key, copy):
        copy.start()
        copies[key] = copy
        sent.append(copy)

    def tail(u, h=None):
        n, first, size, mode = REDUCE_UNITS[u]
        across = slice(None) if h is None else pl.ds(pl.multiple_of(h * 768, 128), 768)
        if n == 0:
            return pl.ds(first, size), across
        if n == 3:
            return slice(None), across
        return slice(None) if h is None else pl.ds(h * 2, 2), slice(None), pl.ds(first, size)

    def blocks(u, h=None):
        n, first, size, mode = REDUCE_UNITS[u]
        if n in (0, 3):
            across = slice(None) if h is None else pl.ds(pl.multiple_of(h * 768, 128), 768)
            start = first if n == 0 else 0

            def at(i):
                return (pl.ds(pl.multiple_of(start + i * 16, 16), 16), across), (
                    pl.ds(pl.multiple_of(i * 16, 16), 16),
                    slice(None),
                )

            return (size if n == 0 else 48) // 16, at
        shift = 0 if h is None else h * 2
        return 4 if h is None else 2, lambda i: ((shift + i, slice(None), slice(first, first + size)), (i,))

    def add_rows(u, side, h, other):
        ref = held[REDUCE_UNITS[u][0]]
        number, at = blocks(u, h)

        def body(k):
            row = k // number
            here, there = at(lax.rem(k, number))
            ref[side, row, *here] = ref[side, row, *here] + other[row, *there]

        loop(4 * number, body)

    def sides(u):
        return (0, 1) if REDUCE_UNITS[u][3] == 2 else (near,)

    def lead(u, row):
        return (slice(None) if REDUCE_UNITS[u][3] == 2 else near, row)

    def of_side(u, k, side):
        return (k, side) if REDUCE_UNITS[u][3] == 2 else (k,)

    def send_halves(u):
        ref = held[REDUCE_UNITS[u][0]]
        for k, r in enumerate((1, 3)):
            src = ref.at[*lead(u, lax.rem(y + 2, 4)), *tail(u, k)]
            begin(("half", u, k), remote(src, halves_y[u].at[k], y_send.at[u, k], y_recv.at[u, k], ys[r]))

    def send_wholes(u):
        ref = held[REDUCE_UNITS[u][0]]
        for k, r in enumerate((1, 3)):
            row = lax.rem(y + r, 4)
            copies["half", u, k].wait_recv()
            number, at = blocks(u, k)
            for side in sides(u):

                def body(i):
                    here, there = at(i)
                    got = halves_y[u][*of_side(u, k, side), *there]
                    ref[side, row, *here] = ref[side, row, *here] + got

                loop(number, body)
            src = ref.at[*lead(u, row), *tail(u)]
            begin(("y", u, k), remote(src, from_y[u].at[k], y_send.at[u, 2 + k], y_recv.at[u, 2 + k], ys[r]))

    def send_p(u, src):
        begin(("p", u), remote(src, from_partner[u], p_send.at[u], p_recv.at[u], partner))

    def send_twin(u):
        src = held[REDUCE_UNITS[u][0]].at[near, y, *tail(u)]
        begin(("t", u), remote(src, theirs[u], t_send.at[u], t_recv.at[u], twin))

    def sum_y(u):
        for k in range(2):
            copies["y", u, k].wait_recv()
        ref = held[REDUCE_UNITS[u][0]]
        number, at = blocks(u)
        for side in sides(u):

            def body(i):
                here, there = at(i)
                total = ref[side, y, *here].astype(F32)
                for k in range(2):
                    total = total + from_y[u][*of_side(u, k, side), *there].astype(F32)
                ref[side, y, *here] = total.astype(ref.dtype)

            loop(number, body)

    ready = set()

    def stage_0(u):
        n, first, size, mode = REDUCE_UNITS[u]
        if n not in ready:
            ready.add(n)
            loads[n].wait()
            for following in first_use[len(ready) + 1 : len(ready) + 2]:
                loads[following].start()
        if mode == 0:
            src = held[n].at[far, :, *tail(u, 1 - xl)]
            begin(("q", u), remote(src, from_twin[u], q_send.at[u], q_recv.at[u], twin))
        elif mode == 1:
            send_p(u, held[n].at[far, :, *tail(u)])
        else:
            send_halves(u)

    def stage_1(u):
        n, first, size, mode = REDUCE_UNITS[u]
        if mode == 0:
            copies["q", u].wait_recv()
            add_rows(u, far, xl, from_twin[u])
            send_p(u, held[n].at[far, :, *tail(u, xl)])
        elif mode == 2:
            send_wholes(u)

    def stage_2(u):
        n, first, size, mode = REDUCE_UNITS[u]
        if mode == 2:
            sum_y(u)
            send_p(u, held[n].at[far, y, *tail(u)])
        else:
            copies["p", u].wait_recv()
            add_rows(u, near, 1 - xl if mode == 0 else None, from_partner[u])
            send_halves(u)

    def stage_3(u):
        n, first, size, mode = REDUCE_UNITS[u]
        if mode == 2:
            copies["p", u].wait_recv()
            number, at = blocks(u)

            def body(i):
                here, there = at(i)
                held[n][near, y, *here] = held[n][near, y, *here] + from_partner[u][there]

            loop(number, body)
            send_twin(u)
        else:
            send_wholes(u)

    def stage_4(u):
        if REDUCE_UNITS[u][3] != 2:
            sum_y(u)
            send_twin(u)

    def stage_5(u):
        n, first, size, mode = REDUCE_UNITS[u]
        copies["t", u].wait_recv()
        number, at = blocks(u)

        def body(i):
            here, there = at(i)
            if n in (0, 3):
                landing[n][here] = held[n][near, y, *here].astype(F32) + theirs[u][there].astype(F32)
            else:
                ended[u][there] = held[n][near, y, *here] + theirs[u][there]

        loop(number, body)
        if n not in (0, 3):
            part = (slice(None), pl.ds(first, size))
            for r in ORDER:
                src, dst = ended[u].at[lax.rem(z + r, 4)], landing[n].at[z, *part]
                begin(("z", u, r), remote(src, dst, z_send.at[u, r - 1], z_recv.at[u, r - 1], zs[r]))
            landing[n][z, :, first : first + size] = ended[u][z]

    stages = (stage_0, stage_1, stage_2, stage_3, stage_4, stage_5)
    for step in range(count + REDUCE_LAGS[-1]):
        for lag, stage in zip(REDUCE_LAGS, stages):
            if 0 <= step - lag < count:
                stage(step - lag)

    def landed(n):
        for u in range(count):
            if REDUCE_UNITS[u][0] == n:
                for r in ORDER:
                    copies["z", u, r].wait_recv()

    o_d[...] = l_d[0:216, :]
    for n, out in ((1, o_g), (2, o_u)):
        landed(n)
        for zz in range(4):
            for q in range(8):
                first = (4 * q + zz) * 216
                out[:, first : first + 216] = landing[n][zz, :, 224 * q : 224 * q + 216].astype(F32)
    landed(4)
    for zz in range(4):
        for q in range(8):
            for part in range(3):
                first, at = part * 1536 + (4 * q + zz) * 48, part * 384 + q * 48
                o_in[:, first : first + 48] = l_in[zz, :, at : at + 48].astype(F32)
    landed(5)
    o_s[...] = l_s[0] + l_s[1] + l_s[2] + l_s[3]
    for copy in sent:
        copy.wait_send()


def reduce(g_d, g_g, g_u, g_o, g_in, g_s):
    shape = jax.ShapeDtypeStruct
    dma = pltpu.SemaphoreType.DMA
    vm = pltpu.VMEM
    count = len(REDUCE_UNITS)
    return pl.pallas_call(
        reduce_kernel,
        out_shape=(
            shape((216, 1536), F32),
            shape((48, 6912), F32),
            shape((48, 6912), F32),
            shape((48, 1536), F32),
            shape((48, 4608), F32),
            shape((8, 128), F32),
        ),
        in_specs=[ANY] * 6,
        out_specs=[VMEM] * 6,
        scratch_shapes=[
            vm((2, 4, 224, 1536), BF16), vm((2, 4, 4, 48, 1792), BF16), vm((2, 4, 4, 48, 1792), BF16),
            vm((2, 4, 48, 1536), BF16), vm((2, 4, 4, 48, 1152), BF16), vm((2, 4, 4, 8, 128), F32),
            vm((224, 1536), F32), vm((4, 48, 1792), BF16), vm((4, 48, 1792), BF16), vm((4, 48, 1152), BF16),
            vm((4, 8, 128), F32),
            dma((6,)), dma((count,)), dma((count,)), dma((count,)), dma((count,)), dma((count, 4)), dma((count, 4)),
            dma((count,)), dma((count,)), dma((count, 3)), dma((count, 3)),
            *(buffer for u in range(count) for buffer in unit_buffers(u) if buffer is not None),
        ],
        compiler_params=pltpu.CompilerParams(
            collective_id=2, has_side_effects=True, vmem_limit_bytes=63 * 2**20
        ),
        name="reduce_grads",
    )(
        g_d.reshape(2, 4, 224, 1536),
        g_g.reshape(2, 4, 4, 48, 1792),
        g_u.reshape(2, 4, 4, 48, 1792),
        g_o.reshape(2, 4, 48, 1536),
        g_in.reshape(2, 4, 4, 48, 1152),
        g_s.reshape(2, 4, 4, 8, 128),
    )


def local(inputs, cotangent, w_in, w_out, w_gate, w_up, w_down, kernel, gain_mix, gain_ffn):
    small = jnp.concatenate([kernel[0], gain_mix, gain_ffn], axis=0).astype(F32)
    small = jnp.pad(small, ((0, 3), (0, 80)))
    y, gx, g_in, g_o, g_g, g_u, g_d, g_s = run_blocks(
        inputs.reshape(128, 1536), cotangent.reshape(128, 1536), small, w_in[0], w_out[0], w_gate[0], w_up[0], w_down[0]
    )
    o_d, o_g, o_u, o_o, o_in, o_s = reduce(g_d, g_g, g_u, g_o, g_in, g_s)
    return (
        y.reshape(1, 2, 64, 1536),
        gx.reshape(1, 2, 64, 1536),
        o_in[None],
        o_o[None],
        o_g[None],
        o_u[None],
        o_d[None],
        o_s[None, 0:3, :48],
        o_s[3:4, :48],
        o_s[4:5, :48],
    )


def solution(mesh):
    names = ("section", "xl", "xh", "y", "z")
    fine = Mesh(mesh.devices.reshape(2, 2, 2, 4, 4), names)
    tokens, shard = ("xl", "xh", "y", "z"), ("xh", "y", "z")
    weight = P("section", shard, None)
    acts = P("section", None, tokens, None)
    return jax.shard_map(
        local,
        mesh=fine,
        in_specs=(
            P(None, tokens, None),
            P(None, tokens, None),
            weight,
            weight,
            weight,
            weight,
            weight,
            P("section", None, shard),
            P("section", shard),
            P("section", shard),
        ),
        out_specs=(
            acts,
            acts,
            weight,
            weight,
            weight,
            weight,
            weight,
            P("section", None, shard),
            P("section", shard),
            P("section", shard),
        ),
        check_vma=False,
    )
```

```python
import functools

import jax
import jax.numpy as jnp
from jax import lax
from jax.experimental import pallas as pl
from jax.experimental.pallas import tpu as pltpu
from jax.sharding import Mesh
from jax.sharding import PartitionSpec as P

F32, BF16 = jnp.float32, jnp.bfloat16
MESH = pl.DeviceIdType.MESH
EPS = 1e-06
ANY = pl.BlockSpec(memory_space=pl.ANY)
VMEM = pl.BlockSpec(memory_space=pltpu.VMEM)
ORDER = (1, 3, 2)

GATHER_UNITS = (
    (0, 0, 128, 0),
    (5, 0, 64, 0),
    (5, 64, 32, 0),
    (1, 0, 1152, 0),
    (2, 0, 1536, 1),
    (3, 0, 640, 0),
    (4, 0, 384, 0),
    (4, 384, 512, 0),
    (4, 896, 768, 0),
    (4, 1664, 128, 0),
    (3, 640, 1152, 0),
    (5, 96, 128, 1),
)
GATHER_LAGS = (1, 2, 4)
FORWARD_AT = ((13, 14, 14, 15, 15, 15, 15, 15), (11, 12, 12, 14, 14, 15, 15, 15))
GO_AFTER = 11
REDUCE_UNITS = (
    (1, 0, 768, 1),
    (1, 768, 256, 2),
    (4, 0, 1024, 0),
    (2, 0, 1024, 2),
    (0, 0, 16, 2),
    (1, 1024, 128, 1),
    (2, 1024, 512, 0),
    (1, 1152, 256, 2),
    (0, 16, 48, 0),
    (4, 1024, 128, 0),
    (5, 0, 128, 2),
    (0, 64, 80, 0),
    (0, 144, 16, 2),
    (1, 1408, 384, 2),
    (2, 1536, 256, 2),
    (0, 160, 64, 0),
    (3, 0, 1536, 0),
)
REDUCE_LAGS = (0, 11, 16, 20, 24, 29)


def place():
    return tuple(lax.axis_index(name) for name in ("section", "xl", "xh", "y", "z"))


def barrier_all(devices):
    barrier = pltpu.get_barrier_semaphore()
    for device in devices:
        pl.semaphore_signal(barrier, inc=1, device_id=device, device_id_type=MESH)
    pl.semaphore_wait(barrier, len(devices))


def remote(src, dst, send, recv, device):
    return pltpu.make_async_remote_copy(
        src_ref=src, dst_ref=dst, send_sem=send, recv_sem=recv, device_id=device, device_id_type=MESH
    )


def plane_peers():
    section, xl, xh, y, z = place()
    partner = {"xh": 1 - xh, "xl": 1 - xl}
    twin = {"xl": 1 - xl}
    zs = {r: {"z": lax.rem(z + r, 4)} for r in ORDER}
    ys = {r: {"y": lax.rem(y + r, 4)} for r in ORDER}
    return partner, twin, zs, ys


def dot_nn(a, b):
    return lax.dot_general(a, b, (((1,), (0,)), ((), ())), preferred_element_type=F32)


def dot_nt(a, b):
    return lax.dot_general(a, b, (((1,), (1,)), ((), ())), preferred_element_type=F32)


def dot_tn(a, b):
    return lax.dot_general(a, b, (((0,), (0,)), ((), ())), preferred_element_type=F32)


def cols(j, width):
    return pl.ds(pl.multiple_of(j * width, width), width)


def loop(count, body):
    def step(j, carry):
        body(j)
        return carry

    lax.fori_loop(0, count, step, 0)


def blocks_kernel(
    x_ref, cot_ref, small, w_in, w_out, w_gate, w_up, w_down,
    y_ref, gx_ref, gin_h, gout_h, gg_h, gu_h, gd_h, gs_ref,
    xa, xn, n2, ea, fa, part, rr, proj, ge, dce, cv, ha, hb, mx, by_gate, by_up, hd, dg, du,
    mid, dmid, dp, g0, win, wout, wg, wu, wd, sm, gains, taps, gtap, ggain,
    store, a_send, a_recv, s_send, s_recv, h_send, h_recv, c_send, c_recv,
    z_send, z_recv, y_send, y_recv, f_send, f_recv, p_send, p_recv, q_send, q_recv, go,
):
    section, xl, xh, y, z = place()
    partner, twin, zs, ys = plane_peers()
    core = {"section": 1 - section}
    group = xl * 8 + xh * 4 + y
    after, before = lax.rem(group + 1, 16), lax.rem(group + 15, 16)
    has_after, has_before = group < 15, group > 0

    def at_group(g):
        return {"xl": g // 8, "xh": lax.rem(g // 4, 2), "y": lax.rem(g, 4)}

    barrier = pltpu.get_barrier_semaphore()

    def hail(device):
        pl.semaphore_signal(barrier, inc=1, device_id=device, device_id_type=MESH)

    for device in (partner, twin, core, *zs.values(), *ys.values()):
        hail(device)

    @pl.when(has_after)
    def _():
        hail(at_group(after))

    @pl.when(has_before)
    def _():
        hail(at_group(before))

    me = xh * 4 + y
    weights = (sm, win, wout, wg, wu, wd)
    cut = (None, dp, None, hd, dg, None)
    rows = (32, 192, 48, 192, 192, 224)
    cut_conv(w_in, dp)
    wout[pl.ds(pl.multiple_of(me * 48, 16), 48), :] = w_out[...]
    first_d = pl.multiple_of(me * 224, 16)
    wd[pl.ds(first_d, 224), :] = jnp.concatenate([w_down[...], jnp.zeros((8, 1536), BF16)], axis=0)
    pl.semaphore_wait(barrier, 10 - (group + 1) // 16 + (group + 15) // 16)

    def of_z(n, ref, first, zz):
        size = rows[n] // 4
        return ref.at[pl.ds(pl.multiple_of(first + zz * size, 8 if n == 0 else 16), size)]

    def rows_q(n, q):
        return pl.multiple_of(q * rows[n], 8 if n == 0 else 16)

    sent, z_copies = [], {}

    def push_z(n):
        size = rows[n] // 4
        for r in ORDER:
            src = small if n == 0 else of_z(n, cut[n], 0, lax.rem(z + r, 4))
            dst = of_z(n, weights[n], me * rows[n], z)
            copy = remote(src, dst, z_send.at[n, r - 1], z_recv.at[n, r - 1], zs[r])
            copy.start()
            z_copies[n, r] = copy
            sent.append(copy)
        mine = pl.ds(pl.multiple_of(me * rows[n] + z * size, 8 if n == 0 else 16), size)
        if n == 0:
            sm[mine, :] = small[...]
        else:
            weights[n][mine, :] = cut[n][pl.ds(pl.multiple_of(z * size, 16), size), 0 : weights[n].shape[1]]

    @pl.when(section == 1)
    def _():
        pl.semaphore_wait(go, 1)

    def own_rows(mb):
        return pl.ds(pl.multiple_of(mb * 256 + z * 64, 64), 64)

    def spread(n, buf, mb):
        at = buf.at[own_rows(mb)]
        return [remote(at, at, a_send.at[n, mb, r - 1], a_recv.at[n, mb, r - 1], zs[r]) for r in ORDER]

    x_all, n_all, e_all, f_all = ([spread(n, buf, mb) for mb in range(2)] for n, buf in enumerate((xa, n2, ea, fa)))

    def begin(copies):
        for copy in copies:
            copy.start()

    def arrived(copies):
        for copy in copies:
            copy.wait_recv()

    mb_rows = [slice(0, 256), slice(256, 512)]
    core_x, core_g = [], []
    for mb in range(2):
        at = pl.ds(mb * 64, 64)
        core_x.append(remote(y_ref.at[at], xa.at[own_rows(mb)], c_send.at[0, mb], c_recv.at[0, mb], core))
        core_g.append(remote(g0.at[at], ea.at[own_rows(mb)], c_send.at[1, mb], c_recv.at[1, mb], core))

    push_z(0)
    push_z(1)

    @pl.when(section == 0)
    def _():
        for mb in range(2):
            xa[own_rows(mb), :] = x_ref[mb * 64 : mb * 64 + 64, :]
            begin(x_all[mb])

    @pl.when(section == 1)
    def _():
        for mb in range(2):
            ea[own_rows(mb), :] = cot_ref[mb * 64 : mb * 64 + 64, :]
            begin(e_all[mb])

    cut_ffn(w_gate, hd)
    push_z(3)
    cut_ffn(w_up, dg)
    push_z(4)

    def piece(u, q):
        n, first, size, way = GATHER_UNITS[u]
        if n == 5:
            return wd.at[pl.ds(pl.multiple_of(q * 224 + first, 16), size)]
        if n == 2:
            return wout.at[pl.ds(rows_q(2, q), 48)]
        return weights[n].at[pl.ds(rows_q(n, q), rows[n]), pl.ds(first, size)]

    def half(u, q, h):
        n, first, size, way = GATHER_UNITS[u]
        if n in (2, 5):
            left = pl.ds(pl.multiple_of(h * 768, 128), 768)
            if n == 5:
                return wd.at[pl.ds(pl.multiple_of(q * 224 + first, 16), size), left]
            return wout.at[pl.ds(rows_q(2, q), 48), left]
        part_rows = rows[n] // 2
        return weights[n].at[
            pl.ds(pl.multiple_of(q * rows[n] + h * part_rows, 8 if n == 0 else 16), part_rows), pl.ds(first, size)
        ]

    y_copies, f_copies, p_copies, q_copies, started = {}, {}, {}, {}, set()

    def go_on(table, key, copy):
        copy.start()
        table[key] = copy
        sent.append(copy)

    def push_y(u, far):
        src = piece(u, (1 - xh if far else xh) * 4 + y)
        for k, r in enumerate((1, 3)):
            at = 2 * far + k
            go_on(y_copies, (u, at), remote(src, src, y_send.at[u, at], y_recv.at[u, at], ys[r]))

    def pass_y(u, far):
        for k, r in enumerate((1, 3)):
            at = 2 * far + k
            y_copies[u, at].wait_recv()
            src = half(u, (1 - xh if far else xh) * 4 + lax.rem(y + 4 - r, 4), k)
            go_on(f_copies, (u, at), remote(src, src, f_send.at[u, at], f_recv.at[u, at], ys[r]))
            if GATHER_UNITS[u][3] == 0:
                push_p(u, r)

    def push_p(u, r):
        src = half(u, xh * 4 + lax.rem(y + 4 - r, 4), xl)
        go_on(p_copies, (u, r), remote(src, src, p_send.at[u, r], p_recv.at[u, r], partner))

    def pass_q(u, r):
        p_copies[u, r].wait_recv()
        src = half(u, (1 - xh) * 4 + lax.rem(y + 4 - r, 4), 1 - xl)
        go_on(q_copies, (u, r), remote(src, src, q_send.at[u, r], q_recv.at[u, r], twin))

    def stage_y(u):
        n = GATHER_UNITS[u][0]
        if n not in started:
            started.add(n)
            if n not in (2, 5):
                for r in ORDER:
                    z_copies[n, r].wait_recv()
        push_p(u, 0)
        push_y(u, 0)

    def stage_p(u):
        if GATHER_UNITS[u][3]:
            pass_q(u, 0)
        pass_y(u, 0)

    def stage_f(u):
        if GATHER_UNITS[u][3]:
            q_copies[u, 0].wait_recv()
            push_y(u, 1)
        else:
            for k in range(2):
                f_copies[u, k].wait_recv()
            push_p(u, 2)

    def stage_q(u):
        if GATHER_UNITS[u][3]:
            pass_y(u, 1)
        else:
            for r in (0, *ORDER):
                pass_q(u, r)

    def need(n):
        for u, unit in enumerate(GATHER_UNITS):
            if unit[0] == n and unit[3]:
                for at in range(4):
                    f_copies[u, at].wait_recv()
            elif unit[0] == n:
                for r in (0, *ORDER):
                    q_copies[u, r].wait_recv()

    def scatter(n, mb, j, r):
        at = cols(j, 512)
        src = part.at[pl.ds(pl.multiple_of(mb * 256 + lax.rem(z + r, 4) * 64, 64), 64), at]
        dst = rr.at[n, r - 1, pl.ds(mb * 64, 64), at]
        return remote(src, dst, s_send.at[n, mb, j, r - 1], s_recv.at[n, mb, j, r - 1], zs[r])

    def sum_over_z(n, mb, block):
        def body(j):
            part[mb_rows[mb], cols(j, 512)] = block(cols(j, 512)).astype(BF16)
            for r in ORDER:
                scatter(n, mb, j, r).start()

        loop(3, body)

    def sum_arrived(n, mb):
        def body(j):
            for r in ORDER:
                scatter(n, mb, j, r).wait_recv()

        loop(3, body)

    def sum_sent(n, mb):
        def body(j):
            for r in ORDER:
                scatter(n, mb, j, r).wait_send()

        loop(3, body)

    def summed(n, at, mine):
        total = part[mine, :].astype(F32)
        for r in range(3):
            total = total + rr[n, r, at, :].astype(F32)
        return total

    def own_blocks(mb, body):
        def step(i):
            at = pl.ds(pl.multiple_of(mb * 64 + i * 32, 32), 32)
            mine = pl.ds(pl.multiple_of(mb * 256 + z * 64 + i * 32, 32), 32)
            body(at, mine)

        loop(2, step)

    def rms(values):
        return lax.rsqrt(jnp.mean(values * values, axis=-1, keepdims=True) + EPS)

    def take_input():
        for f in range(32):
            gains[0:2, 48 * f : 48 * f + 48] = sm[8 * f + 3 : 8 * f + 5, 0:48]
        for q in range(8):
            taps[0:3, 48 * q : 48 * q + 48] = sm[pl.ds(pl.multiple_of(q * 32 + z * 8, 8), 8), :][0:3, 0:48]

    halo_after = [
        remote(ge.at[mb, pl.ds(256, 8)], ha.at[mb], h_send.at[0, mb], h_recv.at[0, mb], at_group(after)) for mb in range(2)
    ]
    halo_before = [
        remote(dce.at[mb, pl.ds(0, 8)], hb.at[mb], h_send.at[1, mb], h_recv.at[1, mb], at_group(before)) for mb in range(2)
    ]

    def project(mb):
        arrived(x_all[mb])

        def norm(i):
            at = pl.ds(pl.multiple_of(mb * 256 + i * 32, 32), 32)
            values = xa[at, :].astype(F32)
            xn[at, :] = (values * rms(values) * gains[0:1, :]).astype(BF16)

        loop(8, norm)

        def body(j):
            proj[j, mb_rows[mb], :] = dot_nn(xn[mb_rows[mb], :], win[:, cols(j, 384)])

        loop(3, body)
        ge[mb, 8:264, :] = proj[0, mb_rows[mb], :] * proj[2, mb_rows[mb], :]

        @pl.when(has_after)
        def _():
            halo_after[mb].start()

    def tap(k):
        return taps[k : k + 1, :]

    def mix(mb):
        @pl.when(has_before)
        def _():
            halo_after[mb].wait_recv()
            ge[mb, 0:8, :] = ha[mb]

        @pl.when(jnp.logical_not(has_before))
        def _():
            ge[mb, 0:8, :] = jnp.zeros((8, 384), F32)

        for zc in range(4):
            t0, at = 8 + 64 * zc, slice(mb * 256 + 64 * zc, mb * 256 + 64 * zc + 64)
            total = tap(0) * ge[mb, t0 : t0 + 64, :]
            for k in (1, 2):
                total = total + tap(k) * ge[mb, t0 - k : t0 - k + 64, :]
            cv[at, :] = total
            mx[at, :] = (proj[1, at, :] * total).astype(BF16)
        sum_over_z(0, mb, lambda at: dot_nn(mx[mb_rows[mb], :], wout[:, at]))

    def middle(mb):
        sum_arrived(0, mb)

        def body(at, mine):
            values = xa[mine, :].astype(F32) + summed(0, at, mine)
            mid[at, :] = values
            n2[mine, :] = (values * rms(values) * gains[1:2, :]).astype(BF16)

        own_blocks(mb, body)
        begin(n_all[mb])

    def gate(mb):
        arrived(n_all[mb])

        def body(j):
            at = cols(j, 896)
            gating = dot_nn(n2[mb_rows[mb], :], wg[:, at])
            up_part = dot_nn(n2[mb_rows[mb], :], wu[:, at])
            sg = jax.nn.sigmoid(gating)
            silu = gating * sg
            by_gate[mb_rows[mb], at] = up_part * sg * (1.0 + gating * (1.0 - sg))
            by_up[mb_rows[mb], at] = silu
            hd[mb_rows[mb], at] = (silu * up_part).astype(BF16)

        loop(2, body)

    def sent_before(mb, first, second):
        @pl.when(section == 0)
        def _():
            sum_sent(first, mb)

        @pl.when(section == 1)
        def _():
            sum_sent(second, mb)

    def down(mb):
        sent_before(mb, 0, 3)
        sum_over_z(1, mb, lambda at: dot_nn(hd[mb_rows[mb], :], wd[:, at]))

    def finish(mb):
        sum_arrived(1, mb)

        def body(at, mine):
            y_ref[at, :] = (mid[at, :] + summed(1, at, mine)).astype(BF16)

        own_blocks(mb, body)

        @pl.when(section == 0)
        def _():
            core_x[mb].start()

    def wait_x():
        @pl.when(section == 1)
        def _():
            for mb in range(2):
                core_x[mb].wait_recv()
                begin(x_all[mb])

    def free_cuts():
        for n in (1, 3, 4):
            for r in ORDER:
                z_copies[n, r].wait_send()

    def both(stage):
        stage(0)
        stage(1)

    def begin_forward():
        need(0)
        take_input()
        need(1)
        wait_x()
        project(0)

    def begin_mix():
        need(2)
        mix(0)

    def begin_gate():
        need(3)
        need(4)
        free_cuts()
        gate(0)

    segments = (
        begin_forward, lambda: project(1), begin_mix, lambda: mix(1),
        lambda: middle(0), lambda: middle(1), begin_gate, lambda: gate(1),
    )
    count = len(GATHER_UNITS)
    lag_p, lag_f, lag_q = GATHER_LAGS
    for step in range(count + lag_q):
        if step < count:
            stage_y(step)
        if 0 <= step - lag_p < count:
            stage_p(step - lag_p)
        if 0 <= step - lag_f < count:
            stage_f(step - lag_f)
        if step == GO_AFTER:

            @pl.when(section == 0)
            def _():
                pl.semaphore_signal(go, inc=1, device_id=core, device_id_type=MESH)

        if 0 <= step - lag_q < count:
            stage_q(step - lag_q)
        for turn, segment in enumerate(segments):
            if step == FORWARD_AT[0][turn]:
                pl.when(section == 0)(segment)
            if step == FORWARD_AT[1][turn]:
                pl.when(section == 1)(segment)

    need(5)

    @pl.when(section == 0)
    def _():
        both(down)
        both(finish)

    ggain[...] = jnp.zeros((2, 1536), F32)

    def take_gradient(mb):
        @pl.when(section == 0)
        def _():
            core_g[mb].wait_recv()
            begin(e_all[mb])

    def back_hidden(mb):
        arrived(e_all[mb])

        def body(j):
            at = cols(j, 896)
            dh = dot_nt(ea[mb_rows[mb], :], wd[at, :])
            dg[mb_rows[mb], at] = (dh * by_gate[mb_rows[mb], at]).astype(BF16)
            du[mb_rows[mb], at] = (dh * by_up[mb_rows[mb], at]).astype(BF16)

        loop(2, body)

    def back_ffn(mb):
        sent_before(mb, 1, 0)
        sum_over_z(2, mb, lambda at: dot_nt(dg[mb_rows[mb], :], wg[at, :]) + dot_nt(du[mb_rows[mb], :], wu[at, :]))

    def back_middle(mb):
        sum_arrived(2, mb)

        def body(at, mine):
            dn2 = summed(2, at, mine)
            values = mid[at, :]
            scale = rms(values)
            weighted = dn2 * gains[1:2, :]
            mean_term = jnp.mean(weighted * values, axis=-1, keepdims=True)
            grad = ea[mine, :].astype(F32) + scale * weighted - values * (scale * scale * scale) * mean_term
            ggain[1:2, :] += jnp.sum(dn2 * values * scale, axis=0, keepdims=True)
            dmid[at, :] = grad
            fa[mine, :] = grad.astype(BF16)

        own_blocks(mb, body)
        begin(f_all[mb])

    def back_mix(mb):
        arrived(f_all[mb])
        dce[mb, 0:256, :] = dot_nt(fa[mb_rows[mb], :], wout[...])
        for zc in range(4):
            at, here = slice(mb * 256 + 64 * zc, mb * 256 + 64 * zc + 64), slice(64 * zc, 64 * zc + 64)
            dm = dce[mb, here, :]
            dp[at, 384:768] = (dm * cv[at, :]).astype(BF16)
            dce[mb, here, :] = dm * proj[1, at, :]

        @pl.when(has_before)
        def _():
            halo_before[mb].start()

    def back_conv(mb):
        @pl.when(has_after)
        def _():
            halo_before[mb].wait_recv()
            dce[mb, 256:264, :] = hb[mb]

        @pl.when(jnp.logical_not(has_after))
        def _():
            dce[mb, 256:264, :] = jnp.zeros((8, 384), F32)

        for zc in range(4):
            at, t0 = slice(mb * 256 + 64 * zc, mb * 256 + 64 * zc + 64), 64 * zc
            total = tap(0) * dce[mb, t0 : t0 + 64, :]
            for k in (1, 2):
                total = total + tap(k) * dce[mb, t0 + k : t0 + k + 64, :]
            dp[at, 0:384] = (total * proj[2, at, :]).astype(BF16)
            dp[at, 768:1152] = (total * proj[0, at, :]).astype(BF16)

    def back_in(mb):
        sum_sent(2, mb)
        sum_over_z(3, mb, lambda at: dot_nt(dp[mb_rows[mb], :], win[at, :]))

    def back_input(mb):
        sum_arrived(3, mb)

        def body(at, mine):
            dn = summed(3, at, mine)
            values = xa[mine, :].astype(F32)
            scale = rms(values)
            weighted = dn * gains[0:1, :]
            mean_term = jnp.mean(weighted * values, axis=-1, keepdims=True)
            grad = dmid[at, :] + scale * weighted - values * (scale * scale * scale) * mean_term
            ggain[0:1, :] += jnp.sum(dn * values * scale, axis=0, keepdims=True)
            gx_ref[at, :] = grad
            g0[at, :] = grad.astype(BF16)

        own_blocks(mb, body)

        @pl.when(section == 1)
        def _():
            core_g[mb].start()

    stores = [
        pltpu.make_async_copy(src, dst, store.at[n])
        for n, (src, dst) in enumerate(((win, gin_h), (wout, gout_h), (wg, gg_h), (wu, gu_h), (wd, gd_h)))
    ]

    def grad(n, width, left, right):
        target = (win, wout, wg, wu, wd)[n]

        def body(j):
            at = cols(j, width)
            target[at, :] = dot_tn(left[:, at], right[...]).astype(BF16)

        loop(target.shape[0] // width, body)
        stores[n].start()

    def grad_taps():
        for k in range(3):
            total = jnp.zeros((1, 384), F32)
            for mb in range(2):
                for zc in range(4):
                    t0 = 8 + 64 * zc - k
                    products = dce[mb, 64 * zc : 64 * zc + 64, :] * ge[mb, t0 : t0 + 64, :]
                    total = total + jnp.sum(products, axis=0, keepdims=True)
            gtap[k : k + 1, :] = total

    both(take_gradient)
    both(lambda mb: (back_hidden(mb), back_ffn(mb)))
    for copy in sent:
        if not any(copy is z_copies[n, r] for n in (1, 3, 4) for r in ORDER):
            copy.wait_send()
    back_middle(0)
    grad(2, 768, n2, dg)
    back_middle(1)
    grad(3, 768, n2, du)
    both(back_mix)
    both(lambda mb: (back_conv(mb), back_in(mb)))
    grad(1, 384, mx, fa)
    grad_taps()
    for mb in range(2):
        back_input(mb)
        pl.when(section == 1)(functools.partial(down, mb))
    grad(4, 896, hd, ea)
    grad(0, 768, xn, dp)

    @pl.when(section == 1)
    def _():
        both(finish)

    gs_ref[...] = jnp.zeros((256, 128), F32)
    for q in range(8):
        at = pl.ds(pl.multiple_of(q * 32 + z * 8, 8), 8)
        gs_ref[at, 0:48] = gtap[:, 48 * q : 48 * q + 48]
    for f in range(32):
        gs_ref[8 * f + 3 : 8 * f + 5, 0:48] = ggain[0:2, 48 * f : 48 * f + 48]

    for mb in range(2):

        @pl.when(section == 1)
        def _():
            core_g[mb].wait_send()

        @pl.when(section == 0)
        def _():
            core_x[mb].wait_send()

        @pl.when(has_after)
        def _():
            halo_after[mb].wait_send()

        @pl.when(has_before)
        def _():
            halo_before[mb].wait_send()

        sent_before(mb, 3, 1)
        for copies in (x_all, n_all, e_all, f_all):
            for copy in copies[mb]:
                copy.wait_send()
    for copy in stores:
        copy.wait()


def cut_conv(weight, out):
    for q in range(8):
        for zz in range(4):
            for part in range(3):
                first, to = part * 1536 + (4 * q + zz) * 48, part * 384 + q * 48
                out[zz * 48 : zz * 48 + 48, to : to + 48] = weight[:, first : first + 48]


def cut_ffn(weight, out):
    for zz in range(4):
        for q in range(8):
            first = (4 * q + zz) * 216
            out[zz * 48 : zz * 48 + 48, 224 * q : 224 * q + 216] = weight[:, first : first + 216]
            out[zz * 48 : zz * 48 + 48, 224 * q + 216 : 224 * q + 224] = jnp.zeros((48, 8), BF16)


def run_blocks(x, cot, small, w_in, w_out, w_gate, w_up, w_down):
    shape = jax.ShapeDtypeStruct
    dma = pltpu.SemaphoreType.DMA
    vm = pltpu.VMEM
    count = len(GATHER_UNITS)
    return pl.pallas_call(
        blocks_kernel,
        out_shape=(
            shape((128, 1536), BF16),
            shape((128, 1536), F32),
            shape((1536, 1152), BF16),
            shape((384, 1536), BF16),
            shape((1536, 1792), BF16),
            shape((1536, 1792), BF16),
            shape((1792, 1536), BF16),
            shape((256, 128), F32),
        ),
        in_specs=[VMEM] * 8,
        out_specs=[VMEM] * 2 + [ANY] * 5 + [VMEM],
        scratch_shapes=[
            vm((512, 1536), BF16), vm((512, 1536), BF16), vm((512, 1536), BF16), vm((512, 1536), BF16),
            vm((512, 1536), BF16), vm((512, 1536), BF16), vm((4, 3, 128, 1536), BF16),
            vm((3, 512, 384), F32), vm((2, 264, 384), F32), vm((2, 264, 384), F32), vm((512, 384), F32),
            vm((2, 8, 384), F32), vm((2, 8, 384), F32), vm((512, 384), BF16),
            vm((512, 1792), F32), vm((512, 1792), F32), vm((512, 1792), BF16), vm((512, 1792), BF16),
            vm((512, 1792), BF16), vm((128, 1536), F32), vm((128, 1536), F32), vm((512, 1152), BF16),
            vm((128, 1536), BF16),
            vm((1536, 1152), BF16), vm((384, 1536), BF16), vm((1536, 1792), BF16), vm((1536, 1792), BF16),
            vm((1792, 1536), BF16), vm((256, 128), F32), vm((8, 1536), F32), vm((8, 384), F32), vm((8, 384), F32),
            vm((2, 1536), F32),
            dma((5,)), dma((4, 2, 3)), dma((4, 2, 3)), dma((4, 2, 3, 3)), dma((4, 2, 3, 3)),
            dma((2, 2)), dma((2, 2)), dma((2, 2)), dma((2, 2)),
            dma((5, 3)), dma((5, 3)), dma((count, 4)), dma((count, 4)), dma((count, 4)), dma((count, 4)),
            dma((count, 4)), dma((count, 4)), dma((count, 4)), dma((count, 4)), pltpu.SemaphoreType.REGULAR,
        ],
        compiler_params=pltpu.CompilerParams(
            collective_id=1, has_side_effects=True, vmem_limit_bytes=63 * 2**20
        ),
        name="two_blocks",
    )(x, cot, small, w_in, w_out, w_gate, w_up, w_down)


def unit_shape(u):
    n, first, size, mode = REDUCE_UNITS[u]
    if n == 0:
        return (size, 1536), (size, 768)
    if n == 3:
        return (48, 1536), (48, 768)
    height = 8 if n == 5 else 48
    return (4, height, size), (2, height, size)


def unit_buffers(u):
    n, first, size, mode = REDUCE_UNITS[u]
    whole, part = unit_shape(u)
    dtype = F32 if n == 5 else BF16
    shapes = {
        0: ((4, *part), (4, *part), (2, *part), (2, *whole)),
        1: (None, (4, *whole), (2, *part), (2, *whole)),
        2: (None, whole, (2, 2, *part), (2, 2, *whole)),
    }[mode]
    shapes += (whole, whole if n in (1, 2, 4, 5) else None)
    return [None if shape is None else pltpu.VMEM(shape, dtype) for shape in shapes]


def reduce_kernel(
    g_d, g_g, g_u, g_o, g_in, g_s,
    o_d, o_g, o_u, o_o, o_in, o_s,
    v_d, v_g, v_u, v_o, v_in, v_s, l_d, l_g, l_u, l_in, l_s,
    load, q_send, q_recv, p_send, p_recv, y_send, y_recv, t_send, t_recv, z_send, z_recv,
    *buffers,
):
    section, xl, xh, y, z = place()
    partner, twin, zs, ys = plane_peers()
    held = (v_d, v_g, v_u, v_o, v_in, v_s)
    landing = (l_d, l_g, l_u, o_o, l_in, l_s)
    loads = [pltpu.make_async_copy(src, held[n], load.at[n]) for n, src in enumerate((g_d, g_g, g_u, g_o, g_in, g_s))]
    first_use = list(dict.fromkeys(unit[0] for unit in REDUCE_UNITS))
    for n in first_use[:2]:
        loads[n].start()
    barrier_all([partner, twin, *zs.values(), *ys.values()])
    count = len(REDUCE_UNITS)
    left = list(buffers)
    slots = [[None if shape is None else left.pop(0) for shape in unit_buffers(u)] for u in range(count)]
    from_twin, from_partner, halves_y, from_y, theirs, ended = zip(*slots)
    near, far = xh, 1 - xh
    sent, copies = [], {}

    def begin(key, copy):
        copy.start()
        copies[key] = copy
        sent.append(copy)

    def tail(u, h=None):
        n, first, size, mode = REDUCE_UNITS[u]
        across = slice(None) if h is None else pl.ds(pl.multiple_of(h * 768, 128), 768)
        if n == 0:
            return pl.ds(first, size), across
        if n == 3:
            return slice(None), across
        return slice(None) if h is None else pl.ds(h * 2, 2), slice(None), pl.ds(first, size)

    def blocks(u, h=None):
        n, first, size, mode = REDUCE_UNITS[u]
        if n in (0, 3):
            across = slice(None) if h is None else pl.ds(pl.multiple_of(h * 768, 128), 768)
            start = first if n == 0 else 0

            def at(i):
                return (pl.ds(pl.multiple_of(start + i * 16, 16), 16), across), (
                    pl.ds(pl.multiple_of(i * 16, 16), 16),
                    slice(None),
                )

            return (size if n == 0 else 48) // 16, at
        shift = 0 if h is None else h * 2
        return 4 if h is None else 2, lambda i: ((shift + i, slice(None), slice(first, first + size)), (i,))

    def add_rows(u, side, h, other):
        ref = held[REDUCE_UNITS[u][0]]
        number, at = blocks(u, h)

        def body(k):
            row = k // number
            here, there = at(lax.rem(k, number))
            ref[side, row, *here] = ref[side, row, *here] + other[row, *there]

        loop(4 * number, body)

    def sides(u):
        return (0, 1) if REDUCE_UNITS[u][3] == 2 else (near,)

    def lead(u, row):
        return (slice(None) if REDUCE_UNITS[u][3] == 2 else near, row)

    def of_side(u, k, side):
        return (k, side) if REDUCE_UNITS[u][3] == 2 else (k,)

    def send_halves(u):
        ref = held[REDUCE_UNITS[u][0]]
        for k, r in enumerate((1, 3)):
            src = ref.at[*lead(u, lax.rem(y + 2, 4)), *tail(u, k)]
            begin(("half", u, k), remote(src, halves_y[u].at[k], y_send.at[u, k], y_recv.at[u, k], ys[r]))

    def send_wholes(u):
        ref = held[REDUCE_UNITS[u][0]]
        for k, r in enumerate((1, 3)):
            row = lax.rem(y + r, 4)
            copies["half", u, k].wait_recv()
            number, at = blocks(u, k)
            for side in sides(u):

                def body(i):
                    here, there = at(i)
                    got = halves_y[u][*of_side(u, k, side), *there]
                    ref[side, row, *here] = ref[side, row, *here] + got

                loop(number, body)
            src = ref.at[*lead(u, row), *tail(u)]
            begin(("y", u, k), remote(src, from_y[u].at[k], y_send.at[u, 2 + k], y_recv.at[u, 2 + k], ys[r]))

    def send_p(u, src):
        begin(("p", u), remote(src, from_partner[u], p_send.at[u], p_recv.at[u], partner))

    def send_twin(u):
        src = held[REDUCE_UNITS[u][0]].at[near, y, *tail(u)]
        begin(("t", u), remote(src, theirs[u], t_send.at[u], t_recv.at[u], twin))

    def sum_y(u):
        for k in range(2):
            copies["y", u, k].wait_recv()
        ref = held[REDUCE_UNITS[u][0]]
        number, at = blocks(u)
        for side in sides(u):

            def body(i):
                here, there = at(i)
                total = ref[side, y, *here].astype(F32)
                for k in range(2):
                    total = total + from_y[u][*of_side(u, k, side), *there].astype(F32)
                ref[side, y, *here] = total.astype(ref.dtype)

            loop(number, body)

    ready = set()

    def stage_0(u):
        n, first, size, mode = REDUCE_UNITS[u]
        if n not in ready:
            ready.add(n)
            loads[n].wait()
            for following in first_use[len(ready) + 1 : len(ready) + 2]:
                loads[following].start()
        if mode == 0:
            src = held[n].at[far, :, *tail(u, 1 - xl)]
            begin(("q", u), remote(src, from_twin[u], q_send.at[u], q_recv.at[u], twin))
        elif mode == 1:
            send_p(u, held[n].at[far, :, *tail(u)])
        else:
            send_halves(u)

    def stage_1(u):
        n, first, size, mode = REDUCE_UNITS[u]
        if mode == 0:
            copies["q", u].wait_recv()
            add_rows(u, far, xl, from_twin[u])
            send_p(u, held[n].at[far, :, *tail(u, xl)])
        elif mode == 2:
            send_wholes(u)

    def stage_2(u):
        n, first, size, mode = REDUCE_UNITS[u]
        if mode == 2:
            sum_y(u)
            send_p(u, held[n].at[far, y, *tail(u)])
        else:
            copies["p", u].wait_recv()
            add_rows(u, near, 1 - xl if mode == 0 else None, from_partner[u])
            send_halves(u)

    def stage_3(u):
        n, first, size, mode = REDUCE_UNITS[u]
        if mode == 2:
            copies["p", u].wait_recv()
            number, at = blocks(u)

            def body(i):
                here, there = at(i)
                held[n][near, y, *here] = held[n][near, y, *here] + from_partner[u][there]

            loop(number, body)
            send_twin(u)
        else:
            send_wholes(u)

    def stage_4(u):
        if REDUCE_UNITS[u][3] != 2:
            sum_y(u)
            send_twin(u)

    def stage_5(u):
        n, first, size, mode = REDUCE_UNITS[u]
        copies["t", u].wait_recv()
        number, at = blocks(u)

        def body(i):
            here, there = at(i)
            if n in (0, 3):
                landing[n][here] = held[n][near, y, *here].astype(F32) + theirs[u][there].astype(F32)
            else:
                ended[u][there] = held[n][near, y, *here] + theirs[u][there]

        loop(number, body)
        if n not in (0, 3):
            part = (slice(None), pl.ds(first, size))
            for r in ORDER:
                src, dst = ended[u].at[lax.rem(z + r, 4)], landing[n].at[z, *part]
                begin(("z", u, r), remote(src, dst, z_send.at[u, r - 1], z_recv.at[u, r - 1], zs[r]))
            landing[n][z, :, first : first + size] = ended[u][z]

    stages = (stage_0, stage_1, stage_2, stage_3, stage_4, stage_5)
    for step in range(count + REDUCE_LAGS[-1]):
        for lag, stage in zip(REDUCE_LAGS, stages):
            if 0 <= step - lag < count:
                stage(step - lag)

    def landed(n):
        for u in range(count):
            if REDUCE_UNITS[u][0] == n:
                for r in ORDER:
                    copies["z", u, r].wait_recv()

    o_d[...] = l_d[0:216, :]
    for n, out in ((1, o_g), (2, o_u)):
        landed(n)
        for zz in range(4):
            for q in range(8):
                first = (4 * q + zz) * 216
                out[:, first : first + 216] = landing[n][zz, :, 224 * q : 224 * q + 216].astype(F32)
    landed(4)
    for zz in range(4):
        for q in range(8):
            for part in range(3):
                first, at = part * 1536 + (4 * q + zz) * 48, part * 384 + q * 48
                o_in[:, first : first + 48] = l_in[zz, :, at : at + 48].astype(F32)
    landed(5)
    o_s[...] = l_s[0] + l_s[1] + l_s[2] + l_s[3]
    for copy in sent:
        copy.wait_send()


def reduce(g_d, g_g, g_u, g_o, g_in, g_s):
    shape = jax.ShapeDtypeStruct
    dma = pltpu.SemaphoreType.DMA
    vm = pltpu.VMEM
    count = len(REDUCE_UNITS)
    return pl.pallas_call(
        reduce_kernel,
        out_shape=(
            shape((216, 1536), F32),
            shape((48, 6912), F32),
            shape((48, 6912), F32),
            shape((48, 1536), F32),
            shape((48, 4608), F32),
            shape((8, 128), F32),
        ),
        in_specs=[ANY] * 6,
        out_specs=[VMEM] * 6,
        scratch_shapes=[
            vm((2, 4, 224, 1536), BF16), vm((2, 4, 4, 48, 1792), BF16), vm((2, 4, 4, 48, 1792), BF16),
            vm((2, 4, 48, 1536), BF16), vm((2, 4, 4, 48, 1152), BF16), vm((2, 4, 4, 8, 128), F32),
            vm((224, 1536), F32), vm((4, 48, 1792), BF16), vm((4, 48, 1792), BF16), vm((4, 48, 1152), BF16),
            vm((4, 8, 128), F32),
            dma((6,)), dma((count,)), dma((count,)), dma((count,)), dma((count,)), dma((count, 4)), dma((count, 4)),
            dma((count,)), dma((count,)), dma((count, 3)), dma((count, 3)),
            *(buffer for u in range(count) for buffer in unit_buffers(u) if buffer is not None),
        ],
        compiler_params=pltpu.CompilerParams(
            collective_id=2, has_side_effects=True, vmem_limit_bytes=63 * 2**20
        ),
        name="reduce_grads",
    )(
        g_d.reshape(2, 4, 224, 1536),
        g_g.reshape(2, 4, 4, 48, 1792),
        g_u.reshape(2, 4, 4, 48, 1792),
        g_o.reshape(2, 4, 48, 1536),
        g_in.reshape(2, 4, 4, 48, 1152),
        g_s.reshape(2, 4, 4, 8, 128),
    )


def local(inputs, cotangent, w_in, w_out, w_gate, w_up, w_down, kernel, gain_mix, gain_ffn):
    small = jnp.concatenate([kernel[0], gain_mix, gain_ffn], axis=0).astype(F32)
    small = jnp.pad(small, ((0, 3), (0, 80)))
    y, gx, g_in, g_o, g_g, g_u, g_d, g_s = run_blocks(
        inputs.reshape(128, 1536), cotangent.reshape(128, 1536), small, w_in[0], w_out[0], w_gate[0], w_up[0], w_down[0]
    )
    o_d, o_g, o_u, o_o, o_in, o_s = reduce(g_d, g_g, g_u, g_o, g_in, g_s)
    return (
        y.reshape(1, 2, 64, 1536),
        gx.reshape(1, 2, 64, 1536),
        o_in[None],
        o_o[None],
        o_g[None],
        o_u[None],
        o_d[None],
        o_s[None, 0:3, :48],
        o_s[3:4, :48],
        o_s[4:5, :48],
    )


def solution(mesh):
    names = ("section", "xl", "xh", "y", "z")
    fine = Mesh(mesh.devices.reshape(2, 2, 2, 4, 4), names)
    tokens, shard = ("xl", "xh", "y", "z"), ("xh", "y", "z")
    weight = P("section", shard, None)
    acts = P("section", None, tokens, None)
    return jax.shard_map(
        local,
        mesh=fine,
        in_specs=(
            P(None, tokens, None),
            P(None, tokens, None),
            weight,
            weight,
            weight,
            weight,
            weight,
            P("section", None, shard),
            P("section", shard),
            P("section", shard),
        ),
        out_specs=(
            acts,
            acts,
            weight,
            weight,
            weight,
            weight,
            weight,
            P("section", None, shard),
            P("section", shard),
            P("section", shard),
        ),
        check_vma=False,
    )
```

```python
import functools

import jax
import jax.numpy as jnp
from jax import lax
from jax.experimental import pallas as pl
from jax.experimental.pallas import tpu as pltpu
from jax.sharding import Mesh
from jax.sharding import PartitionSpec as P

F32, BF16 = jnp.float32, jnp.bfloat16
MESH = pl.DeviceIdType.MESH
EPS = 1e-06
ANY = pl.BlockSpec(memory_space=pl.ANY)
VMEM = pl.BlockSpec(memory_space=pltpu.VMEM)
ORDER = (1, 3, 2)

GATHER_UNITS = (
    (0, 0, 128, 0),
    (5, 0, 64, 0),
    (5, 64, 32, 0),
    (1, 0, 1152, 0),
    (2, 0, 1536, 1),
    (3, 0, 640, 0),
    (4, 0, 384, 0),
    (4, 384, 512, 0),
    (4, 896, 768, 0),
    (4, 1664, 128, 0),
    (3, 640, 1152, 0),
    (5, 96, 128, 1),
)
GATHER_LAGS = (1, 2, 4)
FORWARD_AT = ((13, 14, 14, 15, 15, 15, 15, 15), (11, 12, 12, 14, 14, 15, 15, 15))
GO_AFTER = 11
REDUCE_UNITS = (
    (1, 0, 768, 1),
    (1, 768, 256, 2),
    (4, 0, 1024, 0),
    (2, 0, 1024, 2),
    (0, 0, 16, 2),
    (1, 1024, 128, 1),
    (2, 1024, 512, 0),
    (1, 1152, 256, 2),
    (0, 16, 48, 0),
    (4, 1024, 128, 0),
    (5, 0, 128, 2),
    (0, 64, 80, 0),
    (0, 144, 16, 2),
    (1, 1408, 384, 2),
    (2, 1536, 256, 2),
    (0, 160, 64, 0),
    (3, 0, 1536, 0),
)
REDUCE_LAGS = (0, 11, 16, 20, 24, 29)


def place():
    return tuple(lax.axis_index(name) for name in ("section", "xl", "xh", "y", "z"))


def barrier_all(devices):
    barrier = pltpu.get_barrier_semaphore()
    for device in devices:
        pl.semaphore_signal(barrier, inc=1, device_id=device, device_id_type=MESH)
    pl.semaphore_wait(barrier, len(devices))


def remote(src, dst, send, recv, device):
    return pltpu.make_async_remote_copy(
        src_ref=src, dst_ref=dst, send_sem=send, recv_sem=recv, device_id=device, device_id_type=MESH
    )


def plane_peers():
    section, xl, xh, y, z = place()
    partner = {"xh": 1 - xh, "xl": 1 - xl}
    twin = {"xl": 1 - xl}
    zs = {r: {"z": lax.rem(z + r, 4)} for r in ORDER}
    ys = {r: {"y": lax.rem(y + r, 4)} for r in ORDER}
    return partner, twin, zs, ys


def dot_nn(a, b):
    return lax.dot_general(a, b, (((1,), (0,)), ((), ())), preferred_element_type=F32)


def dot_nt(a, b):
    return lax.dot_general(a, b, (((1,), (1,)), ((), ())), preferred_element_type=F32)


def dot_tn(a, b):
    return lax.dot_general(a, b, (((0,), (0,)), ((), ())), preferred_element_type=F32)


def cols(j, width):
    return pl.ds(pl.multiple_of(j * width, width), width)


def loop(count, body):
    def step(j, carry):
        body(j)
        return carry

    lax.fori_loop(0, count, step, 0)


def blocks_kernel(
    x_ref, cot_ref, small, w_in, w_out, w_gate, w_up, w_down,
    y_ref, gx_ref, gin_h, gout_h, gg_h, gu_h, gd_h, gs_ref,
    xa, xn, n2, ea, fa, part, rr, proj, ge, dce, cv, ha, hb, mx, by_gate, by_up, hd, dg, du,
    mid, dmid, dp, g0, win, wout, wg, wu, wd, sm, gains, taps, gtap, ggain,
    store, a_send, a_recv, s_send, s_recv, h_send, h_recv, c_send, c_recv,
    z_send, z_recv, y_send, y_recv, f_send, f_recv, p_send, p_recv, q_send, q_recv, go,
):
    section, xl, xh, y, z = place()
    partner, twin, zs, ys = plane_peers()
    core = {"section": 1 - section}
    group = xl * 8 + xh * 4 + y
    after, before = lax.rem(group + 1, 16), lax.rem(group + 15, 16)
    has_after, has_before = group < 15, group > 0

    def at_group(g):
        return {"xl": g // 8, "xh": lax.rem(g // 4, 2), "y": lax.rem(g, 4)}

    barrier = pltpu.get_barrier_semaphore()

    def hail(device):
        pl.semaphore_signal(barrier, inc=1, device_id=device, device_id_type=MESH)

    for device in (partner, twin, core, *zs.values(), *ys.values()):
        hail(device)

    @pl.when(has_after)
    def _():
        hail(at_group(after))

    @pl.when(has_before)
    def _():
        hail(at_group(before))

    me = xh * 4 + y
    weights = (sm, win, wout, wg, wu, wd)
    cut = (None, dp, None, hd, dg, None)
    rows = (32, 192, 48, 192, 192, 224)
    cut_conv(w_in, dp)
    wout[pl.ds(pl.multiple_of(me * 48, 16), 48), :] = w_out[...]
    first_d = pl.multiple_of(me * 224, 16)
    wd[pl.ds(first_d, 224), :] = jnp.concatenate([w_down[...], jnp.zeros((8, 1536), BF16)], axis=0)
    pl.semaphore_wait(barrier, 10 - (group + 1) // 16 + (group + 15) // 16)

    def of_z(n, ref, first, zz):
        size = rows[n] // 4
        return ref.at[pl.ds(pl.multiple_of(first + zz * size, 8 if n == 0 else 16), size)]

    def rows_q(n, q):
        return pl.multiple_of(q * rows[n], 8 if n == 0 else 16)

    sent, z_copies = [], {}

    def push_z(n):
        size = rows[n] // 4
        for r in ORDER:
            src = small if n == 0 else of_z(n, cut[n], 0, lax.rem(z + r, 4))
            dst = of_z(n, weights[n], me * rows[n], z)
            copy = remote(src, dst, z_send.at[n, r - 1], z_recv.at[n, r - 1], zs[r])
            copy.start()
            z_copies[n, r] = copy
            sent.append(copy)
        mine = pl.ds(pl.multiple_of(me * rows[n] + z * size, 8 if n == 0 else 16), size)
        if n == 0:
            sm[mine, :] = small[...]
        else:
            weights[n][mine, :] = cut[n][pl.ds(pl.multiple_of(z * size, 16), size), 0 : weights[n].shape[1]]

    @pl.when(section == 1)
    def _():
        pl.semaphore_wait(go, 1)

    def own_rows(mb):
        return pl.ds(pl.multiple_of(mb * 256 + z * 64, 64), 64)

    def spread(n, buf, mb):
        at = buf.at[own_rows(mb)]
        return [remote(at, at, a_send.at[n, mb, r - 1], a_recv.at[n, mb, r - 1], zs[r]) for r in ORDER]

    x_all, n_all, e_all, f_all = ([spread(n, buf, mb) for mb in range(2)] for n, buf in enumerate((xa, n2, ea, fa)))

    def begin(copies):
        for copy in copies:
            copy.start()

    def arrived(copies):
        for copy in copies:
            copy.wait_recv()

    mb_rows = [slice(0, 256), slice(256, 512)]
    core_x, core_g = [], []
    for mb in range(2):
        at = pl.ds(mb * 64, 64)
        core_x.append(remote(y_ref.at[at], xa.at[own_rows(mb)], c_send.at[0, mb], c_recv.at[0, mb], core))
        core_g.append(remote(g0.at[at], ea.at[own_rows(mb)], c_send.at[1, mb], c_recv.at[1, mb], core))

    push_z(0)
    push_z(1)

    @pl.when(section == 0)
    def _():
        for mb in range(2):
            xa[own_rows(mb), :] = x_ref[mb * 64 : mb * 64 + 64, :]
            begin(x_all[mb])

    cut_ffn(w_gate, hd)
    push_z(3)
    cut_ffn(w_up, dg)
    push_z(4)

    @pl.when(section == 1)
    def _():
        for mb in range(2):
            ea[own_rows(mb), :] = cot_ref[mb * 64 : mb * 64 + 64, :]
            begin(e_all[mb])

    def piece(u, q):
        n, first, size, way = GATHER_UNITS[u]
        if n == 5:
            return wd.at[pl.ds(pl.multiple_of(q * 224 + first, 16), size)]
        if n == 2:
            return wout.at[pl.ds(rows_q(2, q), 48)]
        return weights[n].at[pl.ds(rows_q(n, q), rows[n]), pl.ds(first, size)]

    def half(u, q, h):
        n, first, size, way = GATHER_UNITS[u]
        if n in (2, 5):
            left = pl.ds(pl.multiple_of(h * 768, 128), 768)
            if n == 5:
                return wd.at[pl.ds(pl.multiple_of(q * 224 + first, 16), size), left]
            return wout.at[pl.ds(rows_q(2, q), 48), left]
        part_rows = rows[n] // 2
        return weights[n].at[
            pl.ds(pl.multiple_of(q * rows[n] + h * part_rows, 8 if n == 0 else 16), part_rows), pl.ds(first, size)
        ]

    y_copies, f_copies, p_copies, q_copies, started = {}, {}, {}, {}, set()

    def go_on(table, key, copy):
        copy.start()
        table[key] = copy
        sent.append(copy)

    def push_y(u, far):
        src = piece(u, (1 - xh if far else xh) * 4 + y)
        for k, r in enumerate((1, 3)):
            at = 2 * far + k
            go_on(y_copies, (u, at), remote(src, src, y_send.at[u, at], y_recv.at[u, at], ys[r]))

    def pass_y(u, far):
        for k, r in enumerate((1, 3)):
            at = 2 * far + k
            y_copies[u, at].wait_recv()
            src = half(u, (1 - xh if far else xh) * 4 + lax.rem(y + 4 - r, 4), k)
            go_on(f_copies, (u, at), remote(src, src, f_send.at[u, at], f_recv.at[u, at], ys[r]))
            if GATHER_UNITS[u][3] == 0:
                push_p(u, r)

    def push_p(u, r):
        src = half(u, xh * 4 + lax.rem(y + 4 - r, 4), xl)
        go_on(p_copies, (u, r), remote(src, src, p_send.at[u, r], p_recv.at[u, r], partner))

    def pass_q(u, r):
        p_copies[u, r].wait_recv()
        src = half(u, (1 - xh) * 4 + lax.rem(y + 4 - r, 4), 1 - xl)
        go_on(q_copies, (u, r), remote(src, src, q_send.at[u, r], q_recv.at[u, r], twin))

    def stage_y(u):
        n = GATHER_UNITS[u][0]
        if n not in started:
            started.add(n)
            if n not in (2, 5):
                for r in ORDER:
                    z_copies[n, r].wait_recv()
        push_p(u, 0)
        push_y(u, 0)

    def stage_p(u):
        if GATHER_UNITS[u][3]:
            pass_q(u, 0)
        pass_y(u, 0)

    def stage_f(u):
        if GATHER_UNITS[u][3]:
            q_copies[u, 0].wait_recv()
            push_y(u, 1)
        else:
            for k in range(2):
                f_copies[u, k].wait_recv()
            push_p(u, 2)

    def stage_q(u):
        if GATHER_UNITS[u][3]:
            pass_y(u, 1)
        else:
            for r in (0, *ORDER):
                pass_q(u, r)

    def need(n):
        for u, unit in enumerate(GATHER_UNITS):
            if unit[0] == n and unit[3]:
                for at in range(4):
                    f_copies[u, at].wait_recv()
            elif unit[0] == n:
                for r in (0, *ORDER):
                    q_copies[u, r].wait_recv()

    def scatter(n, mb, j, r):
        at = cols(j, 512)
        src = part.at[pl.ds(pl.multiple_of(mb * 256 + lax.rem(z + r, 4) * 64, 64), 64), at]
        dst = rr.at[n, r - 1, pl.ds(mb * 64, 64), at]
        return remote(src, dst, s_send.at[n, mb, j, r - 1], s_recv.at[n, mb, j, r - 1], zs[r])

    def sum_over_z(n, mb, block):
        def body(j):
            part[mb_rows[mb], cols(j, 512)] = block(cols(j, 512)).astype(BF16)
            for r in ORDER:
                scatter(n, mb, j, r).start()

        loop(3, body)

    def sum_arrived(n, mb):
        def body(j):
            for r in ORDER:
                scatter(n, mb, j, r).wait_recv()

        loop(3, body)

    def sum_sent(n, mb):
        def body(j):
            for r in ORDER:
                scatter(n, mb, j, r).wait_send()

        loop(3, body)

    def summed(n, at, mine):
        total = part[mine, :].astype(F32)
        for r in range(3):
            total = total + rr[n, r, at, :].astype(F32)
        return total

    def own_blocks(mb, body):
        def step(i):
            at = pl.ds(pl.multiple_of(mb * 64 + i * 32, 32), 32)
            mine = pl.ds(pl.multiple_of(mb * 256 + z * 64 + i * 32, 32), 32)
            body(at, mine)

        loop(2, step)

    def rms(values):
        return lax.rsqrt(jnp.mean(values * values, axis=-1, keepdims=True) + EPS)

    def take_input():
        for f in range(32):
            gains[0:2, 48 * f : 48 * f + 48] = sm[8 * f + 3 : 8 * f + 5, 0:48]
        for q in range(8):
            taps[0:3, 48 * q : 48 * q + 48] = sm[pl.ds(pl.multiple_of(q * 32 + z * 8, 8), 8), :][0:3, 0:48]

    halo_after = [
        remote(ge.at[mb, pl.ds(256, 8)], ha.at[mb], h_send.at[0, mb], h_recv.at[0, mb], at_group(after)) for mb in range(2)
    ]
    halo_before = [
        remote(dce.at[mb, pl.ds(0, 8)], hb.at[mb], h_send.at[1, mb], h_recv.at[1, mb], at_group(before)) for mb in range(2)
    ]

    def project(mb):
        arrived(x_all[mb])

        def norm(i):
            at = pl.ds(pl.multiple_of(mb * 256 + i * 32, 32), 32)
            values = xa[at, :].astype(F32)
            xn[at, :] = (values * rms(values) * gains[0:1, :]).astype(BF16)

        loop(8, norm)

        def body(j):
            proj[j, mb_rows[mb], :] = dot_nn(xn[mb_rows[mb], :], win[:, cols(j, 384)])

        loop(3, body)
        ge[mb, 8:264, :] = proj[0, mb_rows[mb], :] * proj[2, mb_rows[mb], :]

        @pl.when(has_after)
        def _():
            halo_after[mb].start()

    def tap(k):
        return taps[k : k + 1, :]

    def mix(mb):
        @pl.when(has_before)
        def _():
            halo_after[mb].wait_recv()
            ge[mb, 0:8, :] = ha[mb]

        @pl.when(jnp.logical_not(has_before))
        def _():
            ge[mb, 0:8, :] = jnp.zeros((8, 384), F32)

        for zc in range(4):
            t0, at = 8 + 64 * zc, slice(mb * 256 + 64 * zc, mb * 256 + 64 * zc + 64)
            total = tap(0) * ge[mb, t0 : t0 + 64, :]
            for k in (1, 2):
                total = total + tap(k) * ge[mb, t0 - k : t0 - k + 64, :]
            cv[at, :] = total
            mx[at, :] = (proj[1, at, :] * total).astype(BF16)
        sum_over_z(0, mb, lambda at: dot_nn(mx[mb_rows[mb], :], wout[:, at]))

    def middle(mb):
        sum_arrived(0, mb)

        def body(at, mine):
            values = xa[mine, :].astype(F32) + summed(0, at, mine)
            mid[at, :] = values
            n2[mine, :] = (values * rms(values) * gains[1:2, :]).astype(BF16)

        own_blocks(mb, body)
        begin(n_all[mb])

    def gate(mb):
        arrived(n_all[mb])

        def body(j):
            at = cols(j, 896)
            gating = dot_nn(n2[mb_rows[mb], :], wg[:, at])
            up_part = dot_nn(n2[mb_rows[mb], :], wu[:, at])
            sg = jax.nn.sigmoid(gating)
            silu = gating * sg
            by_gate[mb_rows[mb], at] = up_part * sg * (1.0 + gating * (1.0 - sg))
            by_up[mb_rows[mb], at] = silu
            hd[mb_rows[mb], at] = (silu * up_part).astype(BF16)

        loop(2, body)

    def sent_before(mb, first, second):
        @pl.when(section == 0)
        def _():
            sum_sent(first, mb)

        @pl.when(section == 1)
        def _():
            sum_sent(second, mb)

    def down(mb):
        sent_before(mb, 0, 3)
        sum_over_z(1, mb, lambda at: dot_nn(hd[mb_rows[mb], :], wd[:, at]))

    def finish(mb):
        sum_arrived(1, mb)

        def body(at, mine):
            y_ref[at, :] = (mid[at, :] + summed(1, at, mine)).astype(BF16)

        own_blocks(mb, body)

        @pl.when(section == 0)
        def _():
            core_x[mb].start()

    def wait_x():
        @pl.when(section == 1)
        def _():
            for mb in range(2):
                core_x[mb].wait_recv()
                begin(x_all[mb])

    def free_cuts():
        for n in (1, 3, 4):
            for r in ORDER:
                z_copies[n, r].wait_send()

    def both(stage):
        stage(0)
        stage(1)

    def begin_forward():
        need(0)
        take_input()
        need(1)
        wait_x()
        project(0)

    def begin_mix():
        need(2)
        mix(0)

    def begin_gate():
        need(3)
        need(4)
        free_cuts()
        gate(0)

    segments = (
        begin_forward, lambda: project(1), begin_mix, lambda: mix(1),
        lambda: middle(0), lambda: middle(1), begin_gate, lambda: gate(1),
    )
    count = len(GATHER_UNITS)
    lag_p, lag_f, lag_q = GATHER_LAGS
    for step in range(count + lag_q):
        if step < count:
            stage_y(step)
        if 0 <= step - lag_p < count:
            stage_p(step - lag_p)
        if 0 <= step - lag_f < count:
            stage_f(step - lag_f)
        if step == GO_AFTER:

            @pl.when(section == 0)
            def _():
                pl.semaphore_signal(go, inc=1, device_id=core, device_id_type=MESH)

        if 0 <= step - lag_q < count:
            stage_q(step - lag_q)
        for turn, segment in enumerate(segments):
            if step == FORWARD_AT[0][turn]:
                pl.when(section == 0)(segment)
            if step == FORWARD_AT[1][turn]:
                pl.when(section == 1)(segment)

    need(5)

    @pl.when(section == 0)
    def _():
        both(down)
        both(finish)

    ggain[...] = jnp.zeros((2, 1536), F32)

    def take_gradient(mb):
        @pl.when(section == 0)
        def _():
            core_g[mb].wait_recv()
            begin(e_all[mb])

    def back_hidden(mb):
        arrived(e_all[mb])

        def body(j):
            at = cols(j, 896)
            dh = dot_nt(ea[mb_rows[mb], :], wd[at, :])
            dg[mb_rows[mb], at] = (dh * by_gate[mb_rows[mb], at]).astype(BF16)
            du[mb_rows[mb], at] = (dh * by_up[mb_rows[mb], at]).astype(BF16)

        loop(2, body)

    def back_ffn(mb):
        sent_before(mb, 1, 0)
        sum_over_z(2, mb, lambda at: dot_nt(dg[mb_rows[mb], :], wg[at, :]) + dot_nt(du[mb_rows[mb], :], wu[at, :]))

    def back_middle(mb):
        sum_arrived(2, mb)

        def body(at, mine):
            dn2 = summed(2, at, mine)
            values = mid[at, :]
            scale = rms(values)
            weighted = dn2 * gains[1:2, :]
            mean_term = jnp.mean(weighted * values, axis=-1, keepdims=True)
            grad = ea[mine, :].astype(F32) + scale * weighted - values * (scale * scale * scale) * mean_term
            ggain[1:2, :] += jnp.sum(dn2 * values * scale, axis=0, keepdims=True)
            dmid[at, :] = grad
            fa[mine, :] = grad.astype(BF16)

        own_blocks(mb, body)
        begin(f_all[mb])

    def back_mix(mb):
        arrived(f_all[mb])
        dce[mb, 0:256, :] = dot_nt(fa[mb_rows[mb], :], wout[...])
        for zc in range(4):
            at, here = slice(mb * 256 + 64 * zc, mb * 256 + 64 * zc + 64), slice(64 * zc, 64 * zc + 64)
            dm = dce[mb, here, :]
            dp[at, 384:768] = (dm * cv[at, :]).astype(BF16)
            dce[mb, here, :] = dm * proj[1, at, :]

        @pl.when(has_before)
        def _():
            halo_before[mb].start()

    def back_conv(mb):
        @pl.when(has_after)
        def _():
            halo_before[mb].wait_recv()
            dce[mb, 256:264, :] = hb[mb]

        @pl.when(jnp.logical_not(has_after))
        def _():
            dce[mb, 256:264, :] = jnp.zeros((8, 384), F32)

        for zc in range(4):
            at, t0 = slice(mb * 256 + 64 * zc, mb * 256 + 64 * zc + 64), 64 * zc
            total = tap(0) * dce[mb, t0 : t0 + 64, :]
            for k in (1, 2):
                total = total + tap(k) * dce[mb, t0 + k : t0 + k + 64, :]
            dp[at, 0:384] = (total * proj[2, at, :]).astype(BF16)
            dp[at, 768:1152] = (total * proj[0, at, :]).astype(BF16)

    def back_in(mb):
        sum_sent(2, mb)
        sum_over_z(3, mb, lambda at: dot_nt(dp[mb_rows[mb], :], win[at, :]))

    def back_input(mb):
        sum_arrived(3, mb)

        def body(at, mine):
            dn = summed(3, at, mine)
            values = xa[mine, :].astype(F32)
            scale = rms(values)
            weighted = dn * gains[0:1, :]
            mean_term = jnp.mean(weighted * values, axis=-1, keepdims=True)
            grad = dmid[at, :] + scale * weighted - values * (scale * scale * scale) * mean_term
            ggain[0:1, :] += jnp.sum(dn * values * scale, axis=0, keepdims=True)
            gx_ref[at, :] = grad
            g0[at, :] = grad.astype(BF16)

        own_blocks(mb, body)

        @pl.when(section == 1)
        def _():
            core_g[mb].start()

    stores = [
        pltpu.make_async_copy(src, dst, store.at[n])
        for n, (src, dst) in enumerate(((win, gin_h), (wout, gout_h), (wg, gg_h), (wu, gu_h), (wd, gd_h)))
    ]

    def grad(n, width, left, right):
        target = (win, wout, wg, wu, wd)[n]

        def body(j):
            at = cols(j, width)
            target[at, :] = dot_tn(left[:, at], right[...]).astype(BF16)

        loop(target.shape[0] // width, body)
        stores[n].start()

    def grad_taps():
        for k in range(3):
            total = jnp.zeros((1, 384), F32)
            for mb in range(2):
                for zc in range(4):
                    t0 = 8 + 64 * zc - k
                    products = dce[mb, 64 * zc : 64 * zc + 64, :] * ge[mb, t0 : t0 + 64, :]
                    total = total + jnp.sum(products, axis=0, keepdims=True)
            gtap[k : k + 1, :] = total

    both(take_gradient)
    both(lambda mb: (back_hidden(mb), back_ffn(mb)))
    for copy in sent:
        if not any(copy is z_copies[n, r] for n in (1, 3, 4) for r in ORDER):
            copy.wait_send()
    back_middle(0)
    grad(2, 768, n2, dg)
    back_middle(1)
    grad(3, 768, n2, du)
    both(back_mix)
    both(lambda mb: (back_conv(mb), back_in(mb)))
    grad(1, 384, mx, fa)
    grad_taps()
    for mb in range(2):
        back_input(mb)
        pl.when(section == 1)(functools.partial(down, mb))
    grad(4, 896, hd, ea)
    grad(0, 768, xn, dp)

    @pl.when(section == 1)
    def _():
        both(finish)

    gs_ref[...] = jnp.zeros((256, 128), F32)
    for q in range(8):
        at = pl.ds(pl.multiple_of(q * 32 + z * 8, 8), 8)
        gs_ref[at, 0:48] = gtap[:, 48 * q : 48 * q + 48]
    for f in range(32):
        gs_ref[8 * f + 3 : 8 * f + 5, 0:48] = ggain[0:2, 48 * f : 48 * f + 48]

    for mb in range(2):

        @pl.when(section == 1)
        def _():
            core_g[mb].wait_send()

        @pl.when(section == 0)
        def _():
            core_x[mb].wait_send()

        @pl.when(has_after)
        def _():
            halo_after[mb].wait_send()

        @pl.when(has_before)
        def _():
            halo_before[mb].wait_send()

        sent_before(mb, 3, 1)
        for copies in (x_all, n_all, e_all, f_all):
            for copy in copies[mb]:
                copy.wait_send()
    for copy in stores:
        copy.wait()


def cut_conv(weight, out):
    for q in range(8):
        for zz in range(4):
            for part in range(3):
                first, to = part * 1536 + (4 * q + zz) * 48, part * 384 + q * 48
                out[zz * 48 : zz * 48 + 48, to : to + 48] = weight[:, first : first + 48]


def cut_ffn(weight, out):
    for zz in range(4):
        for q in range(8):
            first = (4 * q + zz) * 216
            out[zz * 48 : zz * 48 + 48, 224 * q : 224 * q + 216] = weight[:, first : first + 216]
            out[zz * 48 : zz * 48 + 48, 224 * q + 216 : 224 * q + 224] = jnp.zeros((48, 8), BF16)


def run_blocks(x, cot, small, w_in, w_out, w_gate, w_up, w_down):
    shape = jax.ShapeDtypeStruct
    dma = pltpu.SemaphoreType.DMA
    vm = pltpu.VMEM
    count = len(GATHER_UNITS)
    return pl.pallas_call(
        blocks_kernel,
        out_shape=(
            shape((128, 1536), BF16),
            shape((128, 1536), F32),
            shape((1536, 1152), BF16),
            shape((384, 1536), BF16),
            shape((1536, 1792), BF16),
            shape((1536, 1792), BF16),
            shape((1792, 1536), BF16),
            shape((256, 128), F32),
        ),
        in_specs=[VMEM] * 8,
        out_specs=[VMEM] * 2 + [ANY] * 5 + [VMEM],
        scratch_shapes=[
            vm((512, 1536), BF16), vm((512, 1536), BF16), vm((512, 1536), BF16), vm((512, 1536), BF16),
            vm((512, 1536), BF16), vm((512, 1536), BF16), vm((4, 3, 128, 1536), BF16),
            vm((3, 512, 384), F32), vm((2, 264, 384), F32), vm((2, 264, 384), F32), vm((512, 384), F32),
            vm((2, 8, 384), F32), vm((2, 8, 384), F32), vm((512, 384), BF16),
            vm((512, 1792), F32), vm((512, 1792), F32), vm((512, 1792), BF16), vm((512, 1792), BF16),
            vm((512, 1792), BF16), vm((128, 1536), F32), vm((128, 1536), F32), vm((512, 1152), BF16),
            vm((128, 1536), BF16),
            vm((1536, 1152), BF16), vm((384, 1536), BF16), vm((1536, 1792), BF16), vm((1536, 1792), BF16),
            vm((1792, 1536), BF16), vm((256, 128), F32), vm((8, 1536), F32), vm((8, 384), F32), vm((8, 384), F32),
            vm((2, 1536), F32),
            dma((5,)), dma((4, 2, 3)), dma((4, 2, 3)), dma((4, 2, 3, 3)), dma((4, 2, 3, 3)),
            dma((2, 2)), dma((2, 2)), dma((2, 2)), dma((2, 2)),
            dma((5, 3)), dma((5, 3)), dma((count, 4)), dma((count, 4)), dma((count, 4)), dma((count, 4)),
            dma((count, 4)), dma((count, 4)), dma((count, 4)), dma((count, 4)), pltpu.SemaphoreType.REGULAR,
        ],
        compiler_params=pltpu.CompilerParams(
            collective_id=1, has_side_effects=True, vmem_limit_bytes=63 * 2**20
        ),
        name="two_blocks",
    )(x, cot, small, w_in, w_out, w_gate, w_up, w_down)


def unit_shape(u):
    n, first, size, mode = REDUCE_UNITS[u]
    if n == 0:
        return (size, 1536), (size, 768)
    if n == 3:
        return (48, 1536), (48, 768)
    height = 8 if n == 5 else 48
    return (4, height, size), (2, height, size)


def unit_buffers(u):
    n, first, size, mode = REDUCE_UNITS[u]
    whole, part = unit_shape(u)
    dtype = F32 if n == 5 else BF16
    shapes = {
        0: ((4, *part), (4, *part), (2, *part), (2, *whole)),
        1: (None, (4, *whole), (2, *part), (2, *whole)),
        2: (None, whole, (2, 2, *part), (2, 2, *whole)),
    }[mode]
    shapes += (whole, whole if n in (1, 2, 4, 5) else None)
    return [None if shape is None else pltpu.VMEM(shape, dtype) for shape in shapes]


def reduce_kernel(
    g_d, g_g, g_u, g_o, g_in, g_s,
    o_d, o_g, o_u, o_o, o_in, o_s,
    v_d, v_g, v_u, v_o, v_in, v_s, l_d, l_g, l_u, l_in, l_s,
    load, q_send, q_recv, p_send, p_recv, y_send, y_recv, t_send, t_recv, z_send, z_recv,
    *buffers,
):
    section, xl, xh, y, z = place()
    partner, twin, zs, ys = plane_peers()
    held = (v_d, v_g, v_u, v_o, v_in, v_s)
    landing = (l_d, l_g, l_u, o_o, l_in, l_s)
    loads = [pltpu.make_async_copy(src, held[n], load.at[n]) for n, src in enumerate((g_d, g_g, g_u, g_o, g_in, g_s))]
    first_use = list(dict.fromkeys(unit[0] for unit in REDUCE_UNITS))
    for n in first_use[:2]:
        loads[n].start()
    barrier_all([partner, twin, *zs.values(), *ys.values()])
    count = len(REDUCE_UNITS)
    left = list(buffers)
    slots = [[None if shape is None else left.pop(0) for shape in unit_buffers(u)] for u in range(count)]
    from_twin, from_partner, halves_y, from_y, theirs, ended = zip(*slots)
    near, far = xh, 1 - xh
    sent, copies = [], {}

    def begin(key, copy):
        copy.start()
        copies[key] = copy
        sent.append(copy)

    def tail(u, h=None):
        n, first, size, mode = REDUCE_UNITS[u]
        across = slice(None) if h is None else pl.ds(pl.multiple_of(h * 768, 128), 768)
        if n == 0:
            return pl.ds(first, size), across
        if n == 3:
            return slice(None), across
        return slice(None) if h is None else pl.ds(h * 2, 2), slice(None), pl.ds(first, size)

    def blocks(u, h=None):
        n, first, size, mode = REDUCE_UNITS[u]
        if n in (0, 3):
            across = slice(None) if h is None else pl.ds(pl.multiple_of(h * 768, 128), 768)
            start = first if n == 0 else 0

            def at(i):
                return (pl.ds(pl.multiple_of(start + i * 16, 16), 16), across), (
                    pl.ds(pl.multiple_of(i * 16, 16), 16),
                    slice(None),
                )

            return (size if n == 0 else 48) // 16, at
        shift = 0 if h is None else h * 2
        return 4 if h is None else 2, lambda i: ((shift + i, slice(None), slice(first, first + size)), (i,))

    def add_rows(u, side, h, other):
        ref = held[REDUCE_UNITS[u][0]]
        number, at = blocks(u, h)

        def body(k):
            row = k // number
            here, there = at(lax.rem(k, number))
            ref[side, row, *here] = ref[side, row, *here] + other[row, *there]

        loop(4 * number, body)

    def sides(u):
        return (0, 1) if REDUCE_UNITS[u][3] == 2 else (near,)

    def lead(u, row):
        return (slice(None) if REDUCE_UNITS[u][3] == 2 else near, row)

    def of_side(u, k, side):
        return (k, side) if REDUCE_UNITS[u][3] == 2 else (k,)

    def send_halves(u):
        ref = held[REDUCE_UNITS[u][0]]
        for k, r in enumerate((1, 3)):
            src = ref.at[*lead(u, lax.rem(y + 2, 4)), *tail(u, k)]
            begin(("half", u, k), remote(src, halves_y[u].at[k], y_send.at[u, k], y_recv.at[u, k], ys[r]))

    def send_wholes(u):
        ref = held[REDUCE_UNITS[u][0]]
        for k, r in enumerate((1, 3)):
            row = lax.rem(y + r, 4)
            copies["half", u, k].wait_recv()
            number, at = blocks(u, k)
            for side in sides(u):

                def body(i):
                    here, there = at(i)
                    got = halves_y[u][*of_side(u, k, side), *there]
                    ref[side, row, *here] = ref[side, row, *here] + got

                loop(number, body)
            src = ref.at[*lead(u, row), *tail(u)]
            begin(("y", u, k), remote(src, from_y[u].at[k], y_send.at[u, 2 + k], y_recv.at[u, 2 + k], ys[r]))

    def send_p(u, src):
        begin(("p", u), remote(src, from_partner[u], p_send.at[u], p_recv.at[u], partner))

    def send_twin(u):
        src = held[REDUCE_UNITS[u][0]].at[near, y, *tail(u)]
        begin(("t", u), remote(src, theirs[u], t_send.at[u], t_recv.at[u], twin))

    def sum_y(u):
        for k in range(2):
            copies["y", u, k].wait_recv()
        ref = held[REDUCE_UNITS[u][0]]
        number, at = blocks(u)
        for side in sides(u):

            def body(i):
                here, there = at(i)
                total = ref[side, y, *here].astype(F32)
                for k in range(2):
                    total = total + from_y[u][*of_side(u, k, side), *there].astype(F32)
                ref[side, y, *here] = total.astype(ref.dtype)

            loop(number, body)

    ready = set()

    def stage_0(u):
        n, first, size, mode = REDUCE_UNITS[u]
        if n not in ready:
            ready.add(n)
            loads[n].wait()
            for following in first_use[len(ready) + 1 : len(ready) + 2]:
                loads[following].start()
        if mode == 0:
            src = held[n].at[far, :, *tail(u, 1 - xl)]
            begin(("q", u), remote(src, from_twin[u], q_send.at[u], q_recv.at[u], twin))
        elif mode == 1:
            send_p(u, held[n].at[far, :, *tail(u)])
        else:
            send_halves(u)

    def stage_1(u):
        n, first, size, mode = REDUCE_UNITS[u]
        if mode == 0:
            copies["q", u].wait_recv()
            add_rows(u, far, xl, from_twin[u])
            send_p(u, held[n].at[far, :, *tail(u, xl)])
        elif mode == 2:
            send_wholes(u)

    def stage_2(u):
        n, first, size, mode = REDUCE_UNITS[u]
        if mode == 2:
            sum_y(u)
            send_p(u, held[n].at[far, y, *tail(u)])
        else:
            copies["p", u].wait_recv()
            add_rows(u, near, 1 - xl if mode == 0 else None, from_partner[u])
            send_halves(u)

    def stage_3(u):
        n, first, size, mode = REDUCE_UNITS[u]
        if mode == 2:
            copies["p", u].wait_recv()
            number, at = blocks(u)

            def body(i):
                here, there = at(i)
                held[n][near, y, *here] = held[n][near, y, *here] + from_partner[u][there]

            loop(number, body)
            send_twin(u)
        else:
            send_wholes(u)

    def stage_4(u):
        if REDUCE_UNITS[u][3] != 2:
            sum_y(u)
            send_twin(u)

    def stage_5(u):
        n, first, size, mode = REDUCE_UNITS[u]
        copies["t", u].wait_recv()
        number, at = blocks(u)

        def body(i):
            here, there = at(i)
            if n in (0, 3):
                landing[n][here] = held[n][near, y, *here].astype(F32) + theirs[u][there].astype(F32)
            else:
                ended[u][there] = held[n][near, y, *here] + theirs[u][there]

        loop(number, body)
        if n not in (0, 3):
            part = (slice(None), pl.ds(first, size))
            for r in ORDER:
                src, dst = ended[u].at[lax.rem(z + r, 4)], landing[n].at[z, *part]
                begin(("z", u, r), remote(src, dst, z_send.at[u, r - 1], z_recv.at[u, r - 1], zs[r]))
            landing[n][z, :, first : first + size] = ended[u][z]

    stages = (stage_0, stage_1, stage_2, stage_3, stage_4, stage_5)
    for step in range(count + REDUCE_LAGS[-1]):
        for lag, stage in zip(REDUCE_LAGS, stages):
            if 0 <= step - lag < count:
                stage(step - lag)

    def landed(n):
        for u in range(count):
            if REDUCE_UNITS[u][0] == n:
                for r in ORDER:
                    copies["z", u, r].wait_recv()

    o_d[...] = l_d[0:216, :]
    for n, out in ((1, o_g), (2, o_u)):
        landed(n)
        for zz in range(4):
            for q in range(8):
                first = (4 * q + zz) * 216
                out[:, first : first + 216] = landing[n][zz, :, 224 * q : 224 * q + 216].astype(F32)
    landed(4)
    for zz in range(4):
        for q in range(8):
            for part in range(3):
                first, at = part * 1536 + (4 * q + zz) * 48, part * 384 + q * 48
                o_in[:, first : first + 48] = l_in[zz, :, at : at + 48].astype(F32)
    landed(5)
    o_s[...] = l_s[0] + l_s[1] + l_s[2] + l_s[3]
    for copy in sent:
        copy.wait_send()


def reduce(g_d, g_g, g_u, g_o, g_in, g_s):
    shape = jax.ShapeDtypeStruct
    dma = pltpu.SemaphoreType.DMA
    vm = pltpu.VMEM
    count = len(REDUCE_UNITS)
    return pl.pallas_call(
        reduce_kernel,
        out_shape=(
            shape((216, 1536), F32),
            shape((48, 6912), F32),
            shape((48, 6912), F32),
            shape((48, 1536), F32),
            shape((48, 4608), F32),
            shape((8, 128), F32),
        ),
        in_specs=[ANY] * 6,
        out_specs=[VMEM] * 6,
        scratch_shapes=[
            vm((2, 4, 224, 1536), BF16), vm((2, 4, 4, 48, 1792), BF16), vm((2, 4, 4, 48, 1792), BF16),
            vm((2, 4, 48, 1536), BF16), vm((2, 4, 4, 48, 1152), BF16), vm((2, 4, 4, 8, 128), F32),
            vm((224, 1536), F32), vm((4, 48, 1792), BF16), vm((4, 48, 1792), BF16), vm((4, 48, 1152), BF16),
            vm((4, 8, 128), F32),
            dma((6,)), dma((count,)), dma((count,)), dma((count,)), dma((count,)), dma((count, 4)), dma((count, 4)),
            dma((count,)), dma((count,)), dma((count, 3)), dma((count, 3)),
            *(buffer for u in range(count) for buffer in unit_buffers(u) if buffer is not None),
        ],
        compiler_params=pltpu.CompilerParams(
            collective_id=2, has_side_effects=True, vmem_limit_bytes=63 * 2**20
        ),
        name="reduce_grads",
    )(
        g_d.reshape(2, 4, 224, 1536),
        g_g.reshape(2, 4, 4, 48, 1792),
        g_u.reshape(2, 4, 4, 48, 1792),
        g_o.reshape(2, 4, 48, 1536),
        g_in.reshape(2, 4, 4, 48, 1152),
        g_s.reshape(2, 4, 4, 8, 128),
    )


def local(inputs, cotangent, w_in, w_out, w_gate, w_up, w_down, kernel, gain_mix, gain_ffn):
    small = jnp.concatenate([kernel[0], gain_mix, gain_ffn], axis=0).astype(F32)
    small = jnp.pad(small, ((0, 3), (0, 80)))
    y, gx, g_in, g_o, g_g, g_u, g_d, g_s = run_blocks(
        inputs.reshape(128, 1536), cotangent.reshape(128, 1536), small, w_in[0], w_out[0], w_gate[0], w_up[0], w_down[0]
    )
    o_d, o_g, o_u, o_o, o_in, o_s = reduce(g_d, g_g, g_u, g_o, g_in, g_s)
    return (
        y.reshape(1, 2, 64, 1536),
        gx.reshape(1, 2, 64, 1536),
        o_in[None],
        o_o[None],
        o_g[None],
        o_u[None],
        o_d[None],
        o_s[None, 0:3, :48],
        o_s[3:4, :48],
        o_s[4:5, :48],
    )


def solution(mesh):
    names = ("section", "xl", "xh", "y", "z")
    fine = Mesh(mesh.devices.reshape(2, 2, 2, 4, 4), names)
    tokens, shard = ("xl", "xh", "y", "z"), ("xh", "y", "z")
    weight = P("section", shard, None)
    acts = P("section", None, tokens, None)
    return jax.shard_map(
        local,
        mesh=fine,
        in_specs=(
            P(None, tokens, None),
            P(None, tokens, None),
            weight,
            weight,
            weight,
            weight,
            weight,
            P("section", None, shard),
            P("section", shard),
            P("section", shard),
        ),
        out_specs=(
            acts,
            acts,
            weight,
            weight,
            weight,
            weight,
            weight,
            P("section", None, shard),
            P("section", shard),
            P("section", shard),
        ),
        check_vma=False,
    )
```
